256 devices in a mesh: tm: 32 (over z, x), ctx: 8 (over y, core).
Axes of the slice: x: 4, y: 4, z: 8, core: 2. Of those that a mesh axis runs over, the one named last changes fastest.
Arguments:
- frames: bfloat16 [4096, 1024], P('tm'), may hold values from -6 to 6
- value_weight: bfloat16 [1024, 1024], P(None, 'ctx'), may hold values from -0.1875 to 0.1875
- gate_weight: bfloat16 [1024, 1024], P(None, 'ctx'), may hold values from -0.1875 to 0.1875
- conv_taps: float32 [31, 1024], P(None, 'ctx'), may hold values from -1 to 1
- out_weight: bfloat16 [1024, 1024], P('ctx'), may hold values from -1 to 1
- adapter: bfloat16 [1024, 8192], P('tm', 'ctx'), may hold values from -0.1875 to 0.1875
- audio_pos: int32 [4096], replicated, may hold values from 0 to 16383, as said below
- text_rows: bfloat16 [16384, 8192], P('tm', 'ctx'), may hold values from -6 to 6
- value_proj: bfloat16 [8192, 4096], P('ctx', 'tm'), may hold values from -0.0625 to 0.0625
- queries: bfloat16 [16384, 4096], P(('tm', 'ctx')), may hold values from -12 to 12
- keys: bfloat16 [16384, 4096], P(('tm', 'ctx')), may hold values from -4 to 4
- grad_out: bfloat16 [16384, 4096], P(('tm', 'ctx')), may hold values from -6 to 6
- window_low: int32 [16384], P('tm'), may hold values from 0 to 16383, as said below
Outputs:
- d_keys: bfloat16 [16384, 4096], P('tm', 'ctx')
- d_hidden: bfloat16 [16384, 8192], P('tm', 'ctx')
The draws below stay inside these ranges and needn't reach their ends.
Inputs may be any that keep to these rules, and one draw needn't show every extreme that they name: `audio_pos`: the positions are distinct. Of the audio rows r = t * 128 .. (t + 1) * 128 - 1 of one time block t, at most 8 land in one block of 512 consecutive positions, and exactly 8 land in some block. The audio rows that land in one block of 512 positions occupy consecutive positions, in the order of r. window_low[i] <= i - 1 for i >= 1, window_low[0] = 0, and i - window_low[i] <= 512, with equality for some i.
All inputs are finite; a program needn't handle non-finite values.
Results may differ from the reference program's by a relative error of at most 0.023.
Values may be sent and summed in bfloat16 or wider, within the bound.
A program may use at most 128 MiB of HBM per device.

```python
import math
import jax
import jax.numpy as jnp
from jax import lax

DE = 1024
KS = 31
D = 8192
HEADS = 32
DH = 128
TOK = 512
AUD_DEV = 128
SEQ = 16384
AUDIO = 4096
N_TM = 32
N_CTX = 8


def shared_pair(key, strength):
    width = HEADS * DH
    key_q, key_k, key_m, key_r, key_e = jax.random.split(key, 5)
    base_q = jnp.clip(jax.random.normal(key_q, (SEQ, width), jnp.float32), -4.0, 4.0)
    base_k = jnp.clip(jax.random.normal(key_k, (SEQ, width), jnp.float32), -4.0, 4.0)
    offset = jax.random.randint(key_r, (), 1, 16)
    positions = jnp.arange(SEQ, dtype=jnp.int32)
    chosen = (positions % 16 == offset)[:, None]
    before = ((positions + 1) % 16 == offset)[:, None]
    factor = jax.random.uniform(key_m, (SEQ, 1), jnp.float32, 1.0, 3.0)
    signs = jnp.where(base_k >= 0.0, 1.0, -1.0)
    strong = signs * jax.random.uniform(key_e, (SEQ, width), jnp.float32, 2.0, 4.0)
    later_strong = jnp.roll(strong, -1, axis=0)
    later_factor = jnp.roll(factor, -1, axis=0)
    lit_chosen = jnp.logical_and(chosen, strength > 0.5)
    lit_before = jnp.logical_and(before, strength > 0.5)
    keys_out = jnp.where(lit_chosen, strong, jnp.where(lit_before, (1.0 - 0.02 / later_factor) * later_strong, base_k))
    queries_out = jnp.where(lit_chosen, factor * strong, base_q)
    return (queries_out, keys_out)


def draw_queries(key, part):
    strength = 0.0
    return shared_pair(key, strength)[0].astype(jnp.bfloat16)


def draw_keys(key, part):
    strength = 0.0
    return shared_pair(key, strength)[1].astype(jnp.bfloat16)


def draw_window_low(key, part):
    key = jax.random.fold_in(key, 7)
    positions = jnp.arange(SEQ, dtype=jnp.int32)
    spans = jax.random.randint(key, (SEQ,), 1, TOK + 1)
    spans = jnp.where(positions == SEQ - 1, TOK, spans)
    return jnp.maximum(positions - spans, 0).astype(jnp.int32)


def draw_audio_pos(key, part):
    key = jax.random.fold_in(key, 5)
    key_p, key_s, key_o = jax.random.split(key, 3)
    capacity = 2 * AUD_DEV // N_TM
    primary = jax.random.permutation(key_p, N_TM).astype(jnp.int32)
    turns = jax.random.randint(key_s, (N_TM, 1), 0, N_TM - 1)
    column = jnp.arange(AUD_DEV, dtype=jnp.int32)[None, :]
    spread = (primary[:, None] + 1 + (column - capacity + turns) % (N_TM - 1)) % N_TM
    target = jnp.where(column < capacity, primary[:, None], spread).reshape(-1)
    hit_table = (target[:, None] == jnp.arange(N_TM, dtype=jnp.int32)[None, :]).astype(jnp.int32)
    rank_rows = jnp.sum((jnp.cumsum(hit_table, axis=0) - hit_table) * hit_table, axis=1)
    loads = jnp.sum(hit_table, axis=0)
    starts = jax.random.randint(key_o, (N_TM,), 0, TOK - loads + 1)
    start_rows = jnp.sum(hit_table * starts[None, :], axis=1)
    return (target * TOK + start_rows + rank_rows).astype(jnp.int32)


def levels(own_key, extent, shards, smallest, high):
    gain = 1.0
    for position, blocks in shards:
        steps = jax.random.uniform(jax.random.fold_in(jax.random.fold_in(own_key, 6), position), (blocks,), jnp.float32, smallest / len(shards), high / len(shards))
        gain = gain * jnp.repeat(jnp.exp(steps), extent[position] // blocks).reshape((-1,) + (1,) * (len(extent) - 1 - position))
    return gain


def scatter_about(key, dims, scale, limit, pieces=(), kind=jnp.bfloat16):
    array = jax.random.normal(key, dims, jnp.float32) * scale
    if len(pieces) > 0:
        array = levels(key, dims, pieces, -0.22, 0.18) * array
    return jnp.clip(array, min=-limit, max=limit).astype(kind)


def setup_inputs(seed: int = 0) -> dict:
    splits = jax.random.split(jax.random.key(seed), 14)
    return {
        "frames": scatter_about(splits[0], (AUDIO, DE), 1.0, 6.0, ((0, 32),)),
        "value_weight": scatter_about(splits[1], (DE, DE), DE ** -0.5, 0.1875, ((1, 8),)),
        "gate_weight": scatter_about(splits[2], (DE, DE), DE ** -0.5, 0.1875, ((1, 8),)),
        "conv_taps": scatter_about(splits[3], (KS, DE), KS ** -0.5, 1.0, ((1, 8),), jnp.float32),
        "out_weight": scatter_about(splits[4], (DE, DE), (DE // 32) ** -0.5, 1.0, ((0, 8),)),
        "adapter": scatter_about(splits[5], (DE, D), DE ** -0.5, 0.1875, ((0, 32), (1, 8))),
        "audio_pos": draw_audio_pos(jax.random.fold_in(splits[13], 71), 0),
        "text_rows": scatter_about(splits[7], (SEQ, D), 1.0, 6.0, ((0, 32), (1, 8))),
        "value_proj": scatter_about(splits[8], (D, HEADS * DH), D ** -0.5, 0.0625, ((0, 8), (1, 32))),
        "queries": draw_queries(jax.random.fold_in(splits[13], 71), 0),
        "keys": draw_keys(jax.random.fold_in(splits[13], 71), 0),
        "grad_out": scatter_about(splits[11], (SEQ, HEADS * DH), 1.0, 6.0, ((0, 256),)),
        "window_low": draw_window_low(jax.random.fold_in(splits[13], 71), 0),
    }


NORM_EPS = 1e-05
MASK_FILL = -1e+30

def window_block(block, queries, keys_pad, values_pad, grad_out, window_low):
    score_scale = 1.0 / math.sqrt(DH)
    width = HEADS * DH
    first_row = (block * TOK).astype(jnp.int32)
    query_rows = lax.dynamic_slice_in_dim(queries, first_row, TOK, 0).astype(jnp.float32).reshape(TOK, HEADS, DH)
    grad_rows = lax.dynamic_slice_in_dim(grad_out, first_row, TOK, 0).astype(jnp.float32).reshape(TOK, HEADS, DH)
    key_rows = lax.dynamic_slice_in_dim(keys_pad, first_row, 2 * TOK, 0).astype(jnp.float32).reshape(2 * TOK, HEADS, DH)
    value_rows = lax.dynamic_slice_in_dim(values_pad, first_row, 2 * TOK, 0).astype(jnp.float32).reshape(2 * TOK, HEADS, DH)
    low_rows = lax.dynamic_slice_in_dim(window_low, first_row, TOK, 0)
    query_pos = first_row + jnp.arange(TOK, dtype=jnp.int32)
    key_pos = first_row - TOK + jnp.arange(2 * TOK, dtype=jnp.int32)
    allowed = (key_pos[None, :] <= query_pos[:, None]) & (key_pos[None, :] >= low_rows[:, None])
    scores = jnp.einsum('ihd,jhd->hij', query_rows, key_rows) * score_scale
    masked = jnp.where(allowed[None], scores, MASK_FILL)
    row_peak = lax.optimization_barrier(jnp.max(masked, axis=2))
    raw_scores = jnp.where(allowed[None], jnp.exp(masked - row_peak[:, :, None]), 0.0)
    row_total = lax.optimization_barrier(jnp.sum(raw_scores, axis=2))
    probs_full = raw_scores / row_total[:, :, None]
    weights_low = lax.optimization_barrier(probs_full.astype(jnp.bfloat16)).astype(jnp.float32)
    attended = jnp.einsum('hij,jhd->ihd', weights_low, value_rows)
    row_delta = jnp.einsum('ihd,ihd->hi', grad_rows, attended)
    grad_scores = jnp.einsum('ihd,jhd->hij', grad_rows, value_rows)
    slopes_full = probs_full * (grad_scores - row_delta[:, :, None])
    slopes = lax.optimization_barrier(slopes_full.astype(jnp.bfloat16)).astype(jnp.float32)
    value_grad = jnp.einsum('hij,ihd->jhd', weights_low, grad_rows).reshape(2 * TOK, width)
    key_grad = (jnp.einsum('hij,ihd->jhd', slopes, query_rows) * score_scale).reshape(2 * TOK, width)
    return (value_grad, key_grad)

def reference(frames, value_weight, gate_weight, conv_taps, out_weight, adapter, audio_pos, text_rows, value_proj, queries, keys, grad_out, window_low):
    width = HEADS * DH
    rows_float = frames.astype(jnp.float32)
    centre = lax.optimization_barrier(jnp.mean(rows_float, axis=1, keepdims=True))
    offsets = rows_float - centre
    spread = lax.optimization_barrier(jnp.mean(offsets * offsets, axis=1, keepdims=True))
    normed = (offsets * lax.rsqrt(spread + NORM_EPS)).astype(jnp.bfloat16)
    value_part = jnp.dot(normed, value_weight, preferred_element_type=jnp.float32)
    gate_part = jnp.dot(normed, gate_weight, preferred_element_type=jnp.float32)
    glu_rows = (value_part * jax.nn.sigmoid(gate_part)).astype(jnp.bfloat16)
    rim_width = (KS - 1) // 2
    padded = jnp.pad(glu_rows.astype(jnp.float32), ((rim_width, rim_width), (0, 0)))
    smooth = jnp.zeros((AUDIO, DE), jnp.float32)
    for offset in range(KS):
        smooth = smooth + conv_taps[offset][None, :] * padded[offset:offset + AUDIO]
    action = (smooth * jax.nn.sigmoid(smooth)).astype(jnp.bfloat16)
    encoded = (rows_float + jnp.dot(action, out_weight, preferred_element_type=jnp.float32)).astype(jnp.bfloat16)
    adapted = jnp.dot(encoded, adapter, preferred_element_type=jnp.float32).astype(jnp.bfloat16)
    hidden = text_rows.at[audio_pos].set(adapted)
    group_cols = D // N_CTX
    hidden_groups = hidden.reshape(SEQ, N_CTX, group_cols).transpose(1, 0, 2)
    proj_groups = value_proj.reshape(N_CTX, group_cols, width)

    def add_group(running, pair):
        term = jnp.dot(pair[0], pair[1], preferred_element_type=jnp.float32)
        rounded = lax.optimization_barrier(term.astype(jnp.bfloat16))
        return (running + rounded.astype(jnp.float32), None)
    value_sum = lax.scan(add_group, jnp.zeros((SEQ, width), jnp.float32), (hidden_groups, proj_groups))[0]
    values = value_sum.astype(jnp.bfloat16)
    zero_block = jnp.zeros((TOK, width), jnp.bfloat16)
    keys_pad = jnp.concatenate([zero_block, keys], axis=0)
    values_pad = jnp.concatenate([zero_block, values], axis=0)

    def one_block(block):
        return window_block(block, queries, keys_pad, values_pad, grad_out, window_low)
    value_parts, key_parts = lax.map(one_block, jnp.arange(N_TM, dtype=jnp.int32))
    zero_tail = jnp.zeros((1, TOK, width), jnp.float32)
    value_total = value_parts[:, TOK:] + jnp.concatenate([value_parts[1:, :TOK], zero_tail], axis=0)
    key_total = key_parts[:, TOK:] + jnp.concatenate([key_parts[1:, :TOK], zero_tail], axis=0)
    value_grad = value_total.reshape(SEQ, width).astype(jnp.bfloat16)
    d_keys = key_total.reshape(SEQ, width).astype(jnp.bfloat16)
    d_hidden = jnp.dot(value_grad, value_proj.T, preferred_element_type=jnp.float32).astype(jnp.bfloat16)
    return (d_keys, d_hidden)
```

```python
import math

import jax
import jax.numpy as jnp
from jax import lax
from jax.experimental import pallas as pl
from jax.experimental.pallas import tpu as pltpu
from jax.sharding import PartitionSpec as P

DH = 128
NORM_EPS = 1e-05
MASK_FILL = -1e30
MESH = pl.DeviceIdType.MESH
F32 = jnp.float32
BF16 = jnp.bfloat16

NT = 32
NC = 8
NX = 4
NZ = 8
TOK = 512
AUD = 128
DE = 1024
COLS = 1024
HC = 512
HH = HC // DH
HALF = TOK // 2
SLOT = 8
TILES = ((0, 0, 0, 256), (0, 256, 0, 512), (1, 0, 0, 512), (1, 256, 256, 256))
N_SEMS = 128


def dot(a, b):
    return jnp.dot(a, b, preferred_element_type=F32)


def dot_t(a, b):
    return lax.dot_general(a, b, (((1,), (1,)), ((), ())), preferred_element_type=F32)


def iota(shape, dim):
    return lax.broadcasted_iota(jnp.int32, shape, dim)


def kernel(
    frames, vw, gw, taps, ow, text, low8, slot8, land_lo, land_hi, adapter, vp, q, k, g,
    dk_out, dh_out,
    W, AD, qs, gs, ks, lown, ext, glu_s, mixs, mixr, enc, adp, pick, inc, hid,
    e_ref, gv_ref, st_own, st_nxt, st_fp, st_fn, dl_own, dl_nxt, dl_fp, dl_fn,
    VG, psend, pown, precv, rsend, rrecv, vbuf, acc,
    ssem, rsem, lsem, aus, aur, rss, rsr,
):
    t = lax.axis_index("tm")
    c = lax.axis_index("ctx")
    x = lax.rem(t, NX)
    z = lax.div(t, NX)
    core = lax.rem(c, 2)
    yy = lax.div(c, 2)
    up = (lax.rem(z + 1, NZ) * NX + x, c)
    dn = (lax.rem(z + NZ - 1, NZ) * NX + x, c)
    nxt = (lax.rem(t + 1, NT), c)
    prv = (lax.rem(t + NT - 1, NT), c)
    mate = (t, c + 1 - 2 * core)

    def ctx_peer(d):
        return (t, lax.rem(c + d, NC))

    def x_peer(d):
        return (z * NX + lax.rem(x + d, NX), c)

    def zat(d):
        return lax.rem(z + d + NZ, NZ)

    def al(v, m):
        return pl.multiple_of(v, m)

    sends = []

    def send(src, dst, dev):
        i = len(sends)
        copy = pltpu.make_async_remote_copy(
            src_ref=src, dst_ref=dst, send_sem=ssem.at[i], recv_sem=rsem.at[i],
            device_id=dev, device_id_type=MESH,
        )
        copy.start()
        sends.append(copy)
        return copy

    def arrived(copies):
        for copy in copies:
            copy.wait_recv()

    locals_ = []

    def local(src, dst):
        copy = pltpu.make_async_copy(src, dst, lsem.at[len(locals_)])
        copy.start()
        locals_.append(copy)
        return copy

    bar = pltpu.get_barrier_semaphore()

    def greet(d, carry):
        pl.semaphore_signal(bar, inc=1, device_id=(lax.rem(t + d, NT), c), device_id_type=MESH)
        return carry

    lax.fori_loop(1, NT, greet, 0)
    for d in range(1, NC):
        pl.semaphore_signal(bar, inc=1, device_id=ctx_peer(d), device_id_type=MESH)

    own_vp = local(vp, W.at[t])
    own_ad = local(adapter, AD.at[pl.ds(al(t * 32, 32), 32)])
    own_rows = pl.ds(al(c * 64, 64), 64)
    own_cols = pl.ds(al(c * HC, HC), HC)
    own_qkg = [
        local(k.at[:, own_cols], ks.at[own_rows]),
        local(q.at[:, own_cols], qs.at[0, own_rows]),
        local(g.at[:, own_cols], gs.at[0, own_rows]),
    ]
    pl.semaphore_wait(bar, NT - 1 + NC - 1)

    halo = [
        send(frames.at[pl.ds(AUD - 16, 16)], ext.at[pl.ds(0, 16)], nxt),
        send(frames.at[pl.ds(0, 16)], ext.at[pl.ds(AUD + 16, 16)], prv),
    ]
    low_copy = send(low8, lown, prv)
    ad_x = [send(adapter, AD.at[pl.ds(al(t * 32, 32), 32)], x_peer(d)) for d in (1, 3, 2)]
    bz = {}
    az = {}
    dz = {}
    bx = {}

    def ring(s, ref_of, part_of, table):
        if s < NZ // 2 - 1:
            u, v = ref_of(zat(-s)), ref_of(zat(s))
        else:
            u, v = part_of(zat(-s), 0), part_of(zat(s), 1)
        table[s] = [send(u, u, up), send(v, v, dn)]

    def b_ref(zz):
        return W.at[zz * NX + x, pl.ds(512, 512)]

    def b_part(zz, p):
        return W.at[zz * NX + x, pl.ds(512 + 256 * p, 256)]

    def a_ref(zz):
        return W.at[pl.ds(zz * NX, NX), pl.ds(0, 512)]

    def a_part(zz, p):
        return W.at[pl.ds(zz * NX + 2 * p, 2), pl.ds(0, 512)]

    def d_ref(zz):
        return AD.at[pl.ds(al(zz * 128, 128), 128)]

    def d_part(zz, p):
        return AD.at[pl.ds(al(zz * 128 + 64 * p, 64), 64)]

    def b_spread(s):
        offsets = (0,) if s < 0 else ((-1 - s, 1 + s) if s < 3 else (4,))
        bx[s] = [send(b_ref(zat(o)), b_ref(zat(o)), x_peer(d)) for o in offsets for d in (1, 3, 2)]

    def a_step(s):
        ring(s, a_ref, a_part, az)

    def b_step(s):
        ring(s, b_ref, b_part, bz)

    def d_step(s):
        ring(s, d_ref, d_part, dz)

    own_vp.wait()
    a_x = [
        send(vp.at[pl.ds(0, 512)], W.at[t, pl.ds(0, 512)], x_peer(d)) for d in (1, 3, 2)
    ]
    b_step(0)
    qkg = []
    for src, dst in ((k, ks), (q, qs.at[0]), (g, gs.at[0])):
        for d in (1, 7, 2, 6, 3, 5, 4):
            peer = lax.rem(c + d, NC)
            qkg.append(send(src.at[:, pl.ds(al(peer * HC, HC), HC)], dst.at[own_rows], (t, peer)))
    b_spread(-1)

    ext[pl.ds(16, AUD), :] = frames[...]
    arrived(halo)
    rows = ext[...].astype(F32)
    centre = jnp.mean(rows, axis=1, keepdims=True)
    off = rows - centre
    spread = jnp.mean(off * off, axis=1, keepdims=True)
    normed = (off * lax.rsqrt(spread + NORM_EPS)).astype(BF16)
    value_part = dot(normed, vw[...])
    gate_part = dot(normed, gw[...])
    glu = (value_part * jax.nn.sigmoid(gate_part)).astype(BF16).astype(F32)
    row = iota(glu.shape, 0)
    first = jnp.where(t == 0, 16, 0)
    last = jnp.where(t == NT - 1, AUD + 16, AUD + 32)
    glu_s[...] = jnp.where((row >= first) & (row < last), glu, 0.0)

    own_ad.wait()
    arrived(ad_x)
    d_step(0)
    arrived(a_x)
    a_step(0)

    smooth = jnp.zeros((AUD, DH), F32)
    for j in range(taps.shape[0]):
        smooth = smooth + taps[pl.ds(j, 1), :] * glu_s[pl.ds(1 + j, AUD), :]
    action = (smooth * jax.nn.sigmoid(smooth)).astype(BF16)
    mixs[...] = dot(action, ow[...]).astype(BF16)
    mix = [
        send(mixs.at[pl.ds(al(lax.rem(c + d, NC) * 16, 16), 16)], mixr.at[d], ctx_peer(d))
        for d in (4, 2, 6, 3, 5, 1, 7)
    ]
    arrived(bz[0])
    b_step(1)
    b_spread(0)
    arrived(mix)
    mine = pl.ds(al(c * 16, 16), 16)
    total = frames[mine, :].astype(F32) + mixs[mine, :].astype(F32)
    for d in range(1, NC):
        total = total + mixr[d].astype(F32)
    enc[mine, :] = total.astype(BF16)
    enc_copies = [send(enc.at[mine], enc.at[mine], ctx_peer(d)) for d in (4, 2, 6, 3, 5, 1, 7)]

    arrived(dz[0])
    d_step(1)
    for copy in own_qkg:
        copy.wait()
    arrived(qkg)
    halo_qg = [send(qs.at[0], qs.at[1], prv), send(gs.at[0], gs.at[1], prv)]
    arrived(bz[1])
    b_step(2)
    b_spread(1)
    arrived(dz[1])
    d_step(2)

    scale = 1.0 / math.sqrt(DH)
    base = t * TOK
    row8 = iota((8, HALF), 0)

    def head_cols(h):
        return pl.ds(al(h * DH, DH), DH)

    def score_tiles(block, lows, limit, stats):
        def one_head(h, carry):
            hs = head_cols(h)
            for b, i0, j0, jn in TILES:
                if b != block:
                    continue
                qi = pl.ds(i0, HALF)
                s = dot_t(ks[pl.ds(j0, jn), hs], qs[b, qi, hs]) * scale
                jj = iota((jn, HALF), 0) + j0
                ok = jj >= lows[pl.ds(0, 1), qi] - base
                if block == 0:
                    ok = ok & (jj <= iota((jn, HALF), 1) + i0)
                else:
                    ok = ok & (jj < limit)
                s = jnp.where(ok, s, MASK_FILL)
                m = jnp.max(s, axis=0, keepdims=True)
                e = jnp.where(ok, jnp.exp(s - m), 0.0)
                n = jnp.sum(e, axis=0, keepdims=True)
                e_ref[b, h, pl.ds(j0, jn), qi] = e
                stats[h, :, qi] = jnp.where(row8 == 0, m, n)
            return carry

        lax.fori_loop(0, HH, one_head, 0)

    score_tiles(0, low8, TOK, st_own)
    stats_a = send(st_own, st_fn, prv)
    arrived(dz[2])
    d_step(3)
    arrived(az[0])
    a_step(1)
    arrived(bz[2])
    b_step(3)
    b_spread(2)

    arrived([low_copy])
    arrived(halo_qg)
    score_tiles(1, lown, jnp.where(t == NT - 1, 0, TOK), st_nxt)
    stats_b = send(st_nxt, st_fp, nxt)

    arrived(dz[3])
    arrived(enc_copies)
    for n in range(4):
        cols = pl.ds(256 * n, 256)
        adp[:, cols] = dot(enc[...], AD[:, cols]).astype(BF16)
    slot_row = iota((NT * 16, AUD), 0)
    picker = ((slot_row // 16) * SLOT + slot_row % SLOT == slot8[pl.ds(0, 1), :]).astype(F32)
    picker = picker.astype(BF16)
    low_half = dot(picker, adp[:, pl.ds(0, 512)])
    high_half = dot(picker, adp[:, pl.ds(512, 512)])
    upper = iota((NT * 16, 512), 0) % 16 < SLOT
    pick[...] = jnp.where(upper, low_half, high_half).astype(BF16)
    my_slot = pl.ds(al(t * 16, 16), 16)

    def audio_copy(d):
        peer = lax.rem(t + d, NT)
        return pltpu.make_async_remote_copy(
            src_ref=pick.at[pl.ds(al(peer * 16, 16), 16)], dst_ref=inc.at[my_slot],
            send_sem=aus.at[d], recv_sem=aur.at[d], device_id=(peer, c), device_id_type=MESH,
        )

    def audio_start(d, carry):
        audio_copy(d).start()
        return carry

    lax.fori_loop(1, NT, audio_start, 0)
    inc[my_slot, :] = pick[my_slot, :]
    arrived(bz[3])
    b_spread(3)

    arrived([stats_a, stats_b])

    def factor(mine_st, other_st, h):
        m1, s1 = mine_st[h, pl.ds(0, 1), :], mine_st[h, pl.ds(1, 1), :]
        m2, s2 = other_st[h, pl.ds(0, 1), :], other_st[h, pl.ds(1, 1), :]
        m = jnp.maximum(m1, m2)
        a1 = jnp.exp(m1 - m)
        return a1 / (s1 * a1 + s2 * jnp.exp(m2 - m))

    def gather_terms(tiles, other, h):
        hs = head_cols(h)
        top = dot(tiles[0], other[0, pl.ds(0, 256), hs]) + dot(tiles[1][:256], other[0, pl.ds(256, 256), hs])
        top = top + dot(tiles[2][:256], other[1, pl.ds(0, 256), hs])
        low = dot(tiles[1][256:], other[0, pl.ds(256, 256), hs])
        low = low + dot(tiles[2][256:], other[1, pl.ds(0, 256), hs])
        low = low + dot(tiles[3], other[1, pl.ds(256, 256), hs])
        return top, low

    def prob_head(h, carry):
        f = (factor(st_own, st_fp, h), factor(st_nxt, st_fn, h))
        tiles = []
        for b, i0, j0, jn in TILES:
            p = e_ref[b, h, pl.ds(j0, jn), pl.ds(i0, HALF)] * f[b][:, i0 : i0 + HALF]
            e_ref[b, h, pl.ds(j0, jn), pl.ds(i0, HALF)] = p
            tiles.append(p.astype(BF16))
        top, low = gather_terms(tiles, gs, h)
        hs = head_cols(h)
        VG[c, pl.ds(0, 256), hs] = top.astype(BF16)
        VG[c, pl.ds(256, 256), hs] = low.astype(BF16)
        return carry

    lax.fori_loop(0, HH, prob_head, 0)
    vg_y = [send(VG.at[c], VG.at[c], ctx_peer(2 * d)) for d in (1, 3, 2)]
    vg_mate = [send(VG.at[c], VG.at[c], mate)]
    arrived(az[1])
    a_step(2)

    def audio_arrived(d, carry):
        audio_copy(d).wait_recv()
        return carry

    lax.fori_loop(1, NT, audio_arrived, 0)
    for land, cols in ((land_lo, pl.ds(0, 512)), (land_hi, pl.ds(512, 512))):
        place = (iota((TOK, NT * 16), 0) == land[pl.ds(0, 1), :]).astype(F32)
        there = jnp.sum(place, axis=1, keepdims=True) > 0.5
        rows_in = dot(place.astype(BF16), inc[...])
        hid[:, cols] = jnp.where(there, rows_in, text[:, cols].astype(F32)).astype(BF16)

    offsets = (0, -1, 1, -2, 2, -3, 3, 4)
    mate_rows = pl.ds(al((1 - core) * HALF, HALF), HALF)
    my_rows = pl.ds(al(core * HALF, HALF), HALF)

    def weights_of(cp):
        return jnp.concatenate([W[cp * HH + j] for j in range(HH)], axis=1)

    pair = []

    def terms(i):
        cp = zat(offsets[i])
        psend[i] = dot(hid[mate_rows, :], weights_of(cp)).astype(BF16)
        pair.append(send(psend.at[i], precv.at[i], mate))
        pown[i] = dot(hid[my_rows, :], weights_of(cp)).astype(BF16)

    def group_copy(d, i):
        return pltpu.make_async_remote_copy(
            src_ref=rsend.at[i], dst_ref=rrecv.at[yy, my_rows],
            send_sem=rss.at[d], recv_sem=rsr.at[d],
            device_id=(t, lax.rem(c + d, NC)), device_id_type=MESH,
        )

    def chip_sum(i):
        cp = zat(offsets[i])
        d = lax.rem(cp - c + NC, NC)
        arrived([pair[i]])
        total = pown[i].astype(F32) + precv[i].astype(F32)
        rsend[i] = total.astype(BF16)

        @pl.when(d != 0)
        def _():
            group_copy(d, i).start()

        @pl.when(d == 0)
        def _():
            rrecv[yy, my_rows, :] = rsend[i]

    arrived(bx[-1])
    terms(0)
    arrived(az[2])
    a_step(3)
    arrived(bx[0])
    terms(1)
    chip_sum(0)
    terms(2)
    chip_sum(1)
    arrived(bx[1])
    terms(3)
    chip_sum(2)
    terms(4)
    chip_sum(3)
    arrived(vg_y)
    for d in (1, 3, 2):
        src = lax.rem(c + NC - 2 * d, NC)
        vg_mate.append(send(VG.at[src], VG.at[src], mate))
    arrived(bx[2])
    terms(5)
    chip_sum(4)
    terms(6)
    chip_sum(5)
    arrived(az[3])
    arrived(bx[3])
    terms(7)
    chip_sum(6)
    chip_sum(7)

    arrived(vg_mate)

    def hidden_grad(n, carry):
        rows_n = pl.ds(al(n * 256, 256), 256)

        def chunk(cc, carry2):
            w = jnp.concatenate([W[cc * HH + j, rows_n, :] for j in range(HH)], axis=1)
            acc[...] += dot_t(VG[cc], w)
            return carry2

        acc[...] = jnp.zeros(acc.shape, F32)
        lax.fori_loop(0, NC, chunk, 0)
        dh_out[:, rows_n] = acc[...].astype(BF16)
        return carry

    lax.fori_loop(0, COLS // 256, hidden_grad, 0)

    for d in range(1, NC):
        group_copy(d, 0).wait_recv()
    total = rrecv[0].astype(F32)
    for y in range(1, NC // 2):
        total = total + rrecv[y].astype(F32)
    vbuf[...] = total.astype(BF16)

    def delta_head(h, carry):
        hs = head_cols(h)
        for b, i0, j0, jn in TILES:
            qi = pl.ds(i0, HALF)
            gv = dot_t(vbuf[pl.ds(j0, jn), hs], gs[b, qi, hs])
            gv_ref[b, h, pl.ds(j0, jn), qi] = gv
            w = e_ref[b, h, pl.ds(j0, jn), qi].astype(BF16).astype(F32)
            part = jnp.sum(w * gv, axis=0, keepdims=True)
            table = dl_own if b == 0 else dl_nxt
            table[h, :, qi] = jnp.where(row8 == 0, part, 0.0)
        return carry

    lax.fori_loop(0, HH, delta_head, 0)
    arrived([send(dl_own, dl_fn, prv), send(dl_nxt, dl_fp, nxt)])

    def key_head(h, carry):
        delta = (
            dl_own[h, pl.ds(0, 1), :] + dl_fp[h, pl.ds(0, 1), :],
            dl_nxt[h, pl.ds(0, 1), :] + dl_fn[h, pl.ds(0, 1), :],
        )
        tiles = []
        for b, i0, j0, jn in TILES:
            qi = pl.ds(i0, HALF)
            p = e_ref[b, h, pl.ds(j0, jn), qi]
            gv = gv_ref[b, h, pl.ds(j0, jn), qi]
            tiles.append((p * (gv - delta[b][:, i0 : i0 + HALF])).astype(BF16))
        top, low = gather_terms(tiles, qs, h)
        hs = head_cols(h)
        dk_out[pl.ds(0, 256), hs] = (top * scale).astype(BF16)
        dk_out[pl.ds(256, 256), hs] = (low * scale).astype(BF16)
        return carry

    lax.fori_loop(0, HH, key_head, 0)

    def audio_sent(d, carry):
        audio_copy(d).wait_send()
        return carry

    lax.fori_loop(1, NT, audio_sent, 0)
    for d in range(1, NC):
        group_copy(d, 0).wait_send()
    for copy in sends:
        copy.wait_send()


def positions(audio_pos):
    t = lax.axis_index("tm")
    order = jnp.arange(AUD, dtype=jnp.int32)
    own = lax.dynamic_slice_in_dim(audio_pos, t * AUD, AUD)
    target = own // TOK
    same = (target[:, None] == target[None, :]) & (order[:, None] < order[None, :])
    slot = target * SLOT + jnp.sum(same.astype(jnp.int32), axis=0)
    table = audio_pos.reshape(NT, AUD)
    here = table // TOK == t
    before = (order[:, None] < order[None, :]).astype(BF16)
    rank = jnp.dot(here.astype(BF16), before, preferred_element_type=F32).astype(jnp.int32)
    slots = jnp.arange(SLOT, dtype=jnp.int32)
    hit = here[:, None, :] & (rank[:, None, :] == slots[None, :, None])
    place = jnp.sum(jnp.where(hit, table[:, None, :] - t * TOK + 1, 0), axis=2) - 1
    none = jnp.full_like(place, -1)
    land_lo = jnp.concatenate([place, none], axis=1).reshape(1, NT * 16)
    land_hi = jnp.concatenate([none, place], axis=1).reshape(1, NT * 16)
    eight = lambda a: jnp.broadcast_to(a, (8, a.shape[-1]))
    return eight(slot[None]), eight(land_lo), eight(land_hi)


def body(
    frames, value_weight, gate_weight, conv_taps, out_weight, adapter, audio_pos, text_rows,
    value_proj, queries, keys, grad_out, window_low,
):
    slot8, land_lo, land_hi = positions(audio_pos)
    low8 = jnp.broadcast_to(window_low[None], (8, TOK))
    vm = pl.BlockSpec(memory_space=pltpu.VMEM)
    hbm = pl.BlockSpec(memory_space=pl.ANY)
    vmem = pltpu.VMEM
    dma = pltpu.SemaphoreType.DMA
    return pl.pallas_call(
        kernel,
        out_shape=(
            jax.ShapeDtypeStruct((TOK, HC), BF16),
            jax.ShapeDtypeStruct((TOK, COLS), BF16),
        ),
        in_specs=[vm] * 10 + [hbm] * 5,
        out_specs=(vm, vm),
        scratch_shapes=[
            vmem((NT, COLS, DH), BF16),
            vmem((DE, COLS), BF16),
            vmem((2, TOK, HC), BF16),
            vmem((2, TOK, HC), BF16),
            vmem((TOK, HC), BF16),
            vmem((8, TOK), jnp.int32),
            vmem((AUD + 32, DE), BF16),
            vmem((AUD + 32, DH), F32),
            vmem((AUD, DE), BF16),
            vmem((NC, 16, DE), BF16),
            vmem((AUD, DE), BF16),
            vmem((AUD, COLS), BF16),
            vmem((NT * 16, 512), BF16),
            vmem((NT * 16, 512), BF16),
            vmem((TOK, COLS), BF16),
            vmem((2, HH, TOK, TOK), F32),
            vmem((2, HH, TOK, TOK), F32),
        ]
        + [vmem((HH, 8, TOK), F32)] * 8
        + [
            vmem((NC, TOK, HC), BF16),
            vmem((NC, HALF, HC), BF16),
            vmem((NC, HALF, HC), BF16),
            vmem((NC, HALF, HC), BF16),
            vmem((NC, HALF, HC), BF16),
            vmem((NC // 2, TOK, HC), BF16),
            vmem((TOK, HC), BF16),
            vmem((TOK, 256), F32),
            dma((N_SEMS,)),
            dma((N_SEMS,)),
            dma((8,)),
            dma((NT,)),
            dma((NT,)),
            dma((NC,)),
            dma((NC,)),
        ],
        compiler_params=pltpu.CompilerParams(
            collective_id=0, has_side_effects=True, vmem_limit_bytes=60 * 1024 * 1024
        ),
        cost_estimate=pl.CostEstimate(flops=13_000_000_000, bytes_accessed=8_000_000, transcendentals=4_000_000),
    )(
        frames, value_weight, gate_weight, conv_taps, out_weight, text_rows, low8, slot8,
        land_lo, land_hi, adapter, value_proj, queries, keys, grad_out,
    )


def solution(mesh):
    return jax.shard_map(
        body,
        mesh=mesh,
        in_specs=(
            P("tm", None),
            P(None, "ctx"),
            P(None, "ctx"),
            P(None, "ctx"),
            P("ctx", None),
            P("tm", "ctx"),
            P(),
            P("tm", "ctx"),
            P("ctx", "tm"),
            P(("tm", "ctx"), None),
            P(("tm", "ctx"), None),
            P(("tm", "ctx"), None),
            P("tm"),
        ),
        out_specs=(P("tm", "ctx"), P("tm", "ctx")),
        check_vma=False,
    )
```

```python
import math

import jax
import jax.numpy as jnp
from jax import lax
from jax.experimental import pallas as pl
from jax.experimental.pallas import tpu as pltpu
from jax.sharding import PartitionSpec as P

DH = 128
NORM_EPS = 1e-05
MASK_FILL = -1e30
MESH = pl.DeviceIdType.MESH
F32 = jnp.float32
BF16 = jnp.bfloat16

NT = 32
NC = 8
NX = 4
NZ = 8
TOK = 512
AUD = 128
DE = 1024
COLS = 1024
HC = 512
HH = HC // DH
HALF = TOK // 2
SLOT = 8
TILES = ((0, 0, 0, 256), (0, 256, 0, 512), (1, 0, 0, 512), (1, 256, 256, 256))
N_SEMS = 160
ROWS_A = 384
ROWS_B = COLS - ROWS_A
OFFSETS = (0, -1, 1, -2, 2, -3, 3, 4)
ORDER = (
    "issue", "i_b0", "i_k", "i_q", "mm", "pos", "LN", "d_s0", "i_bm", "p0", "m0", "conv",
    "d_s1", "b_s1", "i_ax", "hq", "rm", "sc0", "i_g", "enc", "b_s2", "p1", "d_s2", "r0", "hg",
    "p2", "d_s3", "b_s3", "a_s0", "sc1", "m3", "adapt", "r1", "m1", "m2", "prob", "a_s1", "r2",
    "vgr", "place", "t0", "t1", "t2", "rs0", "rs1", "a_s2", "t3", "vgf", "p3", "rs2", "t4",
    "rs3", "dh0", "rs4", "dh1", "r3", "dh2", "dh3", "dh4", "a_s3", "t5", "t6", "dh5", "dh6",
    "rs5", "rs6", "t7", "dh7", "rs7", "delta", "key",
)


def dot(a, b):
    return jnp.dot(a, b, preferred_element_type=F32)


def dot_t(a, b):
    return lax.dot_general(a, b, (((1,), (1,)), ((), ())), preferred_element_type=F32)


def iota(shape, dim):
    return lax.broadcasted_iota(jnp.int32, shape, dim)


def kernel(
    frames, vw, gw, taps, ow, text, low, aud, adapter, vp, q, k, g,
    dk_out, dh_out,
    W, AD, qs, gs, ks, low_s, lown, frames_s, vw_s, gw_s, taps_s, ow_s, text_s,
    slot_s, land_s, ext, glu_s, mixs, mixr, enc, adp, pick, inc, hid,
    e_ref, gv_ref, st_own, st_nxt, st_fp, st_fn, dl_own, dl_nxt, dl_fp, dl_fn,
    VG, psend, pown, precv, rsend, rrecv, vbuf, acc,
    ssem, rsem, lsem, aus, aur, rss, rsr,
):
    t = lax.axis_index("tm")
    c = lax.axis_index("ctx")
    x = lax.rem(t, NX)
    z = lax.div(t, NX)
    core = lax.rem(c, 2)
    yy = lax.div(c, 2)
    up = (lax.rem(z + 1, NZ) * NX + x, c)
    dn = (lax.rem(z + NZ - 1, NZ) * NX + x, c)
    nxt = (lax.rem(t + 1, NT), c)
    prv = (lax.rem(t + NT - 1, NT), c)
    mate = (t, c + 1 - 2 * core)

    def ctx_peer(d):
        return (t, lax.rem(c + d, NC))

    def x_peer(d):
        return (z * NX + lax.rem(x + d, NX), c)

    def zat(d):
        return lax.rem(z + d + NZ, NZ)

    def al(v, m):
        return pl.multiple_of(v, m)

    sends = []
    groups = {}
    waited = set()

    def send(name, src, dst, dev):
        i = len(sends)
        copy = pltpu.make_async_remote_copy(
            src_ref=src, dst_ref=dst, send_sem=ssem.at[i], recv_sem=rsem.at[i],
            device_id=dev, device_id_type=MESH,
        )
        copy.start()
        sends.append(copy)
        groups.setdefault(name, []).append(copy)

    def need(*names):
        for name in names:
            if name not in waited:
                waited.add(name)
                for copy in groups[name]:
                    if name in here:
                        copy.wait()
                    else:
                        copy.wait_recv()

    here = set()

    def local(name, src, dst):
        copy = pltpu.make_async_copy(src, dst, lsem.at[len(here)])
        copy.start()
        here.add(name)
        groups[name] = [copy]

    own_rows = pl.ds(al(c * 64, 64), 64)
    own_cols = pl.ds(al(c * HC, HC), HC)
    ad_rows = pl.ds(al(t * 32, 32), 32)
    rows_a = pl.ds(0, ROWS_A)
    rows_b = pl.ds(ROWS_A, ROWS_B)

    def issue():
        bar = pltpu.get_barrier_semaphore()

        def greet(d, carry):
            pl.semaphore_signal(bar, inc=1, device_id=(lax.rem(t + d, NT), c), device_id_type=MESH)
            return carry

        lax.fori_loop(1, NT, greet, 0)
        for d in range(1, NC):
            pl.semaphore_signal(bar, inc=1, device_id=ctx_peer(d), device_id_type=MESH)
        local("frames", frames, frames_s)
        local("vw", vw, vw_s)
        local("gw", gw, gw_s)
        local("vp", vp, W.at[t])
        local("ad", adapter, AD.at[ad_rows])
        local("taps", taps, taps_s)
        local("ow", ow, ow_s)
        local("k0", k.at[:, own_cols], ks.at[own_rows])
        local("q0", q.at[:, own_cols], qs.at[0, own_rows])
        local("g0", g.at[:, own_cols], gs.at[0, own_rows])
        local("text", text, text_s)
        low_s[...] = jnp.broadcast_to(low[...], low_s.shape)
        pl.semaphore_wait(bar, NT - 1 + NC - 1)
        send("fh", frames.at[pl.ds(AUD - 16, 16)], ext.at[pl.ds(0, 16)], nxt)
        send("fh", frames.at[pl.ds(0, 16)], ext.at[pl.ds(AUD + 16, 16)], prv)
        for d in (1, 3, 2):
            send("adx", adapter, AD.at[ad_rows], x_peer(d))
        send("low", low_s, lown, prv)

    def b_ref(zz, xx=x):
        return W.at[zz * NX + xx, rows_b]

    def b_part(zz, p):
        return W.at[zz * NX + x, pl.ds(ROWS_A + ROWS_B // 2 * p, ROWS_B // 2)]

    def a_ref(zz):
        return W.at[pl.ds(zz * NX, NX), rows_a]

    def a_part(zz, p):
        return W.at[pl.ds(zz * NX + 2 * p, 2), rows_a]

    def d_ref(zz):
        return AD.at[pl.ds(al(zz * 128, 128), 128)]

    def d_part(zz, p):
        return AD.at[pl.ds(al(zz * 128 + 64 * p, 64), 64)]

    def ring(name, s, ref_of, part_of):
        if s < NZ // 2 - 1:
            u, v = ref_of(zat(-s)), ref_of(zat(s))
        else:
            u, v = part_of(zat(-s), 0), part_of(zat(s), 1)
        send(f"{name}{s}", u, u, up)
        send(f"{name}{s}", v, v, dn)

    def a_step(s):
        need(*([f"a{s - 1}"] if s else ["ax", "vp"]))
        ring("a", s, a_ref, a_part)

    def b_step(s):
        need(*([f"b{s - 1}"] if s else ["vp"]))
        ring("b", s, b_ref, b_part)

    def d_step(s):
        need(*([f"d{s - 1}"] if s else ["adx", "ad"]))
        ring("d", s, d_ref, d_part)

    def reached(s):
        return (0,) if s < 0 else ((-1 - s, 1 + s) if s < 3 else (4,))

    def spread(s, d, kind):
        need(f"b{s}" if s >= 0 else "vp")
        for o in reached(s):
            send(f"{kind}{s}", b_ref(zat(o)), b_ref(zat(o)), x_peer(d))

    def relay(s):
        need(f"p{s}")
        behind = lax.rem(x + NX - 1, NX)
        for o in reached(s):
            send(f"r{s}", b_ref(zat(o), behind), b_ref(zat(o), behind), x_peer(1))

    def issue_ax():
        for d in (1, 3, 2):
            send("ax", vp.at[rows_a], W.at[t, rows_a], x_peer(d))

    def regroup(name, src, dst):
        for d in (1, 7, 2, 6, 3, 5, 4):
            peer = lax.rem(c + d, NC)
            send(name, src.at[:, pl.ds(al(peer * HC, HC), HC)], dst.at[own_rows], (t, peer))

    def positions():
        order = (iota((AUD, AUD), 0) < iota((AUD, AUD), 1)).astype(F32).astype(BF16)
        own = aud[pl.ds(t, 1), :]
        target = own // TOK
        hit = (iota((NT, AUD), 0) == target).astype(F32)
        rank = jnp.sum(dot(hit.astype(BF16), order) * hit, axis=0, keepdims=True)
        slot = target * SLOT + rank.astype(jnp.int32)
        slot_s[...] = jnp.broadcast_to(slot, slot_s.shape)
        table = aud[...]
        landing = table // TOK == t
        landing_rank = dot(landing.astype(F32).astype(BF16), order)
        spot = jnp.where(landing, table - t * TOK + 1, 0)
        n = NT * 16
        grow = (iota((n, NT), 0) // 16 == iota((n, NT), 1)).astype(F32).astype(BF16)
        spot_hi = dot(grow, (spot // 16).astype(F32).astype(BF16))
        spot_lo = dot(grow, (spot % 16).astype(F32).astype(BF16))
        ranks = dot(grow, jnp.where(landing, landing_rank, 64.0).astype(BF16))
        place = spot_hi * 16.0 + spot_lo
        r = (iota((n, AUD), 0) % 16).astype(F32)
        eye = iota((n, n), 0) == iota((n, n), 1)
        for half in range(2):
            col = jnp.sum(jnp.where(ranks == r - 8.0 * half, place, 0.0), axis=1, keepdims=True) - 1.0
            line = jnp.sum(jnp.where(eye, col, 0.0), axis=0, keepdims=True)
            land_s[half] = jnp.broadcast_to(line, (8, n)).astype(jnp.int32)

    def norm_glu():
        need("frames", "vw", "gw")
        ext[pl.ds(16, AUD), :] = frames_s[...]
        need("fh")
        rows = ext[...].astype(F32)
        centre = jnp.mean(rows, axis=1, keepdims=True)
        off = rows - centre
        spread_ = jnp.mean(off * off, axis=1, keepdims=True)
        normed = (off * lax.rsqrt(spread_ + NORM_EPS)).astype(BF16)
        value_part = dot(normed, vw_s[...])
        gate_part = dot(normed, gw_s[...])
        glu = (value_part * jax.nn.sigmoid(gate_part)).astype(BF16).astype(F32)
        row = iota(glu.shape, 0)
        first = jnp.where(t == 0, 16, 0)
        last = jnp.where(t == NT - 1, AUD + 16, AUD + 32)
        glu_s[...] = jnp.where((row >= first) & (row < last), glu, 0.0)

    def conv():
        need("taps", "ow")
        smooth = jnp.zeros((AUD, DH), F32)
        for j in range(taps_s.shape[0]):
            smooth = smooth + taps_s[pl.ds(j, 1), :] * glu_s[pl.ds(1 + j, AUD), :]
        action = (smooth * jax.nn.sigmoid(smooth)).astype(BF16)
        mixs[...] = dot(action, ow_s[...]).astype(BF16)
        for d in (4, 2, 6, 3, 5, 1, 7):
            rows_d = pl.ds(al(lax.rem(c + d, NC) * 16, 16), 16)
            send("mix", mixs.at[rows_d], mixr.at[d], ctx_peer(d))

    def encode():
        need("mix")
        mine = pl.ds(al(c * 16, 16), 16)
        total = frames_s[mine, :].astype(F32) + mixs[mine, :].astype(F32)
        for d in range(1, NC):
            total = total + mixr[d].astype(F32)
        enc[mine, :] = total.astype(BF16)
        for d in (4, 2, 6, 3, 5, 1, 7):
            send("enc", enc.at[mine], enc.at[mine], ctx_peer(d))

    def halo(name):
        part = qs if name == "q" else gs
        need(name, name + "0")
        send("h" + name, part.at[0], part.at[1], prv)

    scale = 1.0 / math.sqrt(DH)
    base = t * TOK
    row8 = iota((8, HALF), 0)

    def head_cols(h):
        return pl.ds(al(h * DH, DH), DH)

    def score_tiles(block, lows, limit, stats):
        def one_head(h, carry):
            hs = head_cols(h)
            for b, i0, j0, jn in TILES:
                if b != block:
                    continue
                qi = pl.ds(i0, HALF)
                s = dot_t(ks[pl.ds(j0, jn), hs], qs[b, qi, hs]) * scale
                jj = iota((jn, HALF), 0) + j0
                ok = jj >= lows[pl.ds(0, 1), qi] - base
                if block == 0:
                    ok = ok & (jj <= iota((jn, HALF), 1) + i0)
                else:
                    ok = ok & (jj < limit)
                s = jnp.where(ok, s, MASK_FILL)
                m = jnp.max(s, axis=0, keepdims=True)
                e = jnp.where(ok, jnp.exp(s - m), 0.0)
                n = jnp.sum(e, axis=0, keepdims=True)
                e_ref[b, h, pl.ds(j0, jn), qi] = e
                stats[h, :, qi] = jnp.where(row8 == 0, m, n)
            return carry

        lax.fori_loop(0, HH, one_head, 0)

    def score_own():
        need("k", "k0", "q", "q0")
        score_tiles(0, low_s, TOK, st_own)
        send("sta", st_own, st_fn, prv)

    def score_next():
        need("k", "k0", "hq", "low")
        score_tiles(1, lown, jnp.where(t == NT - 1, 0, TOK), st_nxt)
        send("stb", st_nxt, st_fp, nxt)

    my_slot = pl.ds(al(t * 16, 16), 16)

    def audio_copy(d):
        peer = lax.rem(t + d, NT)
        return pltpu.make_async_remote_copy(
            src_ref=pick.at[pl.ds(al(peer * 16, 16), 16)], dst_ref=inc.at[my_slot],
            send_sem=aus.at[d], recv_sem=aur.at[d], device_id=(peer, c), device_id_type=MESH,
        )

    def adapt():
        need("d3", "enc")
        for n in range(4):
            cols = pl.ds(256 * n, 256)
            adp[:, cols] = dot(enc[...], AD[:, cols]).astype(BF16)
        slot_row = iota((NT * 16, AUD), 0)
        picker = ((slot_row // 16) * SLOT + slot_row % SLOT == slot_s[pl.ds(0, 1), :]).astype(F32)
        picker = picker.astype(BF16)
        low_half = dot(picker, adp[:, pl.ds(0, 512)])
        high_half = dot(picker, adp[:, pl.ds(512, 512)])
        upper = iota((NT * 16, 512), 0) % 16 < SLOT
        pick[...] = jnp.where(upper, low_half, high_half).astype(BF16)

        def audio_start(d, carry):
            audio_copy(d).start()
            return carry

        lax.fori_loop(1, NT, audio_start, 0)
        inc[my_slot, :] = pick[my_slot, :]

    def factor(mine_st, other_st, h):
        m1, s1 = mine_st[h, pl.ds(0, 1), :], mine_st[h, pl.ds(1, 1), :]
        m2, s2 = other_st[h, pl.ds(0, 1), :], other_st[h, pl.ds(1, 1), :]
        m = jnp.maximum(m1, m2)
        a1 = jnp.exp(m1 - m)
        return a1 / (s1 * a1 + s2 * jnp.exp(m2 - m))

    def gather_terms(tiles, other, h):
        hs = head_cols(h)
        first, second = pl.ds(0, 256), pl.ds(256, 256)
        top = dot(tiles[0], other[0, first, hs]) + dot(tiles[1][:256], other[0, second, hs])
        top = top + dot(tiles[2][:256], other[1, first, hs])
        bottom = dot(tiles[1][256:], other[0, second, hs])
        bottom = bottom + dot(tiles[2][256:], other[1, first, hs])
        bottom = bottom + dot(tiles[3], other[1, second, hs])
        return top, bottom

    def prob():
        need("sta", "stb", "g", "g0", "hg")

        def prob_head(h, carry):
            f = (factor(st_own, st_fp, h), factor(st_nxt, st_fn, h))
            tiles = []
            for b, i0, j0, jn in TILES:
                p = e_ref[b, h, pl.ds(j0, jn), pl.ds(i0, HALF)] * f[b][:, i0 : i0 + HALF]
                e_ref[b, h, pl.ds(j0, jn), pl.ds(i0, HALF)] = p
                tiles.append(p.astype(BF16))
            top, bottom = gather_terms(tiles, gs, h)
            hs = head_cols(h)
            VG[c, pl.ds(0, 256), hs] = top.astype(BF16)
            VG[c, pl.ds(256, 256), hs] = bottom.astype(BF16)
            return carry

        lax.fori_loop(0, HH, prob_head, 0)
        send("vg1", VG.at[c], VG.at[c], ctx_peer(2))
        send("vg3", VG.at[c], VG.at[c], ctx_peer(6))
        send("vgc", VG.at[c], VG.at[c], mate)

    below, above, across = [lax.rem(c + d, NC) for d in (6, 2, 4)]

    def vg_relay():
        need("vg1", "vg3")
        one, two = VG.at[below, pl.ds(0, 256)], VG.at[above, pl.ds(256, 256)]
        send("vg2", one, one, ctx_peer(2))
        send("vg2", two, two, ctx_peer(6))
        send("vgc", VG.at[below], VG.at[below], mate)
        send("vgc", VG.at[above], VG.at[above], mate)

    def vg_last():
        need("vg2")
        send("vgc", VG.at[across], VG.at[across], mate)

    def place():
        need("text")

        def audio_arrived(d, carry):
            audio_copy(d).wait_recv()
            return carry

        lax.fori_loop(1, NT, audio_arrived, 0)
        for half in range(2):
            cols = pl.ds(512 * half, 512)
            hits = (iota((TOK, NT * 16), 0) == land_s[half, pl.ds(0, 1), :]).astype(F32)
            there = jnp.sum(hits, axis=1, keepdims=True) > 0.5
            rows_in = dot(hits.astype(BF16), inc[...])
            hid[:, cols] = jnp.where(there, rows_in, text_s[:, cols].astype(F32)).astype(BF16)

    mate_rows = pl.ds(al((1 - core) * HALF, HALF), HALF)
    my_rows = pl.ds(al(core * HALF, HALF), HALF)

    def weights_ready(i):
        s = (i - 1) // 2
        need(f"m{s}", f"p{s}", f"r{s}")
        need(*([f"a{s}", f"b{s}"] if i else ["ax", "vp"]))

    def terms(i):
        weights_ready(i)
        cp = zat(OFFSETS[i])
        w = jnp.concatenate([W[cp * HH + j] for j in range(HH)], axis=1)
        psend[i] = dot(hid[mate_rows, :], w).astype(BF16)
        send(f"pair{i}", psend.at[i], precv.at[i], mate)
        w = jnp.concatenate([W[cp * HH + j] for j in range(HH)], axis=1)
        pown[i] = dot(hid[my_rows, :], w).astype(BF16)

    def group_copy(d, i):
        return pltpu.make_async_remote_copy(
            src_ref=rsend.at[i], dst_ref=rrecv.at[yy, my_rows],
            send_sem=rss.at[d], recv_sem=rsr.at[d],
            device_id=(t, lax.rem(c + d, NC)), device_id_type=MESH,
        )

    def chip_sum(i):
        cp = zat(OFFSETS[i])
        d = lax.rem(cp - c + NC, NC)
        need(f"pair{i}")
        total = pown[i].astype(F32) + precv[i].astype(F32)
        rsend[i] = total.astype(BF16)

        @pl.when(d != 0)
        def _():
            group_copy(d, i).start()

        @pl.when(d == 0)
        def _():
            rrecv[yy, my_rows, :] = rsend[i]

    added = []

    def hidden_grad(i):
        weights_ready(i)
        need("vgc")
        cp = zat(OFFSETS[i])
        added.append(i)
        first, last = len(added) == 1, len(added) == NC

        def part(n, carry):
            rows_n = pl.ds(al(n * 256, 256), 256)
            w = jnp.concatenate([W[cp * HH + j, rows_n, :] for j in range(HH)], axis=1)
            term = dot_t(VG[cp], w)
            if not first:
                term = term + acc[n]
            if last:
                dh_out[:, rows_n] = term.astype(BF16)
            else:
                acc[n] = term
            return carry

        lax.fori_loop(0, COLS // 256, part, 0)

    def delta():
        for d in range(1, NC):
            group_copy(d, 0).wait_recv()
        total = rrecv[0].astype(F32)
        for y in range(1, NC // 2):
            total = total + rrecv[y].astype(F32)
        vbuf[...] = total.astype(BF16)

        def delta_head(h, carry):
            hs = head_cols(h)
            for b, i0, j0, jn in TILES:
                qi = pl.ds(i0, HALF)
                gv = dot_t(vbuf[pl.ds(j0, jn), hs], gs[b, qi, hs])
                gv_ref[b, h, pl.ds(j0, jn), qi] = gv
                w = e_ref[b, h, pl.ds(j0, jn), qi].astype(BF16).astype(F32)
                part = jnp.sum(w * gv, axis=0, keepdims=True)
                table = dl_own if b == 0 else dl_nxt
                table[h, :, qi] = jnp.where(row8 == 0, part, 0.0)
            return carry

        lax.fori_loop(0, HH, delta_head, 0)
        send("dl", dl_own, dl_fn, prv)
        send("dl", dl_nxt, dl_fp, nxt)

    def key():
        need("dl")

        def key_head(h, carry):
            deltas = (
                dl_own[h, pl.ds(0, 1), :] + dl_fp[h, pl.ds(0, 1), :],
                dl_nxt[h, pl.ds(0, 1), :] + dl_fn[h, pl.ds(0, 1), :],
            )
            tiles = []
            for b, i0, j0, jn in TILES:
                qi = pl.ds(i0, HALF)
                p = e_ref[b, h, pl.ds(j0, jn), qi]
                gv = gv_ref[b, h, pl.ds(j0, jn), qi]
                tiles.append((p * (gv - deltas[b][:, i0 : i0 + HALF])).astype(BF16))
            top, bottom = gather_terms(tiles, qs, h)
            hs = head_cols(h)
            dk_out[pl.ds(0, 256), hs] = (top * scale).astype(BF16)
            dk_out[pl.ds(256, 256), hs] = (bottom * scale).astype(BF16)
            return carry

        lax.fori_loop(0, HH, key_head, 0)

    steps = {
        "issue": issue, "i_ax": issue_ax,
        "i_b0": lambda: b_step(0), "i_bm": lambda: spread(-1, 1, "p"), "mm": lambda: spread(-1, 3, "m"),
        "i_k": lambda: regroup("k", k, ks),
        "i_q": lambda: regroup("q", q, qs.at[0]),
        "i_g": lambda: regroup("g", g, gs.at[0]),
        "pos": positions, "LN": norm_glu, "conv": conv, "enc": encode, "adapt": adapt, "place": place,
        "hq": lambda: halo("q"), "hg": lambda: halo("g"),
        "sc0": score_own, "sc1": score_next, "prob": prob, "vgr": vg_relay, "vgf": vg_last,
        "rm": lambda: relay(-1), "delta": delta, "key": key,
    }
    for s in range(4):
        steps[f"a_s{s}"] = lambda s=s: a_step(s)
        steps[f"b_s{s}"] = lambda s=s: b_step(s)
        steps[f"d_s{s}"] = lambda s=s: d_step(s)
        steps[f"p{s}"] = lambda s=s: spread(s, 1, "p")
        steps[f"m{s}"] = lambda s=s: spread(s, 3, "m")
        steps[f"r{s}"] = lambda s=s: relay(s)
    for i in range(NC):
        steps[f"t{i}"] = lambda i=i: terms(i)
        steps[f"rs{i}"] = lambda i=i: chip_sum(i)
        steps[f"dh{i}"] = lambda i=i: hidden_grad(i)
    for name in ORDER:
        steps[name]()

    def audio_sent(d, carry):
        audio_copy(d).wait_send()
        return carry

    lax.fori_loop(1, NT, audio_sent, 0)
    for d in range(1, NC):
        group_copy(d, 0).wait_send()
    for name in groups:
        need(name)
    for copy in sends:
        copy.wait_send()


def body(
    frames, value_weight, gate_weight, conv_taps, out_weight, adapter, audio_pos, text_rows,
    value_proj, queries, keys, grad_out, window_low,
):
    vm = pl.BlockSpec(memory_space=pltpu.VMEM)
    hbm = pl.BlockSpec(memory_space=pl.ANY)
    vmem = pltpu.VMEM
    dma = pltpu.SemaphoreType.DMA
    return pl.pallas_call(
        kernel,
        out_shape=(
            jax.ShapeDtypeStruct((TOK, HC), BF16),
            jax.ShapeDtypeStruct((TOK, COLS), BF16),
        ),
        in_specs=[hbm] * 6 + [vm] * 2 + [hbm] * 5,
        out_specs=(vm, vm),
        scratch_shapes=[
            vmem((NT, COLS, DH), BF16),
            vmem((DE, COLS), BF16),
            vmem((2, TOK, HC), BF16),
            vmem((2, TOK, HC), BF16),
            vmem((TOK, HC), BF16),
            vmem((8, TOK), jnp.int32),
            vmem((8, TOK), jnp.int32),
            vmem((AUD, DE), BF16),
            vmem((DE, DH), BF16),
            vmem((DE, DH), BF16),
            vmem(conv_taps.shape, F32),
            vmem((DH, DE), BF16),
            vmem((TOK, COLS), BF16),
            vmem((8, AUD), jnp.int32),
            vmem((2, 8, NT * 16), jnp.int32),
            vmem((AUD + 32, DE), BF16),
            vmem((AUD + 32, DH), F32),
            vmem((AUD, DE), BF16),
            vmem((NC, 16, DE), BF16),
            vmem((AUD, DE), BF16),
            vmem((AUD, COLS), BF16),
            vmem((NT * 16, 512), BF16),
            vmem((NT * 16, 512), BF16),
            vmem((TOK, COLS), BF16),
            vmem((2, HH, TOK, TOK), F32),
            vmem((2, HH, TOK, TOK), F32),
        ]
        + [vmem((HH, 8, TOK), F32)] * 8
        + [
            vmem((NC, TOK, HC), BF16),
            vmem((NC, HALF, HC), BF16),
            vmem((NC, HALF, HC), BF16),
            vmem((NC, HALF, HC), BF16),
            vmem((NC, HALF, HC), BF16),
            vmem((NC // 2, TOK, HC), BF16),
            vmem((TOK, HC), BF16),
            vmem((COLS // 256, TOK, 256), F32),
            dma((N_SEMS,)),
            dma((N_SEMS,)),
            dma((16,)),
            dma((NT,)),
            dma((NT,)),
            dma((NC,)),
            dma((NC,)),
        ],
        compiler_params=pltpu.CompilerParams(
            collective_id=0, has_side_effects=True, vmem_limit_bytes=60 * 1024 * 1024
        ),
        cost_estimate=pl.CostEstimate(flops=13_000_000_000, bytes_accessed=8_000_000, transcendentals=4_000_000),
    )(
        frames, value_weight, gate_weight, conv_taps, out_weight, text_rows,
        window_low.reshape(1, TOK), audio_pos.reshape(NT, AUD),
        adapter, value_proj, queries, keys, grad_out,
    )


def solution(mesh):
    return jax.shard_map(
        body,
        mesh=mesh,
        in_specs=(
            P("tm", None),
            P(None, "ctx"),
            P(None, "ctx"),
            P(None, "ctx"),
            P("ctx", None),
            P("tm", "ctx"),
            P(),
            P("tm", "ctx"),
            P("ctx", "tm"),
            P(("tm", "ctx"), None),
            P(("tm", "ctx"), None),
            P(("tm", "ctx"), None),
            P("tm"),
        ),
        out_specs=(P("tm", "ctx"), P("tm", "ctx")),
        check_vma=False,
    )
```

```python
import math

import jax
import jax.numpy as jnp
from jax import lax
from jax.experimental import pallas as pl
from jax.experimental.pallas import tpu as pltpu
from jax.sharding import PartitionSpec as P

DH = 128
NORM_EPS = 1e-05
MASK_FILL = -1e30
MESH = pl.DeviceIdType.MESH
F32 = jnp.float32
BF16 = jnp.bfloat16

NT = 32
NC = 8
NX = 4
NZ = 8
TOK = 512
AUD = 128
DE = 1024
COLS = 1024
HC = 512
HH = HC // DH
HALF = TOK // 2
SLOT = 8
TILES = ((0, 0, 0, 256), (0, 256, 0, 512), (1, 0, 0, 512), (1, 256, 256, 256))
N_SEMS = 160
ROWS_A = 352
ROWS_B = COLS - ROWS_A
OFFSETS = (0, -1, 1, -2, 2, -3, 3, 4)
ORDER = (
    "issue", "i_b0", "i_k", "i_q", "i_ax", "mm", "b_s1", "p0", "m0", "LN", "fk", "fq", "conv",
    "i_g", "d_s0", "b_s2", "i_bm", "rm", "hq", "sc0", "b_s3", "pos", "enc", "fg", "d_s1", "r0",
    "p3", "hg", "d_s2", "d_s3", "a_s0", "p1", "sc1", "adapt", "m1", "p2", "m2", "m3", "prob",
    "r1", "a_s1", "r3", "vgr", "place", "t0", "t1", "r2", "vgf", "t2", "rs0", "a_s2", "t3",
    "rs1", "t4", "rs2", "ad0", "dh0", "rs3", "dh1", "ad1", "rs4", "dh2", "dh3", "dh4", "ad2",
    "a_s3", "t5", "ad3", "t6", "ad4", "dh5", "rs5", "dh6", "rs6", "t7", "dh7", "ad5", "ad6",
    "rs7", "ad7", "delta", "key",
)


def dot(a, b):
    return jnp.dot(a, b, preferred_element_type=F32)


def dot_t(a, b):
    return lax.dot_general(a, b, (((1,), (1,)), ((), ())), preferred_element_type=F32)


def iota(shape, dim):
    return lax.broadcasted_iota(jnp.int32, shape, dim)


def kernel(
    frames, vw, gw, taps, ow, text, low, aud, adapter, vp, q, k, g,
    dk_out, dh_out,
    W, AD, qs, gs, ks, low_s, lown, frames_s, vw_s, gw_s, taps_s, ow_s, text_s,
    slot_s, land_s, ext, glu_s, mixs, mixr, enc, adp, pick, inc, hid,
    e_ref, gv_ref, st_own, st_nxt, st_fp, st_fn, dl_own, dl_nxt, dl_fp, dl_fn,
    VG, psend, pown, precv, rsend, radd, rrecv, vbuf, acc, stage,
    ssem, rsem, lsem, aus, aur, rss, rsr,
):
    t = lax.axis_index("tm")
    c = lax.axis_index("ctx")
    x = lax.rem(t, NX)
    z = lax.div(t, NX)
    core = lax.rem(c, 2)
    yy = lax.div(c, 2)
    up = (lax.rem(z + 1, NZ) * NX + x, c)
    dn = (lax.rem(z + NZ - 1, NZ) * NX + x, c)
    nxt = (lax.rem(t + 1, NT), c)
    prv = (lax.rem(t + NT - 1, NT), c)
    mate = (t, c + 1 - 2 * core)

    def ctx_peer(d):
        return (t, lax.rem(c + d, NC))

    def x_peer(d):
        return (z * NX + lax.rem(x + d, NX), c)

    def zat(d):
        return lax.rem(z + d + NZ, NZ)

    def al(v, m):
        return pl.multiple_of(v, m)

    sends = []
    groups = {}
    waited = set()

    def send(name, src, dst, dev):
        i = len(sends)
        copy = pltpu.make_async_remote_copy(
            src_ref=src, dst_ref=dst, send_sem=ssem.at[i], recv_sem=rsem.at[i],
            device_id=dev, device_id_type=MESH,
        )
        copy.start()
        sends.append(copy)
        groups.setdefault(name, []).append(copy)

    def need(*names):
        for name in names:
            if name not in waited:
                waited.add(name)
                for copy in groups[name]:
                    if name in here:
                        copy.wait()
                    else:
                        copy.wait_recv()

    here = set()

    def local(name, src, dst):
        copy = pltpu.make_async_copy(src, dst, lsem.at[len(here)])
        copy.start()
        here.add(name)
        groups[name] = [copy]

    own_rows = pl.ds(al(c * 64, 64), 64)
    own_cols = pl.ds(al(c * HC, HC), HC)
    ad_rows = pl.ds(al(t * 32, 32), 32)
    rows_a = pl.ds(0, ROWS_A)
    rows_b = pl.ds(ROWS_A, ROWS_B)

    def issue():
        bar = pltpu.get_barrier_semaphore()

        def greet(d, carry):
            pl.semaphore_signal(bar, inc=1, device_id=(lax.rem(t + d, NT), c), device_id_type=MESH)
            return carry

        lax.fori_loop(1, NT, greet, 0)
        for d in range(1, NC):
            pl.semaphore_signal(bar, inc=1, device_id=ctx_peer(d), device_id_type=MESH)
        local("frames", frames, frames_s)
        local("vw", vw, vw_s)
        local("gw", gw, gw_s)
        local("vp", vp, W.at[t])
        local("ad", adapter, AD.at[ad_rows])
        local("taps", taps, taps_s)
        local("ow", ow, ow_s)
        local("k0", k.at[:, own_cols], ks.at[own_rows])
        local("q0", q.at[:, own_cols], qs.at[0, own_rows])
        local("g0", g.at[:, own_cols], gs.at[0, own_rows])
        local("text", text, text_s)
        low_s[...] = jnp.broadcast_to(low[...], low_s.shape)
        pl.semaphore_wait(bar, NT - 1 + NC - 1)
        send("fh", frames.at[pl.ds(AUD - 16, 16)], ext.at[pl.ds(0, 16)], nxt)
        send("fh", frames.at[pl.ds(0, 16)], ext.at[pl.ds(AUD + 16, 16)], prv)
        for d in (1, 3, 2):
            send("adx", adapter, AD.at[ad_rows], x_peer(d))
        send("low", low_s, lown, prv)

    def b_ref(zz, xx=x):
        return W.at[zz * NX + xx, rows_b]

    def b_part(zz, p):
        return W.at[zz * NX + x, pl.ds(ROWS_A + ROWS_B // 2 * p, ROWS_B // 2)]

    def a_ref(zz):
        return W.at[pl.ds(zz * NX, NX), rows_a]

    def a_part(zz, p):
        return W.at[pl.ds(zz * NX + 2 * p, 2), rows_a]

    def d_ref(zz):
        return AD.at[pl.ds(al(zz * 128, 128), 128)]

    def d_part(zz, p):
        return AD.at[pl.ds(al(zz * 128 + 64 * p, 64), 64)]

    def ring(name, s, ref_of, part_of):
        if s < NZ // 2 - 1:
            u, v = ref_of(zat(-s)), ref_of(zat(s))
        else:
            u, v = part_of(zat(-s), 0), part_of(zat(s), 1)
        send(f"{name}{s}", u, u, up)
        send(f"{name}{s}", v, v, dn)

    def a_step(s):
        need(*([f"a{s - 1}"] if s else ["ax", "vp"]))
        ring("a", s, a_ref, a_part)

    def b_step(s):
        need(*([f"b{s - 1}"] if s else ["vp"]))
        ring("b", s, b_ref, b_part)

    def d_step(s):
        need(*([f"d{s - 1}"] if s else ["adx", "ad"]))
        ring("d", s, d_ref, d_part)

    def reached(s):
        return (0,) if s < 0 else ((-1 - s, 1 + s) if s < 3 else (4,))

    def spread(s, d, kind):
        need(f"b{s}" if s >= 0 else "vp")
        for o in reached(s):
            send(f"{kind}{s}", b_ref(zat(o)), b_ref(zat(o)), x_peer(d))

    def relay(s):
        turn = 3 if s in (-1, 3) else 1
        need(f"p{s}" if turn == 1 else f"m{s}")
        origin = lax.rem(x + NX - turn, NX)
        for o in reached(s):
            send(f"r{s}", b_ref(zat(o), origin), b_ref(zat(o), origin), x_peer(turn))

    def issue_ax():
        for d in (1, 3, 2):
            send("ax", vp.at[rows_a], W.at[t, rows_a], x_peer(d))

    def beside(cc):
        return cc + 1 - 2 * core

    def regroup(name, src, dst, stage):
        y_up, y_dn, far = [lax.rem(c + d, NC) for d in (2, 6, 4)]

        def piece(peer):
            return src.at[:, pl.ds(al(peer * HC, HC), HC)]

        send(name + "s", piece(far), stage.at[0], (t, y_up))
        send(name + "s", piece(beside(far)), stage.at[1], (t, y_dn))
        for peer in (y_up, y_dn, beside(y_up), beside(y_dn), beside(c)):
            send(name, piece(peer), dst.at[own_rows], (t, peer))

    def regroup_relay(name, dst, stage):
        need(name + "s")
        y_up, y_dn = [lax.rem(c + d, NC) for d in (2, 6)]
        send(name + "2", stage.at[0], dst.at[pl.ds(al(y_dn * 64, 64), 64)], (t, y_up))
        send(name + "2", stage.at[1], dst.at[pl.ds(al(y_up * 64, 64), 64)], (t, beside(y_dn)))

    def positions():
        order = (iota((AUD, AUD), 0) < iota((AUD, AUD), 1)).astype(F32).astype(BF16)
        own = aud[pl.ds(t, 1), :]
        target = own // TOK
        hit = (iota((NT, AUD), 0) == target).astype(F32)
        rank = jnp.sum(dot(hit.astype(BF16), order) * hit, axis=0, keepdims=True)
        slot = target * SLOT + rank.astype(jnp.int32)
        slot_s[...] = jnp.broadcast_to(slot, slot_s.shape)
        table = aud[...]
        landing = table // TOK == t
        landing_rank = dot(landing.astype(F32).astype(BF16), order)
        spot = jnp.where(landing, table - t * TOK + 1, 0)
        n = NT * 16
        grow = (iota((n, NT), 0) // 16 == iota((n, NT), 1)).astype(F32).astype(BF16)
        spot_hi = dot(grow, (spot // 16).astype(F32).astype(BF16))
        spot_lo = dot(grow, (spot % 16).astype(F32).astype(BF16))
        ranks = dot(grow, jnp.where(landing, landing_rank, 64.0).astype(BF16))
        place = spot_hi * 16.0 + spot_lo
        r = (iota((n, AUD), 0) % 16).astype(F32)
        eye = iota((n, n), 0) == iota((n, n), 1)
        for half in range(2):
            col = jnp.sum(jnp.where(ranks == r - 8.0 * half, place, 0.0), axis=1, keepdims=True) - 1.0
            line = jnp.sum(jnp.where(eye, col, 0.0), axis=0, keepdims=True)
            land_s[half] = jnp.broadcast_to(line, (8, n)).astype(jnp.int32)

    def norm_glu():
        need("frames", "vw", "gw")
        ext[pl.ds(16, AUD), :] = frames_s[...]
        need("fh")
        rows = ext[...].astype(F32)
        centre = jnp.mean(rows, axis=1, keepdims=True)
        off = rows - centre
        spread_ = jnp.mean(off * off, axis=1, keepdims=True)
        normed = (off * lax.rsqrt(spread_ + NORM_EPS)).astype(BF16)
        value_part = dot(normed, vw_s[...])
        gate_part = dot(normed, gw_s[...])
        glu = (value_part * jax.nn.sigmoid(gate_part)).astype(BF16).astype(F32)
        row = iota(glu.shape, 0)
        first = jnp.where(t == 0, 16, 0)
        last = jnp.where(t == NT - 1, AUD + 16, AUD + 32)
        glu_s[...] = jnp.where((row >= first) & (row < last), glu, 0.0)

    def conv():
        need("taps", "ow")
        smooth = jnp.zeros((AUD, DH), F32)
        for j in range(taps_s.shape[0]):
            smooth = smooth + taps_s[pl.ds(j, 1), :] * glu_s[pl.ds(1 + j, AUD), :]
        action = (smooth * jax.nn.sigmoid(smooth)).astype(BF16)
        mixs[...] = dot(action, ow_s[...]).astype(BF16)
        for d in (4, 2, 6, 3, 5, 1, 7):
            rows_d = pl.ds(al(lax.rem(c + d, NC) * 16, 16), 16)
            send("mix", mixs.at[rows_d], mixr.at[d], ctx_peer(d))

    def encode():
        need("mix")
        mine = pl.ds(al(c * 16, 16), 16)
        total = frames_s[mine, :].astype(F32) + mixs[mine, :].astype(F32)
        for d in range(1, NC):
            total = total + mixr[d].astype(F32)
        enc[mine, :] = total.astype(BF16)
        for d in (4, 2, 6, 3, 5, 1, 7):
            send("enc", enc.at[mine], enc.at[mine], ctx_peer(d))

    def halo(name):
        part = qs if name == "q" else gs
        need(name, name + "2", name + "0")
        send("h" + name, part.at[0], part.at[1], prv)

    scale = 1.0 / math.sqrt(DH)
    base = t * TOK
    row8 = iota((8, HALF), 0)

    def head_cols(h):
        return pl.ds(al(h * DH, DH), DH)

    def score_tiles(block, lows, limit, stats):
        def one_head(h, carry):
            hs = head_cols(h)
            for b, i0, j0, jn in TILES:
                if b != block:
                    continue
                qi = pl.ds(i0, HALF)
                s = dot_t(ks[pl.ds(j0, jn), hs], qs[b, qi, hs]) * scale
                jj = iota((jn, HALF), 0) + j0
                ok = jj >= lows[pl.ds(0, 1), qi] - base
                if block == 0:
                    ok = ok & (jj <= iota((jn, HALF), 1) + i0)
                else:
                    ok = ok & (jj < limit)
                s = jnp.where(ok, s, MASK_FILL)
                m = jnp.max(s, axis=0, keepdims=True)
                e = jnp.where(ok, jnp.exp(s - m), 0.0)
                n = jnp.sum(e, axis=0, keepdims=True)
                e_ref[b, h, pl.ds(j0, jn), qi] = e
                stats[h, :, qi] = jnp.where(row8 == 0, m, n)
            return carry

        lax.fori_loop(0, HH, one_head, 0)

    def score_own():
        need("k", "k2", "k0", "q", "q2", "q0")
        score_tiles(0, low_s, TOK, st_own)
        send("sta", st_own, st_fn, prv)

    def score_next():
        need("k", "k2", "k0", "hq", "low")
        score_tiles(1, lown, jnp.where(t == NT - 1, 0, TOK), st_nxt)
        send("stb", st_nxt, st_fp, nxt)

    my_slot = pl.ds(al(t * 16, 16), 16)

    def audio_copy(d):
        peer = lax.rem(t + d, NT)
        return pltpu.make_async_remote_copy(
            src_ref=pick.at[pl.ds(al(peer * 16, 16), 16)], dst_ref=inc.at[my_slot],
            send_sem=aus.at[d], recv_sem=aur.at[d], device_id=(peer, c), device_id_type=MESH,
        )

    def adapt():
        need("d3", "enc")
        for n in range(4):
            cols = pl.ds(256 * n, 256)
            adp[:, cols] = dot(enc[...], AD[:, cols]).astype(BF16)
        slot_row = iota((NT * 16, AUD), 0)
        picker = ((slot_row // 16) * SLOT + slot_row % SLOT == slot_s[pl.ds(0, 1), :]).astype(F32)
        picker = picker.astype(BF16)
        low_half = dot(picker, adp[:, pl.ds(0, 512)])
        high_half = dot(picker, adp[:, pl.ds(512, 512)])
        upper = iota((NT * 16, 512), 0) % 16 < SLOT
        pick[...] = jnp.where(upper, low_half, high_half).astype(BF16)

        def audio_start(d, carry):
            audio_copy(d).start()
            return carry

        lax.fori_loop(1, NT, audio_start, 0)
        inc[my_slot, :] = pick[my_slot, :]

    def factor(mine_st, other_st, h):
        m1, s1 = mine_st[h, pl.ds(0, 1), :], mine_st[h, pl.ds(1, 1), :]
        m2, s2 = other_st[h, pl.ds(0, 1), :], other_st[h, pl.ds(1, 1), :]
        m = jnp.maximum(m1, m2)
        a1 = jnp.exp(m1 - m)
        return a1 / (s1 * a1 + s2 * jnp.exp(m2 - m))

    def gather_terms(tiles, other, h):
        hs = head_cols(h)
        first, second = pl.ds(0, 256), pl.ds(256, 256)
        top = dot(tiles[0], other[0, first, hs]) + dot(tiles[1][:256], other[0, second, hs])
        top = top + dot(tiles[2][:256], other[1, first, hs])
        bottom = dot(tiles[1][256:], other[0, second, hs])
        bottom = bottom + dot(tiles[2][256:], other[1, first, hs])
        bottom = bottom + dot(tiles[3], other[1, second, hs])
        return top, bottom

    def prob():
        need("sta", "stb", "g", "g2", "g0", "hg")

        def prob_head(h, carry):
            f = (factor(st_own, st_fp, h), factor(st_nxt, st_fn, h))
            tiles = []
            for b, i0, j0, jn in TILES:
                p = e_ref[b, h, pl.ds(j0, jn), pl.ds(i0, HALF)] * f[b][:, i0 : i0 + HALF]
                e_ref[b, h, pl.ds(j0, jn), pl.ds(i0, HALF)] = p
                tiles.append(p.astype(BF16))
            top, bottom = gather_terms(tiles, gs, h)
            hs = head_cols(h)
            VG[c, pl.ds(0, 256), hs] = top.astype(BF16)
            VG[c, pl.ds(256, 256), hs] = bottom.astype(BF16)
            return carry

        lax.fori_loop(0, HH, prob_head, 0)
        send("vg1", VG.at[c], VG.at[c], ctx_peer(2))
        send("vg3", VG.at[c], VG.at[c], ctx_peer(6))
        send("vgc", VG.at[c], VG.at[c], mate)

    below, above, across = [lax.rem(c + d, NC) for d in (6, 2, 4)]

    def vg_relay():
        need("vg1", "vg3")
        one, two = VG.at[below, pl.ds(0, 256)], VG.at[above, pl.ds(256, 256)]
        send("vg2", one, one, ctx_peer(2))
        send("vg2", two, two, ctx_peer(6))
        send("vgc", VG.at[below], VG.at[below], mate)
        send("vgc", VG.at[above], VG.at[above], mate)

    def vg_last():
        need("vg2")
        send("vgc", VG.at[across], VG.at[across], mate)

    def place():
        need("text")

        def audio_arrived(d, carry):
            audio_copy(d).wait_recv()
            return carry

        lax.fori_loop(1, NT, audio_arrived, 0)
        for half in range(2):
            cols = pl.ds(512 * half, 512)
            hits = (iota((TOK, NT * 16), 0) == land_s[half, pl.ds(0, 1), :]).astype(F32)
            there = jnp.sum(hits, axis=1, keepdims=True) > 0.5
            rows_in = dot(hits.astype(BF16), inc[...])
            hid[:, cols] = jnp.where(there, rows_in, text_s[:, cols].astype(F32)).astype(BF16)

    mate_rows = pl.ds(al((1 - core) * HALF, HALF), HALF)
    my_rows = pl.ds(al(core * HALF, HALF), HALF)

    def weights_ready(i):
        s = (i - 1) // 2
        need(f"m{s}", f"p{s}", f"r{s}")
        need(*([f"a{s}", f"b{s}"] if i else ["ax", "vp"]))

    def terms(i):
        weights_ready(i)
        cp = zat(OFFSETS[i])
        w = jnp.concatenate([W[cp * HH + j] for j in range(HH)], axis=1)
        psend[i] = dot(hid[mate_rows, :], w).astype(BF16)
        send(f"pair{i}", psend.at[i], precv.at[i], mate)
        w = jnp.concatenate([W[cp * HH + j] for j in range(HH)], axis=1)
        pown[i] = dot(hid[my_rows, :], w).astype(BF16)

    def owner_copy(side, kd, i):
        owner = lax.rem(yy + 1 + 2 * side, NC // 2) * 2 + kd
        return pltpu.make_async_remote_copy(
            src_ref=rsend.at[i], dst_ref=rrecv.at[1 + side, my_rows],
            send_sem=rss.at[2 * side + kd], recv_sem=rsr.at[2 * side + core],
            device_id=(t, owner), device_id_type=MESH,
        )

    def add_copy(kd, i):
        return pltpu.make_async_remote_copy(
            src_ref=rsend.at[i], dst_ref=radd.at[kd],
            send_sem=rss.at[4 + kd], recv_sem=rsr.at[4 + kd],
            device_id=(t, lax.rem(c + 2 + 4 * core, NC)), device_id_type=MESH,
        )

    def mate_copy(i):
        return pltpu.make_async_remote_copy(
            src_ref=rsend.at[i], dst_ref=rrecv.at[0, my_rows],
            send_sem=rss.at[6], recv_sem=rsr.at[6], device_id=mate, device_id_type=MESH,
        )

    def owner_of(i):
        cp = zat(OFFSETS[i])
        return lax.rem(lax.div(cp, 2) - yy + NC // 2, NC // 2), lax.rem(cp, 2)

    def chip_sum(i):
        e, kd = owner_of(i)
        need(f"pair{i}")
        total = pown[i].astype(F32) + precv[i].astype(F32)
        rsend[i] = total.astype(BF16)

        @pl.when(e == 2)
        def _():
            add_copy(kd, i).start()

        @pl.when(e == 3 - 2 * core)
        def _():
            owner_copy(lax.div(e, 2), kd, i).start()

        @pl.when((e == 0) & (kd != core))
        def _():
            mate_copy(i).start()

        @pl.when((e == 0) & (kd == core))
        def _():
            rrecv[0, my_rows, :] = rsend[i]

    def added_sum(i):
        e, kd = owner_of(i)

        @pl.when(e == 1 + 2 * core)
        def _():
            add_copy(kd, i).wait_recv()
            total = rsend[i].astype(F32) + radd[kd].astype(F32)
            rsend[i] = total.astype(BF16)
            owner_copy(lax.div(e, 2), kd, i).start()

    added = []

    def hidden_grad(i):
        weights_ready(i)
        need("vgc")
        cp = zat(OFFSETS[i])
        added.append(i)
        first, last = len(added) == 1, len(added) == NC

        def part(n, carry):
            rows_n = pl.ds(al(n * 256, 256), 256)
            w = jnp.concatenate([W[cp * HH + j, rows_n, :] for j in range(HH)], axis=1)
            term = dot_t(VG[cp], w)
            if not first:
                term = term + acc[n]
            if last:
                dh_out[:, rows_n] = term.astype(BF16)
            else:
                acc[n] = term
            return carry

        lax.fori_loop(0, COLS // 256, part, 0)

    def delta():
        for n in (0, 1, 2, 3, 6):
            pltpu.make_async_remote_copy(
                src_ref=rsend.at[0], dst_ref=rrecv.at[0, my_rows], send_sem=rss.at[n],
                recv_sem=rsr.at[n], device_id=mate, device_id_type=MESH,
            ).wait_recv()
        total = rrecv[0].astype(F32) + rrecv[1].astype(F32) + rrecv[2].astype(F32)
        vbuf[...] = total.astype(BF16)

        def delta_head(h, carry):
            hs = head_cols(h)
            for b, i0, j0, jn in TILES:
                qi = pl.ds(i0, HALF)
                gv = dot_t(vbuf[pl.ds(j0, jn), hs], gs[b, qi, hs])
                gv_ref[b, h, pl.ds(j0, jn), qi] = gv
                w = e_ref[b, h, pl.ds(j0, jn), qi].astype(BF16).astype(F32)
                part = jnp.sum(w * gv, axis=0, keepdims=True)
                table = dl_own if b == 0 else dl_nxt
                table[h, :, qi] = jnp.where(row8 == 0, part, 0.0)
            return carry

        lax.fori_loop(0, HH, delta_head, 0)
        send("dl", dl_own, dl_fn, prv)
        send("dl", dl_nxt, dl_fp, nxt)

    def key():
        need("dl")

        def key_head(h, carry):
            deltas = (
                dl_own[h, pl.ds(0, 1), :] + dl_fp[h, pl.ds(0, 1), :],
                dl_nxt[h, pl.ds(0, 1), :] + dl_fn[h, pl.ds(0, 1), :],
            )
            tiles = []
            for b, i0, j0, jn in TILES:
                qi = pl.ds(i0, HALF)
                p = e_ref[b, h, pl.ds(j0, jn), qi]
                gv = gv_ref[b, h, pl.ds(j0, jn), qi]
                tiles.append((p * (gv - deltas[b][:, i0 : i0 + HALF])).astype(BF16))
            top, bottom = gather_terms(tiles, qs, h)
            hs = head_cols(h)
            dk_out[pl.ds(0, 256), hs] = (top * scale).astype(BF16)
            dk_out[pl.ds(256, 256), hs] = (bottom * scale).astype(BF16)
            return carry

        lax.fori_loop(0, HH, key_head, 0)

    steps = {
        "issue": issue, "i_ax": issue_ax,
        "i_b0": lambda: b_step(0), "i_bm": lambda: spread(-1, 1, "p"), "mm": lambda: spread(-1, 3, "m"),
        "i_k": lambda: regroup("k", k, ks, stage.at[0]),
        "i_q": lambda: regroup("q", q, qs.at[0], stage.at[1]),
        "i_g": lambda: regroup("g", g, gs.at[0], stage.at[2]),
        "fk": lambda: regroup_relay("k", ks, stage.at[0]),
        "fq": lambda: regroup_relay("q", qs.at[0], stage.at[1]),
        "fg": lambda: regroup_relay("g", gs.at[0], stage.at[2]),
        "pos": positions, "LN": norm_glu, "conv": conv, "enc": encode, "adapt": adapt, "place": place,
        "hq": lambda: halo("q"), "hg": lambda: halo("g"),
        "sc0": score_own, "sc1": score_next, "prob": prob, "vgr": vg_relay, "vgf": vg_last,
        "rm": lambda: relay(-1), "delta": delta, "key": key,
    }
    for s in range(4):
        steps[f"a_s{s}"] = lambda s=s: a_step(s)
        steps[f"b_s{s}"] = lambda s=s: b_step(s)
        steps[f"d_s{s}"] = lambda s=s: d_step(s)
        steps[f"p{s}"] = lambda s=s: spread(s, 1, "p")
        steps[f"m{s}"] = lambda s=s: spread(s, 3, "m")
        steps[f"r{s}"] = lambda s=s: relay(s)
    for i in range(NC):
        steps[f"t{i}"] = lambda i=i: terms(i)
        steps[f"rs{i}"] = lambda i=i: chip_sum(i)
        steps[f"ad{i}"] = lambda i=i: added_sum(i)
        steps[f"dh{i}"] = lambda i=i: hidden_grad(i)
    for name in ORDER:
        steps[name]()

    def audio_sent(d, carry):
        audio_copy(d).wait_send()
        return carry

    lax.fori_loop(1, NT, audio_sent, 0)
    for n in range(7):
        pltpu.make_async_remote_copy(
            src_ref=rsend.at[0], dst_ref=rrecv.at[0, my_rows], send_sem=rss.at[n],
            recv_sem=rsr.at[n], device_id=mate, device_id_type=MESH,
        ).wait_send()
    for name in groups:
        need(name)
    for copy in sends:
        copy.wait_send()


def body(
    frames, value_weight, gate_weight, conv_taps, out_weight, adapter, audio_pos, text_rows,
    value_proj, queries, keys, grad_out, window_low,
):
    vm = pl.BlockSpec(memory_space=pltpu.VMEM)
    hbm = pl.BlockSpec(memory_space=pl.ANY)
    vmem = pltpu.VMEM
    dma = pltpu.SemaphoreType.DMA
    return pl.pallas_call(
        kernel,
        out_shape=(
            jax.ShapeDtypeStruct((TOK, HC), BF16),
            jax.ShapeDtypeStruct((TOK, COLS), BF16),
        ),
        in_specs=[hbm] * 6 + [vm] * 2 + [hbm] * 5,
        out_specs=(vm, vm),
        scratch_shapes=[
            vmem((NT, COLS, DH), BF16),
            vmem((DE, COLS), BF16),
            vmem((2, TOK, HC), BF16),
            vmem((2, TOK, HC), BF16),
            vmem((TOK, HC), BF16),
            vmem((8, TOK), jnp.int32),
            vmem((8, TOK), jnp.int32),
            vmem((AUD, DE), BF16),
            vmem((DE, DH), BF16),
            vmem((DE, DH), BF16),
            vmem(conv_taps.shape, F32),
            vmem((DH, DE), BF16),
            vmem((TOK, COLS), BF16),
            vmem((8, AUD), jnp.int32),
            vmem((2, 8, NT * 16), jnp.int32),
            vmem((AUD + 32, DE), BF16),
            vmem((AUD + 32, DH), F32),
            vmem((AUD, DE), BF16),
            vmem((NC, 16, DE), BF16),
            vmem((AUD, DE), BF16),
            vmem((AUD, COLS), BF16),
            vmem((NT * 16, 512), BF16),
            vmem((NT * 16, 512), BF16),
            vmem((TOK, COLS), BF16),
            vmem((2, HH, TOK, TOK), F32),
            vmem((2, HH, TOK, TOK), F32),
        ]
        + [vmem((HH, 8, TOK), F32)] * 8
        + [
            vmem((NC, TOK, HC), BF16),
            vmem((NC, HALF, HC), BF16),
            vmem((NC, HALF, HC), BF16),
            vmem((NC, HALF, HC), BF16),
            vmem((NC, HALF, HC), BF16),
            vmem((2, HALF, HC), BF16),
            vmem((3, TOK, HC), BF16),
            vmem((TOK, HC), BF16),
            vmem((COLS // 256, TOK, 256), F32),
            vmem((3, 2, 64, HC), BF16),
            dma((N_SEMS,)),
            dma((N_SEMS,)),
            dma((16,)),
            dma((NT,)),
            dma((NT,)),
            dma((NC,)),
            dma((NC,)),
        ],
        compiler_params=pltpu.CompilerParams(
            collective_id=0, has_side_effects=True, vmem_limit_bytes=60 * 1024 * 1024
        ),
        cost_estimate=pl.CostEstimate(flops=13_000_000_000, bytes_accessed=8_000_000, transcendentals=4_000_000),
    )(
        frames, value_weight, gate_weight, conv_taps, out_weight, text_rows,
        window_low.reshape(1, TOK), audio_pos.reshape(NT, AUD),
        adapter, value_proj, queries, keys, grad_out,
    )


def solution(mesh):
    return jax.shard_map(
        body,
        mesh=mesh,
        in_specs=(
            P("tm", None),
            P(None, "ctx"),
            P(None, "ctx"),
            P(None, "ctx"),
            P("ctx", None),
            P("tm", "ctx"),
            P(),
            P("tm", "ctx"),
            P("ctx", "tm"),
            P(("tm", "ctx"), None),
            P(("tm", "ctx"), None),
            P(("tm", "ctx"), None),
            P("tm"),
        ),
        out_specs=(P("tm", "ctx"), P("tm", "ctx")),
        check_vma=False,
    )
```

```python
import math

import jax
import jax.numpy as jnp
from jax import lax
from jax.experimental import pallas as pl
from jax.experimental.pallas import tpu as pltpu
from jax.sharding import PartitionSpec as P

DH = 128
NORM_EPS = 1e-05
MASK_FILL = -1e30
MESH = pl.DeviceIdType.MESH
F32 = jnp.float32
BF16 = jnp.bfloat16

NT = 32
NC = 8
NX = 4
NZ = 8
TOK = 512
AUD = 128
DE = 1024
COLS = 1024
HC = 512
HH = HC // DH
HALF = TOK // 2
SLOT = 8
TILES = ((0, 0, 0, 256), (0, 256, 0, 512), (1, 0, 0, 512), (1, 256, 256, 256))


def dot(a, b):
    return jnp.dot(a, b, preferred_element_type=F32)


def dot_t(a, b):
    return lax.dot_general(a, b, (((1,), (1,)), ((), ())), preferred_element_type=F32)


def iota(shape, dim):
    return lax.broadcasted_iota(jnp.int32, shape, dim)


class Wires:
    def __init__(self, ssem, rsem, lsem):
        self.ssem, self.rsem, self.lsem = ssem, rsem, lsem
        self.sent, self.groups, self.waited, self.locals_ = [], {}, set(), 0

    def send(self, name, src, dst, dev):
        i = len(self.sent)
        copy = pltpu.make_async_remote_copy(
            src_ref=src, dst_ref=dst, send_sem=self.ssem.at[i], recv_sem=self.rsem.at[i],
            device_id=dev, device_id_type=MESH,
        )
        copy.start()
        self.sent.append(copy)
        self.groups.setdefault(name, []).append(copy.wait_recv)

    def local(self, name, src, dst):
        copy = pltpu.make_async_copy(src, dst, self.lsem.at[self.locals_])
        self.locals_ += 1
        copy.start()
        self.groups.setdefault(name, []).append(copy.wait)

    def need(self, *names):
        for name in names:
            if name not in self.waited:
                self.waited.add(name)
                for wait in self.groups[name]:
                    wait()

    def finish(self):
        self.need(*self.groups)
        for copy in self.sent:
            copy.wait_send()


class Place:
    def __init__(self):
        t, c = lax.axis_index("tm"), lax.axis_index("ctx")
        self.t, self.c = t, c
        self.x, self.z = lax.rem(t, NX), lax.div(t, NX)
        self.core, self.yy = lax.rem(c, 2), lax.div(c, 2)
        self.up = (lax.rem(self.z + 1, NZ) * NX + self.x, c)
        self.dn = (lax.rem(self.z + NZ - 1, NZ) * NX + self.x, c)
        self.nxt = (lax.rem(t + 1, NT), c)
        self.prv = (lax.rem(t + NT - 1, NT), c)
        self.y_up, self.y_dn, self.far = [lax.rem(c + d, NC) for d in (2, 6, 4)]

    def ctx_peer(self, d):
        return (self.t, lax.rem(self.c + d, NC))

    def x_peer(self, d):
        return (self.z * NX + lax.rem(self.x + d, NX), self.c)

    def zat(self, d):
        return lax.rem(self.z + d + NZ, NZ)

    def beside(self, cc):
        return cc + 1 - 2 * self.core

    def mate(self):
        return (self.t, self.beside(self.c))


def al(v, m):
    return pl.multiple_of(v, m)


def signal_to(bar, dev):
    pl.semaphore_signal(bar, inc=1, device_id=dev, device_id_type=MESH)


def head_cols(h):
    return pl.ds(al(h * DH, DH), DH)


def gather_terms(tiles, other, h):
    hs = head_cols(h)
    first, second = pl.ds(0, 256), pl.ds(256, 256)
    top = dot(tiles[0], other[0, first, hs]) + dot(tiles[1][:256], other[0, second, hs])
    top = top + dot(tiles[2][:256], other[1, first, hs])
    bottom = dot(tiles[1][256:], other[0, second, hs])
    bottom = bottom + dot(tiles[2][256:], other[1, first, hs])
    bottom = bottom + dot(tiles[3], other[1, second, hs])
    return top, bottom


SCALE = 1.0 / math.sqrt(DH)


def kernel_a(
    frames, vw, gw, taps, ow, low, adapter, q, k, g,
    enc_o, AD, ks, qs, gs, lown,
    frames_s, vw_s, gw_s, taps_s, ow_s, low_s, ext, glu_s, mixs, mixr, enc_s, stage,
    ssem, rsem, lsem,
):
    me = Place()
    w = Wires(ssem, rsem, lsem)
    t, c = me.t, me.c
    own_rows = pl.ds(al(c * 64, 64), 64)
    own_cols = pl.ds(al(c * HC, HC), HC)
    ad_rows = pl.ds(al(t * 32, 32), 32)

    bar = pltpu.get_barrier_semaphore()
    for dev in (me.up, me.dn, me.nxt, me.prv):
        signal_to(bar, dev)
    for d in range(1, NX):
        signal_to(bar, me.x_peer(d))
    for d in range(1, NC):
        signal_to(bar, me.ctx_peer(d))
    w.local("frames", frames, frames_s)
    w.local("vw", vw, vw_s)
    w.local("gw", gw, gw_s)
    w.local("ad", adapter, AD.at[ad_rows])
    w.local("taps", taps, taps_s)
    w.local("ow", ow, ow_s)
    w.local("q0", q.at[:, own_cols], qs.at[0, own_rows])
    w.local("k0", k.at[:, own_cols], ks.at[own_rows])
    w.local("g0", g.at[:, own_cols], gs.at[own_rows])
    low_s[...] = jnp.broadcast_to(low[...], low_s.shape)
    pl.semaphore_wait(bar, 4 + NX - 1 + NC - 1)
    w.send("fh", frames.at[pl.ds(AUD - 16, 16)], ext.at[pl.ds(0, 16)], me.nxt)
    w.send("fh", frames.at[pl.ds(0, 16)], ext.at[pl.ds(AUD + 16, 16)], me.prv)
    for d in (1, 3, 2):
        w.send("adx", adapter, AD.at[ad_rows], me.x_peer(d))
    w.send("low", low_s, lown, me.prv)

    def d_step(s):
        def rows(zz, at, n):
            return AD.at[pl.ds(al(zz * 128 + at, 64), n)]

        if s < NZ // 2 - 1:
            u, v = rows(me.zat(-s), 0, 128), rows(me.zat(s), 0, 128)
        else:
            u, v = rows(me.zat(-s), 0, 64), rows(me.zat(s), 64, 64)
        w.send(f"d{s}", u, u, me.up)
        w.send(f"d{s}", v, v, me.dn)

    def regroup(name, src, dst, st):
        def piece(peer):
            return src.at[:, pl.ds(al(peer * HC, HC), HC)]

        w.send(name + "s", piece(me.far), st.at[0], (t, me.y_up))
        w.send(name + "s", piece(me.beside(me.far)), st.at[1], (t, me.y_dn))
        for peer in (me.y_up, me.y_dn, me.beside(me.y_up), me.beside(me.y_dn), me.beside(c)):
            w.send(name, piece(peer), dst.at[own_rows], (t, peer))

    def regroup_relay(name, dst, st):
        w.need(name + "s")
        w.send(name + "2", st.at[0], dst.at[pl.ds(al(me.y_dn * 64, 64), 64)], (t, me.y_up))
        w.send(name + "2", st.at[1], dst.at[pl.ds(al(me.y_up * 64, 64), 64)], (t, me.beside(me.y_dn)))

    regroup("q", q, qs.at[0], stage.at[0])
    regroup("k", k, ks, stage.at[1])

    w.need("frames", "vw", "gw")
    ext[pl.ds(16, AUD), :] = frames_s[...]
    w.need("fh")
    rows = ext[...].astype(F32)
    centre = jnp.mean(rows, axis=1, keepdims=True)
    off = rows - centre
    spread = jnp.mean(off * off, axis=1, keepdims=True)
    normed = (off * lax.rsqrt(spread + NORM_EPS)).astype(BF16)
    value_part = dot(normed, vw_s[...])
    gate_part = dot(normed, gw_s[...])
    glu = (value_part * jax.nn.sigmoid(gate_part)).astype(BF16).astype(F32)
    row = iota(glu.shape, 0)
    first = jnp.where(t == 0, 16, 0)
    last = jnp.where(t == NT - 1, AUD + 16, AUD + 32)
    glu_s[...] = jnp.where((row >= first) & (row < last), glu, 0.0)
    w.need("ad", "adx")
    d_step(0)

    w.need("taps", "ow")
    smooth = jnp.zeros((AUD, DH), F32)
    for j in range(taps_s.shape[0]):
        smooth = smooth + taps_s[pl.ds(j, 1), :] * glu_s[pl.ds(1 + j, AUD), :]
    action = (smooth * jax.nn.sigmoid(smooth)).astype(BF16)
    mixs[...] = dot(action, ow_s[...]).astype(BF16)
    for d in (4, 2, 6, 3, 5, 1, 7):
        rows_d = pl.ds(al(lax.rem(c + d, NC) * 16, 16), 16)
        w.send("mix", mixs.at[rows_d], mixr.at[d], me.ctx_peer(d))
    regroup_relay("q", qs.at[0], stage.at[0])
    regroup("g", g, gs, stage.at[2])
    regroup_relay("k", ks, stage.at[1])

    w.need("mix")
    mine = pl.ds(al(c * 16, 16), 16)
    total = frames_s[mine, :].astype(F32) + mixs[mine, :].astype(F32)
    for d in range(1, NC):
        total = total + mixr[d].astype(F32)
    enc_s[...] = total.astype(BF16)
    for d in (4, 2, 6, 3, 5, 1, 7):
        w.send("enc", enc_s, enc_o.at[mine], me.ctx_peer(d))
    w.local("enc0", enc_s, enc_o.at[mine])

    w.need("d0")
    d_step(1)
    w.need("q", "q2", "q0")
    w.send("hq", qs.at[0], qs.at[1], me.prv)
    regroup_relay("g", gs, stage.at[2])
    w.need("d1")
    d_step(2)
    w.need("d2")
    d_step(3)
    w.finish()


def positions(t, aud, slot_s, land_s):
    order = (iota((AUD, AUD), 0) < iota((AUD, AUD), 1)).astype(F32).astype(BF16)
    own = aud[pl.ds(t, 1), :]
    target = own // TOK
    hit = (iota((NT, AUD), 0) == target).astype(F32)
    rank = jnp.sum(dot(hit.astype(BF16), order) * hit, axis=0, keepdims=True)
    slot = target * SLOT + rank.astype(jnp.int32)
    slot_s[...] = jnp.broadcast_to(slot, slot_s.shape)
    table = aud[...]
    landing = table // TOK == t
    landing_rank = dot(landing.astype(F32).astype(BF16), order)
    spot = jnp.where(landing, table - t * TOK + 1, 0)
    n = NT * 16
    grow = (iota((n, NT), 0) // 16 == iota((n, NT), 1)).astype(F32).astype(BF16)
    spot_hi = dot(grow, (spot // 16).astype(F32).astype(BF16))
    spot_lo = dot(grow, (spot % 16).astype(F32).astype(BF16))
    ranks = dot(grow, jnp.where(landing, landing_rank, 64.0).astype(BF16))
    place = spot_hi * 16.0 + spot_lo
    r = (iota((n, AUD), 0) % 16).astype(F32)
    eye = iota((n, n), 0) == iota((n, n), 1)
    for half in range(2):
        col = jnp.sum(jnp.where(ranks == r - 8.0 * half, place, 0.0), axis=1, keepdims=True) - 1.0
        line = jnp.sum(jnp.where(eye, col, 0.0), axis=0, keepdims=True)
        land_s[half] = jnp.broadcast_to(line, (8, n)).astype(jnp.int32)


def kernel_b(
    enc_i, ad_i, ks_i, qs_i, gs_i, lown_i, low, aud, text, first_a, first_b,
    hid_o, pb_o, VG, gs_o,
    enc, AD, ks, qs, gs, low_s, lown, text_s, slot_s, land_s, adp, pick, inc, hid,
    e_ref, pb, vg, st_own, st_nxt, st_fp, st_fn,
    ssem, rsem, lsem, aus, aur,
):
    me = Place()
    w = Wires(ssem, rsem, lsem)
    t, c = me.t, me.c
    bar = pltpu.get_barrier_semaphore()

    def greet(d, carry):
        signal_to(bar, (lax.rem(t + d, NT), c))
        return carry

    lax.fori_loop(1, NT, greet, 0)
    for dev in ((t, me.y_up), (t, me.y_dn), me.mate()):
        signal_to(bar, dev)
    w.local("ad", ad_i, AD)
    w.local("enc", enc_i, enc)
    w.local("ks", ks_i, ks)
    w.local("qs", qs_i, qs)
    w.local("gs", gs_i, gs.at[0])
    w.local("lown", lown_i, lown)
    w.local("text", text, text_s)
    low_s[...] = jnp.broadcast_to(low[...], low_s.shape)
    pl.semaphore_wait(bar, NT - 1 + 3)
    w.send("hg", gs_i, gs.at[1], me.prv)

    positions(t, aud, slot_s, land_s)

    my_slot = pl.ds(al(t * 16, 16), 16)

    def audio_copy(d):
        peer = lax.rem(t + d, NT)
        return pltpu.make_async_remote_copy(
            src_ref=pick.at[pl.ds(al(peer * 16, 16), 16)], dst_ref=inc.at[my_slot],
            send_sem=aus.at[d], recv_sem=aur.at[d], device_id=(peer, c), device_id_type=MESH,
        )

    w.need("ad", "enc")
    for n in range(4):
        cols = pl.ds(256 * n, 256)
        adp[:, cols] = dot(enc[...], AD[:, cols]).astype(BF16)
    slot_row = iota((NT * 16, AUD), 0)
    picker = ((slot_row // 16) * SLOT + slot_row % SLOT == slot_s[pl.ds(0, 1), :]).astype(F32)
    picker = picker.astype(BF16)
    low_half = dot(picker, adp[:, pl.ds(0, 512)])
    high_half = dot(picker, adp[:, pl.ds(512, 512)])
    upper = iota((NT * 16, 512), 0) % 16 < SLOT
    pick[...] = jnp.where(upper, low_half, high_half).astype(BF16)

    def audio_start(d, carry):
        audio_copy(d).start()
        return carry

    lax.fori_loop(1, NT, audio_start, 0)
    inc[my_slot, :] = pick[my_slot, :]

    base = t * TOK
    row8 = iota((8, HALF), 0)

    def score_tiles(block, lows, limit, stats):
        def one_head(h, carry):
            hs = head_cols(h)
            for b, i0, j0, jn in TILES:
                if b != block:
                    continue
                qi = pl.ds(i0, HALF)
                s = dot_t(ks[pl.ds(j0, jn), hs], qs[b, qi, hs]) * SCALE
                jj = iota((jn, HALF), 0) + j0
                ok = jj >= lows[pl.ds(0, 1), qi] - base
                if block == 0:
                    ok = ok & (jj <= iota((jn, HALF), 1) + i0)
                else:
                    ok = ok & (jj < limit)
                s = jnp.where(ok, s, MASK_FILL)
                m = jnp.max(s, axis=0, keepdims=True)
                e = jnp.where(ok, jnp.exp(s - m), 0.0)
                n = jnp.sum(e, axis=0, keepdims=True)
                e_ref[b, h, pl.ds(j0, jn), qi] = e
                stats[h, :, qi] = jnp.where(row8 == 0, m, n)
            return carry

        lax.fori_loop(0, HH, one_head, 0)

    w.need("ks", "qs", "lown")
    score_tiles(1, lown, jnp.where(t == NT - 1, 0, TOK), st_nxt)
    w.send("stb", st_nxt, st_fp, me.nxt)
    score_tiles(0, low_s, TOK, st_own)
    w.send("sta", st_own, st_fn, me.prv)

    def factor(mine_st, other_st, h):
        m1, s1 = mine_st[h, pl.ds(0, 1), :], mine_st[h, pl.ds(1, 1), :]
        m2, s2 = other_st[h, pl.ds(0, 1), :], other_st[h, pl.ds(1, 1), :]
        m = jnp.maximum(m1, m2)
        a1 = jnp.exp(m1 - m)
        return a1 / (s1 * a1 + s2 * jnp.exp(m2 - m))

    w.need("sta", "stb", "gs", "hg")
    blank = jnp.zeros((256, 256), BF16)

    def prob_head(h, carry):
        f = (factor(st_own, st_fp, h), factor(st_nxt, st_fn, h))
        tiles = []
        for b, i0, j0, jn in TILES:
            at = (b, h, pl.ds(j0, jn), pl.ds(i0, HALF))
            p = (e_ref[at] * f[b][:, i0 : i0 + HALF]).astype(BF16)
            pb[at] = p
            tiles.append(p)
        pb[0, h, pl.ds(256, 256), pl.ds(0, 256)] = blank
        pb[1, h, pl.ds(0, 256), pl.ds(256, 256)] = blank
        top, bottom = gather_terms(tiles, gs, h)
        hs = head_cols(h)
        vg[pl.ds(0, 256), hs] = top.astype(BF16)
        vg[pl.ds(256, 256), hs] = bottom.astype(BF16)
        return carry

    lax.fori_loop(0, HH, prob_head, 0)
    w.send("vg1", vg, VG.at[c], (t, me.y_up))
    w.send("vg3", vg, VG.at[c], (t, me.y_dn))
    w.send("vgc", vg, VG.at[c], me.mate())
    w.local("vg0", vg, VG.at[c])
    w.local("pb", pb, pb_o)
    w.local("gso", gs, gs_o)

    def audio_arrived(d, carry):
        audio_copy(d).wait_recv()
        return carry

    lax.fori_loop(1, NT, audio_arrived, 0)
    w.need("text")
    for half in range(2):
        cols = pl.ds(512 * half, 512)
        hits = (iota((TOK, NT * 16), 0) == land_s[half, pl.ds(0, 1), :]).astype(F32)
        there = jnp.sum(hits, axis=1, keepdims=True) > 0.5
        rows_in = dot(hits.astype(BF16), inc[...])
        hid[:, cols] = jnp.where(there, rows_in, text_s[:, cols].astype(F32)).astype(BF16)
    w.local("hid", hid, hid_o)

    w.need("vg1", "vg3")
    one, two = VG.at[me.y_dn, pl.ds(0, 256)], VG.at[me.y_up, pl.ds(256, 256)]
    w.send("vg2", one, one, (t, me.y_up))
    w.send("vg2", two, two, (t, me.y_dn))
    w.send("vgc", VG.at[me.y_dn], VG.at[me.y_dn], me.mate())
    w.send("vgc", VG.at[me.y_up], VG.at[me.y_up], me.mate())
    w.need("vg2")
    w.send("vgc", VG.at[me.far], VG.at[me.far], me.mate())

    def audio_sent(d, carry):
        audio_copy(d).wait_send()
        return carry

    lax.fori_loop(1, NT, audio_sent, 0)
    w.finish()


CHUNKS = ((2, 0), (2, 1), (1, 0), (1, 1), (3, 0), (3, 1), (0, 0), (0, 1))
ORDER = (
    "t0", "t1", "rs0", "t2", "rs1", "t3", "rs2", "t4", "rs3", "ad2", "t5", "rs4", "t6", "rs5",
    "ad5", "t7", "rs6", "rs7", "dh0", "dh1", "dh2", "dh3", "dh4", "dh5", "dh6", "dh7", "delta", "key",
)


def kernel_c(
    hid_i, wa, wb, vg_i, pb_i, gs_i, qs_i,
    dk_out, dh_out,
    hid, W, VG, pb, gs, qs, gv_ref, dl_own, dl_nxt, dl_fp, dl_fn,
    psend, pown, precv, rsend, radd, rrecv, vbuf, acc,
    ssem, rsem, lsem, rss, rsr,
):
    me = Place()
    w = Wires(ssem, rsem, lsem)
    t, c, core, yy = me.t, me.c, me.core, me.yy
    mate = me.mate()
    bar = pltpu.get_barrier_semaphore()
    near = (me.y_up, me.y_dn, me.beside(me.y_up), me.beside(me.y_dn), me.beside(c))
    for dev in [(t, cc) for cc in near] + [me.nxt, me.prv]:
        signal_to(bar, dev)
    w.local("hid", hid_i, hid)

    def chunk_of(i):
        e, kd = CHUNKS[i]
        return lax.rem(yy + e, NC // 2) * 2 + kd

    for i in range(NC):
        cp = chunk_of(i)
        w.local(f"w{i}", wa.at[pl.ds(cp * HH, HH)], W.at[i, :, pl.ds(0, 512)])
        for j in range(HH):
            w.local(f"w{i}", wb.at[j, cp], W.at[i, j, pl.ds(512, 512)])
    w.local("vg", vg_i, VG)
    w.local("gs", gs_i, gs)
    w.local("pb", pb_i, pb)
    w.local("qs", qs_i, qs)
    pl.semaphore_wait(bar, len(near) + 2)

    mate_rows = pl.ds(al((1 - core) * HALF, HALF), HALF)
    my_rows = pl.ds(al(core * HALF, HALF), HALF)

    def terms(i):
        w.need("hid", f"w{i}")
        wide = jnp.concatenate([W[i, j] for j in range(HH)], axis=1)
        psend[i] = dot(hid[mate_rows, :], wide).astype(BF16)
        w.send(f"pair{i}", psend.at[i], precv.at[i], mate)
        wide = jnp.concatenate([W[i, j] for j in range(HH)], axis=1)
        pown[i] = dot(hid[my_rows, :], wide).astype(BF16)

    def owner_copy(i):
        e, kd = CHUNKS[i]
        side = e // 2
        return pltpu.make_async_remote_copy(
            src_ref=rsend.at[i], dst_ref=rrecv.at[1 + side, my_rows],
            send_sem=rss.at[2 * side + kd], recv_sem=rsr.at[2 * side + core],
            device_id=(t, chunk_of(i)), device_id_type=MESH,
        )

    def mate_copy(i):
        return pltpu.make_async_remote_copy(
            src_ref=rsend.at[i], dst_ref=rrecv.at[0, my_rows],
            send_sem=rss.at[4], recv_sem=rsr.at[4], device_id=mate, device_id_type=MESH,
        )

    def chip_sum(i):
        e, kd = CHUNKS[i]
        w.need(f"pair{i}")
        total = pown[i].astype(F32) + precv[i].astype(F32)
        rsend[i] = total.astype(BF16)
        if e == 2:
            w.send(f"add{kd}", rsend.at[i], radd.at[kd], (t, me.y_dn if kd else me.y_up))
        elif (e, kd) in ((1, 1), (3, 0)):
            owner_copy(i).start()
        elif e == 0:
            @pl.when(kd != core)
            def _():
                mate_copy(i).start()

            @pl.when(kd == core)
            def _():
                rrecv[0, my_rows, :] = rsend[i]

    def added_sum(i):
        kd = CHUNKS[i][1]
        w.need(f"add{kd}")
        total = rsend[i].astype(F32) + radd[kd].astype(F32)
        rsend[i] = total.astype(BF16)
        owner_copy(i).start()

    added = []

    def hidden_grad(i):
        w.need("vg", f"w{i}")
        cp = chunk_of(i)
        added.append(i)
        first, last = len(added) == 1, len(added) == NC

        def part(n, carry):
            rows_n = pl.ds(al(n * 256, 256), 256)
            wide = jnp.concatenate([W[i, j, rows_n, :] for j in range(HH)], axis=1)
            term = dot_t(VG[cp], wide)
            if not first:
                term = term + acc[n]
            if last:
                dh_out[:, rows_n] = term.astype(BF16)
            else:
                acc[n] = term
            return carry

        lax.fori_loop(0, COLS // 256, part, 0)

    row8 = iota((8, HALF), 0)

    def delta():
        for n in range(5):
            pltpu.make_async_remote_copy(
                src_ref=rsend.at[0], dst_ref=rrecv.at[0, my_rows], send_sem=rss.at[n],
                recv_sem=rsr.at[n], device_id=mate, device_id_type=MESH,
            ).wait_recv()
        total = rrecv[0].astype(F32) + rrecv[1].astype(F32) + rrecv[2].astype(F32)
        vbuf[...] = total.astype(BF16)
        w.need("gs", "pb")

        def delta_head(h, carry):
            hs = head_cols(h)
            for b, i0, j0, jn in TILES:
                qi = pl.ds(i0, HALF)
                gv = dot_t(vbuf[pl.ds(j0, jn), hs], gs[b, qi, hs])
                gv_ref[b, h, pl.ds(j0, jn), qi] = gv
                p = pb[b, h, pl.ds(j0, jn), qi].astype(F32)
                part = jnp.sum(p * gv, axis=0, keepdims=True)
                table = dl_own if b == 0 else dl_nxt
                table[h, :, qi] = jnp.where(row8 == 0, part, 0.0)
            return carry

        lax.fori_loop(0, HH, delta_head, 0)
        w.send("dl", dl_own, dl_fn, me.prv)
        w.send("dl", dl_nxt, dl_fp, me.nxt)

    def key():
        w.need("dl", "qs")

        def key_head(h, carry):
            deltas = (
                dl_own[h, pl.ds(0, 1), :] + dl_fp[h, pl.ds(0, 1), :],
                dl_nxt[h, pl.ds(0, 1), :] + dl_fn[h, pl.ds(0, 1), :],
            )
            tiles = []
            for b, i0, j0, jn in TILES:
                qi = pl.ds(i0, HALF)
                p = pb[b, h, pl.ds(j0, jn), qi].astype(F32)
                gv = gv_ref[b, h, pl.ds(j0, jn), qi]
                tiles.append((p * (gv - deltas[b][:, i0 : i0 + HALF])).astype(BF16))
            top, bottom = gather_terms(tiles, qs, h)
            hs = head_cols(h)
            dk_out[pl.ds(0, 256), hs] = (top * SCALE).astype(BF16)
            dk_out[pl.ds(256, 256), hs] = (bottom * SCALE).astype(BF16)
            return carry

        lax.fori_loop(0, HH, key_head, 0)

    steps = {"delta": delta, "key": key}
    for i in range(NC):
        steps[f"t{i}"] = lambda i=i: terms(i)
        steps[f"rs{i}"] = lambda i=i: chip_sum(i)
        steps[f"ad{i}"] = lambda i=i: added_sum(i)
        steps[f"dh{i}"] = lambda i=i: hidden_grad(i)
    for name in ORDER:
        steps[name]()
    for n in range(5):
        pltpu.make_async_remote_copy(
            src_ref=rsend.at[0], dst_ref=rrecv.at[0, my_rows], send_sem=rss.at[n],
            recv_sem=rsr.at[n], device_id=mate, device_id_type=MESH,
        ).wait_send()
    w.finish()


def call(kernel, n, out_shape, in_specs, out_specs, scratch, flops, moved):
    return pl.pallas_call(
        kernel,
        out_shape=out_shape,
        in_specs=in_specs,
        out_specs=out_specs,
        scratch_shapes=scratch,
        compiler_params=pltpu.CompilerParams(
            collective_id=n, has_side_effects=True, vmem_limit_bytes=60 * 1024 * 1024
        ),
        cost_estimate=pl.CostEstimate(flops=flops, bytes_accessed=moved, transcendentals=0),
    )


def body(
    frames, value_weight, gate_weight, conv_taps, out_weight, adapter, audio_pos, text_rows,
    value_proj, queries, keys, grad_out, window_low,
):
    along_x = [[NX * zz + xx for xx in range(NX)] for zz in range(NZ)]
    along_z = [[NX * zz + xx for zz in range(NZ)] for xx in range(NX)]
    first_a = lax.all_gather(value_proj[:512], "tm", axis_index_groups=along_x)
    first_b = lax.all_gather(value_proj[512:], "tm", axis_index_groups=along_z)
    low = window_low.reshape(1, TOK)
    vm = pl.BlockSpec(memory_space=pltpu.VMEM)
    hbm = pl.BlockSpec(memory_space=pl.ANY)
    vmem = pltpu.VMEM
    dma = pltpu.SemaphoreType.DMA
    shape = jax.ShapeDtypeStruct
    enc, ad, ks, qs, gs, lown = call(
        kernel_a, 0,
        (
            shape((AUD, DE), BF16), shape((DE, COLS), BF16), shape((TOK, HC), BF16),
            shape((2, TOK, HC), BF16), shape((TOK, HC), BF16), shape((8, TOK), jnp.int32),
        ),
        [hbm] * 5 + [vm] + [hbm] * 4, (hbm,) * 6,
        [
            vmem((AUD, DE), BF16),
            vmem((DE, DH), BF16),
            vmem((DE, DH), BF16),
            vmem(conv_taps.shape, F32),
            vmem((DH, DE), BF16),
            vmem((8, TOK), jnp.int32),
            vmem((AUD + 32, DE), BF16),
            vmem((AUD + 32, DH), F32),
            vmem((AUD, DE), BF16),
            vmem((NC, 16, DE), BF16),
            vmem((16, DE), BF16),
            vmem((3, 2, 64, HC), BF16),
            dma((64,)), dma((64,)), dma((16,)),
        ],
        200_000_000, 20_000_000,
    )(
        frames, value_weight, gate_weight, conv_taps, out_weight, low, adapter,
        queries, keys, grad_out,
    )
    enc, first_a, first_b = lax.optimization_barrier((enc, first_a, first_b))
    weights_a = lax.all_gather(first_a, "tm", axis_index_groups=along_z).reshape(NT, 512, DH)
    weights_b = lax.all_gather(first_b, "tm", axis_index_groups=along_x)
    hid, pb, vg, gs2 = call(
        kernel_b, 1,
        (
            shape((TOK, COLS), BF16), shape((2, HH, TOK, TOK), BF16),
            shape((NC, TOK, HC), BF16), shape((2, TOK, HC), BF16),
        ),
        [hbm] * 6 + [vm] * 2 + [hbm] * 3, (hbm,) * 4,
        [
            vmem((AUD, DE), BF16),
            vmem((DE, COLS), BF16),
            vmem((TOK, HC), BF16),
            vmem((2, TOK, HC), BF16),
            vmem((2, TOK, HC), BF16),
            vmem((8, TOK), jnp.int32),
            vmem((8, TOK), jnp.int32),
            vmem((TOK, COLS), BF16),
            vmem((8, AUD), jnp.int32),
            vmem((2, 8, NT * 16), jnp.int32),
            vmem((AUD, COLS), BF16),
            vmem((NT * 16, 512), BF16),
            vmem((NT * 16, 512), BF16),
            vmem((TOK, COLS), BF16),
            vmem((2, HH, TOK, TOK), F32),
            vmem((2, HH, TOK, TOK), BF16),
            vmem((TOK, HC), BF16),
        ]
        + [vmem((HH, 8, TOK), F32)] * 4
        + [dma((16,)), dma((16,)), dma((16,)), dma((NT,)), dma((NT,))],
        3_000_000_000, 60_000_000,
    )(
        enc, ad, ks, qs, gs, lown, low, audio_pos.reshape(NT, AUD), text_rows, first_a, first_b,
    )
    return call(
        kernel_c, 2,
        (shape((TOK, HC), BF16), shape((TOK, COLS), BF16)),
        [hbm] * 7, (vm, vm),
        [
            vmem((TOK, COLS), BF16),
            vmem((NC, HH, COLS, DH), BF16),
            vmem((NC, TOK, HC), BF16),
            vmem((2, HH, TOK, TOK), BF16),
            vmem((2, TOK, HC), BF16),
            vmem((2, TOK, HC), BF16),
            vmem((2, HH, TOK, TOK), F32),
        ]
        + [vmem((HH, 8, TOK), F32)] * 4
        + [
            vmem((NC, HALF, HC), BF16),
            vmem((NC, HALF, HC), BF16),
            vmem((NC, HALF, HC), BF16),
            vmem((NC, HALF, HC), BF16),
            vmem((2, HALF, HC), BF16),
            vmem((3, TOK, HC), BF16),
            vmem((TOK, HC), BF16),
            vmem((COLS // 256, TOK, 256), F32),
            dma((16,)), dma((16,)), dma((64,)), dma((8,)), dma((8,)),
        ],
        10_000_000_000, 30_000_000,
    )(hid, weights_a, weights_b, vg, pb, gs2, qs)


def solution(mesh):
    return jax.shard_map(
        body,
        mesh=mesh,
        in_specs=(
            P("tm", None),
            P(None, "ctx"),
            P(None, "ctx"),
            P(None, "ctx"),
            P("ctx", None),
            P("tm", "ctx"),
            P(),
            P("tm", "ctx"),
            P("ctx", "tm"),
            P(("tm", "ctx"), None),
            P(("tm", "ctx"), None),
            P(("tm", "ctx"), None),
            P("tm"),
        ),
        out_specs=(P("tm", "ctx"), P("tm", "ctx")),
        check_vma=False,
    )
```

```python
import math

import jax
import jax.numpy as jnp
from jax import lax
from jax.experimental import pallas as pl
from jax.experimental.pallas import tpu as pltpu
from jax.sharding import PartitionSpec as P

DH = 128
NORM_EPS = 1e-05
MASK_FILL = -1e30
MESH = pl.DeviceIdType.MESH
F32 = jnp.float32
BF16 = jnp.bfloat16

NT = 32
NC = 8
NX = 4
NZ = 8
TOK = 512
AUD = 128
DE = 1024
COLS = 1024
HC = 512
HH = HC // DH
HALF = TOK // 2
SLOT = 8
TILES = ((0, 0, 0, 256), (0, 256, 0, 512), (1, 0, 0, 512), (1, 256, 256, 256))
N_SEMS = 160
QUART = COLS // NX
ROWS_A = 576
ROWS_B = COLS - ROWS_A
OFFSETS = (0, -1, 1, -2, 2, -3, 3, 4)
ORDER = (
    "issue", "i_b0", "i_q", "mm", "i_ax", "LN", "b_s1", "m0", "fq", "conv", "i_g", "d_s0", "p0",
    "b_s2", "rm", "hq", "d_s1", "a_s0", "p1", "enc", "b_s3", "fg", "r0", "encx", "hg", "i_k",
    "pos", "d_s2", "a_s1", "fk", "p3", "r1", "er", "sc1", "sc0", "m2", "d_s3", "p2", "i_bm",
    "m1", "a_s2", "m3", "adapt", "r2", "prob", "r3", "vgr", "place", "t3", "t0", "t2", "a_s3",
    "rs3", "t4", "rs0", "t5", "ad3", "rs2", "rs4", "t6", "ad0", "t1", "rs5", "ad2", "t7", "ad4",
    "rs6", "vgf", "rs7", "ad6", "dh0", "dh2", "dh3", "dh7", "ad5", "rs1", "dh1", "ad7", "dh5",
    "dh6", "ad1", "delta", "dh4", "key",
)


def dot(a, b):
    return jnp.dot(a, b, preferred_element_type=F32)


def dot_t(a, b):
    return lax.dot_general(a, b, (((1,), (1,)), ((), ())), preferred_element_type=F32)


def iota(shape, dim):
    return lax.broadcasted_iota(jnp.int32, shape, dim)


def kernel(
    frames, vw, gw, taps, ow, text, low, aud, adapter, vp, q, k, g,
    dk_out, dh_out,
    W, AD, qs, gs, ks, low_s, lown, frames_s, vw_s, gw_s, taps_s, ow_s, text_s,
    slot_s, land_s, ext, glu_s, mixs, mixr, enc, adp, pick, inc, hid,
    e_ref, gv_ref, st_own, st_nxt, st_fp, st_fn, dl_own, dl_nxt, dl_fp, dl_fn,
    VG, psend, pown, precv, rsend, radd, rrecv, vbuf, acc, stage,
    ssem, rsem, lsem, aus, aur, rss, rsr,
):
    t = lax.axis_index("tm")
    c = lax.axis_index("ctx")
    x = lax.rem(t, NX)
    z = lax.div(t, NX)
    core = lax.rem(c, 2)
    yy = lax.div(c, 2)
    up = (lax.rem(z + 1, NZ) * NX + x, c)
    dn = (lax.rem(z + NZ - 1, NZ) * NX + x, c)
    nxt = (lax.rem(t + 1, NT), c)
    prv = (lax.rem(t + NT - 1, NT), c)
    mate = (t, c + 1 - 2 * core)

    def ctx_peer(d):
        return (t, lax.rem(c + d, NC))

    def x_peer(d):
        return (z * NX + lax.rem(x + d, NX), c)

    def zat(d):
        return lax.rem(z + d + NZ, NZ)

    def al(v, m):
        return pl.multiple_of(v, m)

    sends = []
    groups = {}
    waited = set()

    def send(name, src, dst, dev):
        i = len(sends)
        copy = pltpu.make_async_remote_copy(
            src_ref=src, dst_ref=dst, send_sem=ssem.at[i], recv_sem=rsem.at[i],
            device_id=dev, device_id_type=MESH,
        )
        copy.start()
        sends.append(copy)
        groups.setdefault(name, []).append(copy)

    def need(*names):
        for name in names:
            if name not in waited:
                waited.add(name)
                for copy in groups[name]:
                    if name in here:
                        copy.wait()
                    else:
                        copy.wait_recv()

    here = set()

    def local(name, src, dst):
        copy = pltpu.make_async_copy(src, dst, lsem.at[len(here)])
        copy.start()
        here.add(name)
        groups[name] = [copy]

    own_rows = pl.ds(al(c * 64, 64), 64)
    own_cols = pl.ds(al(c * HC, HC), HC)
    ad_rows = pl.ds(al(t * 32, 32), 32)
    rows_a = pl.ds(0, ROWS_A)
    rows_b = pl.ds(ROWS_A, ROWS_B)

    def issue():
        bar = pltpu.get_barrier_semaphore()

        def greet(d, carry):
            pl.semaphore_signal(bar, inc=1, device_id=(lax.rem(t + d, NT), c), device_id_type=MESH)
            return carry

        lax.fori_loop(1, NT, greet, 0)
        for d in range(1, NC):
            pl.semaphore_signal(bar, inc=1, device_id=ctx_peer(d), device_id_type=MESH)
        local("frames", frames, frames_s)
        local("vw", vw, vw_s)
        local("gw", gw, gw_s)
        local("vp", vp, W.at[t])
        local("ad", adapter.at[:, pl.ds(al(x * QUART, QUART), QUART)], AD.at[ad_rows])
        local("taps", taps, taps_s)
        local("ow", ow, ow_s)
        local("k0", k.at[:, own_cols], ks.at[own_rows])
        local("q0", q.at[:, own_cols], qs.at[0, own_rows])
        local("g0", g.at[:, own_cols], gs.at[0, own_rows])
        local("text", text, text_s)
        low_s[...] = jnp.broadcast_to(low[...], low_s.shape)
        pl.semaphore_wait(bar, NT - 1 + NC - 1)
        send("fh", frames.at[pl.ds(AUD - 16, 16)], ext.at[pl.ds(0, 16)], nxt)
        send("fh", frames.at[pl.ds(0, 16)], ext.at[pl.ds(AUD + 16, 16)], prv)
        for d in (1, 3, 2):
            quarter = pl.ds(al(lax.rem(x + d, NX) * QUART, QUART), QUART)
            send("adx", adapter.at[:, quarter], AD.at[ad_rows], x_peer(d))
        send("low", low_s, lown, prv)

    def b_ref(zz, xx=x):
        return W.at[zz * NX + xx, rows_b]

    def b_part(zz, p):
        return W.at[zz * NX + x, pl.ds(ROWS_A + ROWS_B // 2 * p, ROWS_B // 2)]

    def a_ref(zz):
        return W.at[pl.ds(zz * NX, NX), rows_a]

    def a_part(zz, p):
        return W.at[pl.ds(zz * NX + 2 * p, 2), rows_a]

    def d_ref(zz):
        return AD.at[pl.ds(al(zz * 128, 128), 128)]

    def d_part(zz, p):
        return AD.at[pl.ds(al(zz * 128 + 64 * p, 64), 64)]

    def ring(name, s, ref_of, part_of):
        if s < NZ // 2 - 1:
            u, v = ref_of(zat(-s)), ref_of(zat(s))
        else:
            u, v = part_of(zat(-s), 0), part_of(zat(s), 1)
        send(f"{name}{s}", u, u, up)
        send(f"{name}{s}", v, v, dn)

    def a_step(s):
        need(*([f"a{s - 1}"] if s else ["ax", "vp"]))
        ring("a", s, a_ref, a_part)

    def b_step(s):
        need(*([f"b{s - 1}"] if s else ["vp"]))
        ring("b", s, b_ref, b_part)

    def d_step(s):
        need(*([f"d{s - 1}"] if s else ["adx", "ad"]))
        ring("d", s, d_ref, d_part)

    def reached(s):
        return (0,) if s < 0 else ((-1 - s, 1 + s) if s < 3 else (4,))

    def spread(s, d, kind):
        need(f"b{s}" if s >= 0 else "vp")
        for o in reached(s):
            send(f"{kind}{s}", b_ref(zat(o)), b_ref(zat(o)), x_peer(d))

    def relay(s):
        turn = 3 if s in (-1, 3) else 1
        need(f"p{s}" if turn == 1 else f"m{s}")
        origin = lax.rem(x + NX - turn, NX)
        for o in reached(s):
            send(f"r{s}", b_ref(zat(o), origin), b_ref(zat(o), origin), x_peer(turn))

    def issue_ax():
        for d in (1, 3, 2):
            send("ax", vp.at[rows_a], W.at[t, rows_a], x_peer(d))

    def beside(cc):
        return cc + 1 - 2 * core

    def regroup(name, src, dst, stage):
        y_up, y_dn, far = [lax.rem(c + d, NC) for d in (2, 6, 4)]

        def piece(peer):
            return src.at[:, pl.ds(al(peer * HC, HC), HC)]

        send(name + "s", piece(far), stage.at[0], (t, y_up))
        send(name + "s", piece(beside(far)), stage.at[1], (t, y_dn))
        for peer in (y_up, y_dn, beside(y_up), beside(y_dn), beside(c)):
            send(name, piece(peer), dst.at[own_rows], (t, peer))

    def regroup_relay(name, dst, stage):
        need(name + "s")
        y_up, y_dn = [lax.rem(c + d, NC) for d in (2, 6)]
        send(name + "2", stage.at[0], dst.at[pl.ds(al(y_dn * 64, 64), 64)], (t, y_up))
        send(name + "2", stage.at[1], dst.at[pl.ds(al(y_up * 64, 64), 64)], (t, beside(y_dn)))

    def positions():
        order = (iota((AUD, AUD), 0) < iota((AUD, AUD), 1)).astype(F32).astype(BF16)
        for b in range(NX):
            target = aud[pl.ds(z * NX + b, 1), :] // TOK
            hit = (iota((NT, AUD), 0) == target).astype(F32)
            rank = jnp.sum(dot(hit.astype(BF16), order) * hit, axis=0, keepdims=True)
            slot = target * (NX * SLOT) + b * SLOT + rank.astype(jnp.int32)
            slot_s[:, pl.ds(b * AUD, AUD)] = jnp.broadcast_to(slot, (8, AUD))
        table = aud[...]
        landing = table // TOK == t
        landing_rank = dot(landing.astype(F32).astype(BF16), order)
        spot = jnp.where(landing, table - t * TOK + 1, 0)
        n = NT * SLOT
        grow = (iota((n, NT), 0) // SLOT == iota((n, NT), 1)).astype(F32).astype(BF16)
        spot_hi = dot(grow, (spot // 16).astype(F32).astype(BF16))
        spot_lo = dot(grow, (spot % 16).astype(F32).astype(BF16))
        ranks = dot(grow, jnp.where(landing, landing_rank, 64.0).astype(BF16))
        spots = spot_hi * 16.0 + spot_lo
        r = (iota((n, AUD), 0) % SLOT).astype(F32)
        col = jnp.sum(jnp.where(ranks == r, spots, 0.0), axis=1, keepdims=True) - 1.0
        eye = iota((n, n), 0) == iota((n, n), 1)
        line = jnp.sum(jnp.where(eye, col, 0.0), axis=0, keepdims=True)
        land_s[...] = jnp.broadcast_to(line, (8, n)).astype(jnp.int32)

    def norm_glu():
        need("frames", "vw", "gw")
        ext[pl.ds(16, AUD), :] = frames_s[...]
        need("fh")
        rows = ext[...].astype(F32)
        centre = jnp.mean(rows, axis=1, keepdims=True)
        off = rows - centre
        spread_ = jnp.mean(off * off, axis=1, keepdims=True)
        normed = (off * lax.rsqrt(spread_ + NORM_EPS)).astype(BF16)
        value_part = dot(normed, vw_s[...])
        gate_part = dot(normed, gw_s[...])
        glu = (value_part * jax.nn.sigmoid(gate_part)).astype(BF16).astype(F32)
        row = iota(glu.shape, 0)
        first = jnp.where(t == 0, 16, 0)
        last = jnp.where(t == NT - 1, AUD + 16, AUD + 32)
        glu_s[...] = jnp.where((row >= first) & (row < last), glu, 0.0)

    def conv():
        need("taps", "ow")
        smooth = jnp.zeros((AUD, DH), F32)
        for j in range(taps_s.shape[0]):
            smooth = smooth + taps_s[pl.ds(j, 1), :] * glu_s[pl.ds(1 + j, AUD), :]
        action = (smooth * jax.nn.sigmoid(smooth)).astype(BF16)
        mixs[...] = dot(action, ow_s[...]).astype(BF16)
        for d in (4, 2, 6, 3, 5, 1, 7):
            rows_d = pl.ds(al(lax.rem(c + d, NC) * 16, 16), 16)
            send("mix", mixs.at[rows_d], mixr.at[d], ctx_peer(d))

    def encode():
        need("mix")
        mine = pl.ds(al(c * 16, 16), 16)
        total = frames_s[mine, :].astype(F32) + mixs[mine, :].astype(F32)
        for d in range(1, NC):
            total = total + mixr[d].astype(F32)
        enc[x, mine, :] = total.astype(BF16)
        for d in (4, 2, 6, 3, 5, 1, 7):
            send("enc", enc.at[x, mine], enc.at[x, mine], ctx_peer(d))

    def encode_x():
        need("enc")
        for d in (1, 3):
            send("ex", enc.at[x], enc.at[x], x_peer(d))

    def encode_relay():
        need("ex")
        for d, at in ((1, 0), (3, AUD // 2)):
            part = enc.at[lax.rem(x + NX - d, NX), pl.ds(at, AUD // 2)]
            send("ex2", part, part, x_peer(d))

    def halo(name):
        part = qs if name == "q" else gs
        need(name, name + "2", name + "0")
        send("h" + name, part.at[0], part.at[1], prv)

    scale = 1.0 / math.sqrt(DH)
    base = t * TOK
    row8 = iota((8, HALF), 0)

    def head_cols(h):
        return pl.ds(al(h * DH, DH), DH)

    def score_tiles(block, lows, limit, stats):
        def one_head(h, carry):
            hs = head_cols(h)
            for b, i0, j0, jn in TILES:
                if b != block:
                    continue
                qi = pl.ds(i0, HALF)
                s = dot_t(ks[pl.ds(j0, jn), hs], qs[b, qi, hs]) * scale
                jj = iota((jn, HALF), 0) + j0
                ok = jj >= lows[pl.ds(0, 1), qi] - base
                if block == 0:
                    ok = ok & (jj <= iota((jn, HALF), 1) + i0)
                else:
                    ok = ok & (jj < limit)
                s = jnp.where(ok, s, MASK_FILL)
                m = jnp.max(s, axis=0, keepdims=True)
                e = jnp.where(ok, jnp.exp(s - m), 0.0)
                n = jnp.sum(e, axis=0, keepdims=True)
                e_ref[b, h, pl.ds(j0, jn), qi] = e
                stats[h, :, qi] = jnp.where(row8 == 0, m, n)
            return carry

        lax.fori_loop(0, HH, one_head, 0)

    def score_own():
        need("k", "k2", "k0", "q", "q2", "q0")
        score_tiles(0, low_s, TOK, st_own)
        send("sta", st_own, st_fn, prv)

    def score_next():
        need("k", "k2", "k0", "hq", "low")
        score_tiles(1, lown, jnp.where(t == NT - 1, 0, TOK), st_nxt)
        send("stb", st_nxt, st_fp, nxt)

    group_rows = NX * SLOT
    my_slot = pl.ds(al(z * group_rows, group_rows), group_rows)

    def slot_rows(tm):
        return pl.ds(al(tm * group_rows, group_rows), group_rows)

    def audio_copy(d):
        peer = lax.rem(t + d, NT)
        return pltpu.make_async_remote_copy(
            src_ref=pick.at[slot_rows(peer)], dst_ref=inc.at[x, my_slot],
            send_sem=aus.at[d], recv_sem=aur.at[d], device_id=(peer, c), device_id_type=MESH,
        )

    def adapt():
        need("d3", "ex", "ex2")
        adp[...] = dot(enc[...].reshape(NX * AUD, DE), AD[...]).astype(BF16)
        for n in range(4):
            slot_row = iota((256, NX * AUD), 0) + 256 * n
            picker = (slot_row == slot_s[pl.ds(0, 1), :]).astype(F32).astype(BF16)
            pick[pl.ds(256 * n, 256), :] = dot(picker, adp[...]).astype(BF16)

        def audio_start(d, carry):
            audio_copy(d).start()
            return carry

        lax.fori_loop(1, NT, audio_start, 0)
        inc[x, my_slot, :] = pick[slot_rows(t), :]

    def factor(mine_st, other_st, h):
        m1, s1 = mine_st[h, pl.ds(0, 1), :], mine_st[h, pl.ds(1, 1), :]
        m2, s2 = other_st[h, pl.ds(0, 1), :], other_st[h, pl.ds(1, 1), :]
        m = jnp.maximum(m1, m2)
        a1 = jnp.exp(m1 - m)
        return a1 / (s1 * a1 + s2 * jnp.exp(m2 - m))

    def gather_terms(tiles, other, h):
        hs = head_cols(h)
        first, second = pl.ds(0, 256), pl.ds(256, 256)
        top = dot(tiles[0], other[0, first, hs]) + dot(tiles[1][:256], other[0, second, hs])
        top = top + dot(tiles[2][:256], other[1, first, hs])
        bottom = dot(tiles[1][256:], other[0, second, hs])
        bottom = bottom + dot(tiles[2][256:], other[1, first, hs])
        bottom = bottom + dot(tiles[3], other[1, second, hs])
        return top, bottom

    def prob():
        need("sta", "stb", "g", "g2", "g0", "hg")

        def prob_head(h, carry):
            f = (factor(st_own, st_fp, h), factor(st_nxt, st_fn, h))
            tiles = []
            for b, i0, j0, jn in TILES:
                p = e_ref[b, h, pl.ds(j0, jn), pl.ds(i0, HALF)] * f[b][:, i0 : i0 + HALF]
                e_ref[b, h, pl.ds(j0, jn), pl.ds(i0, HALF)] = p
                tiles.append(p.astype(BF16))
            top, bottom = gather_terms(tiles, gs, h)
            hs = head_cols(h)
            VG[c, pl.ds(0, 256), hs] = top.astype(BF16)
            VG[c, pl.ds(256, 256), hs] = bottom.astype(BF16)
            return carry

        lax.fori_loop(0, HH, prob_head, 0)
        send("vg1", VG.at[c], VG.at[c], ctx_peer(2))
        send("vg3", VG.at[c], VG.at[c], ctx_peer(6))
        send("vgc", VG.at[c], VG.at[c], mate)

    below, above, across = [lax.rem(c + d, NC) for d in (6, 2, 4)]

    def vg_relay():
        need("vg1", "vg3")
        one, two = VG.at[below, pl.ds(0, 256)], VG.at[above, pl.ds(256, 256)]
        send("vg2", one, one, ctx_peer(2))
        send("vg2", two, two, ctx_peer(6))
        send("vgc", VG.at[below], VG.at[below], mate)
        send("vgc", VG.at[above], VG.at[above], mate)

    def vg_last():
        need("vg2")
        send("vgc", VG.at[across], VG.at[across], mate)

    def place():
        need("text")

        def audio_arrived(d, carry):
            audio_copy(d).wait_recv()
            return carry

        lax.fori_loop(1, NT, audio_arrived, 0)
        hits = (iota((TOK, NT * SLOT), 0) == land_s[pl.ds(0, 1), :]).astype(F32)
        there = jnp.sum(hits, axis=1, keepdims=True) > 0.5
        hits = hits.astype(BF16)
        for n in range(NX):
            cols = pl.ds(QUART * n, QUART)
            rows_in = dot(hits, inc[n])
            hid[:, cols] = jnp.where(there, rows_in, text_s[:, cols].astype(F32)).astype(BF16)

    mate_rows = pl.ds(al((1 - core) * HALF, HALF), HALF)
    my_rows = pl.ds(al(core * HALF, HALF), HALF)

    def weights_ready(i):
        s = (i - 1) // 2
        need(f"m{s}", f"p{s}", f"r{s}")
        need(*([f"a{s}", f"b{s}"] if i else ["ax", "vp"]))

    def terms(i):
        weights_ready(i)
        cp = zat(OFFSETS[i])
        w = jnp.concatenate([W[cp * HH + j] for j in range(HH)], axis=1)
        psend[i] = dot(hid[mate_rows, :], w).astype(BF16)
        send(f"pair{i}", psend.at[i], precv.at[i], mate)
        w = jnp.concatenate([W[cp * HH + j] for j in range(HH)], axis=1)
        pown[i] = dot(hid[my_rows, :], w).astype(BF16)

    def owner_copy(side, kd, i):
        owner = lax.rem(yy + 1 + 2 * side, NC // 2) * 2 + kd
        return pltpu.make_async_remote_copy(
            src_ref=rsend.at[i], dst_ref=rrecv.at[1 + side, my_rows],
            send_sem=rss.at[2 * side + kd], recv_sem=rsr.at[2 * side + core],
            device_id=(t, owner), device_id_type=MESH,
        )

    def add_copy(kd, i):
        return pltpu.make_async_remote_copy(
            src_ref=rsend.at[i], dst_ref=radd.at[kd],
            send_sem=rss.at[4 + kd], recv_sem=rsr.at[4 + kd],
            device_id=(t, lax.rem(c + 2 + 4 * core, NC)), device_id_type=MESH,
        )

    def mate_copy(i):
        return pltpu.make_async_remote_copy(
            src_ref=rsend.at[i], dst_ref=rrecv.at[0, my_rows],
            send_sem=rss.at[6], recv_sem=rsr.at[6], device_id=mate, device_id_type=MESH,
        )

    def owner_of(i):
        cp = zat(OFFSETS[i])
        return lax.rem(lax.div(cp, 2) - yy + NC // 2, NC // 2), lax.rem(cp, 2)

    def chip_sum(i):
        e, kd = owner_of(i)
        need(f"pair{i}")
        total = pown[i].astype(F32) + precv[i].astype(F32)
        rsend[i] = total.astype(BF16)

        @pl.when(e == 2)
        def _():
            add_copy(kd, i).start()

        @pl.when(e == 3 - 2 * core)
        def _():
            owner_copy(lax.div(e, 2), kd, i).start()

        @pl.when((e == 0) & (kd != core))
        def _():
            mate_copy(i).start()

        @pl.when((e == 0) & (kd == core))
        def _():
            rrecv[0, my_rows, :] = rsend[i]

    def added_sum(i):
        e, kd = owner_of(i)

        @pl.when(e == 1 + 2 * core)
        def _():
            add_copy(kd, i).wait_recv()
            total = rsend[i].astype(F32) + radd[kd].astype(F32)
            rsend[i] = total.astype(BF16)
            owner_copy(lax.div(e, 2), kd, i).start()

    added = []

    def hidden_grad(i):
        weights_ready(i)
        need("vgc")
        cp = zat(OFFSETS[i])
        added.append(i)
        first, last = len(added) == 1, len(added) == NC

        def part(n, carry):
            rows_n = pl.ds(al(n * 256, 256), 256)
            w = jnp.concatenate([W[cp * HH + j, rows_n, :] for j in range(HH)], axis=1)
            term = dot_t(VG[cp], w)
            if not first:
                term = term + acc[n]
            if last:
                dh_out[:, rows_n] = term.astype(BF16)
            else:
                acc[n] = term
            return carry

        lax.fori_loop(0, COLS // 256, part, 0)

    def delta():
        for n in (0, 1, 2, 3, 6):
            pltpu.make_async_remote_copy(
                src_ref=rsend.at[0], dst_ref=rrecv.at[0, my_rows], send_sem=rss.at[n],
                recv_sem=rsr.at[n], device_id=mate, device_id_type=MESH,
            ).wait_recv()
        total = rrecv[0].astype(F32) + rrecv[1].astype(F32) + rrecv[2].astype(F32)
        vbuf[...] = total.astype(BF16)

        def delta_head(h, carry):
            hs = head_cols(h)
            for b, i0, j0, jn in TILES:
                qi = pl.ds(i0, HALF)
                gv = dot_t(vbuf[pl.ds(j0, jn), hs], gs[b, qi, hs])
                gv_ref[b, h, pl.ds(j0, jn), qi] = gv
                w = e_ref[b, h, pl.ds(j0, jn), qi].astype(BF16).astype(F32)
                part = jnp.sum(w * gv, axis=0, keepdims=True)
                table = dl_own if b == 0 else dl_nxt
                table[h, :, qi] = jnp.where(row8 == 0, part, 0.0)
            return carry

        lax.fori_loop(0, HH, delta_head, 0)
        send("dl", dl_own, dl_fn, prv)
        send("dl", dl_nxt, dl_fp, nxt)

    def key():
        need("dl")

        def key_head(h, carry):
            deltas = (
                dl_own[h, pl.ds(0, 1), :] + dl_fp[h, pl.ds(0, 1), :],
                dl_nxt[h, pl.ds(0, 1), :] + dl_fn[h, pl.ds(0, 1), :],
            )
            tiles = []
            for b, i0, j0, jn in TILES:
                qi = pl.ds(i0, HALF)
                p = e_ref[b, h, pl.ds(j0, jn), qi]
                gv = gv_ref[b, h, pl.ds(j0, jn), qi]
                tiles.append((p * (gv - deltas[b][:, i0 : i0 + HALF])).astype(BF16))
            top, bottom = gather_terms(tiles, qs, h)
            hs = head_cols(h)
            dk_out[pl.ds(0, 256), hs] = (top * scale).astype(BF16)
            dk_out[pl.ds(256, 256), hs] = (bottom * scale).astype(BF16)
            return carry

        lax.fori_loop(0, HH, key_head, 0)

    steps = {
        "issue": issue, "i_ax": issue_ax,
        "i_b0": lambda: b_step(0), "i_bm": lambda: spread(-1, 1, "p"), "mm": lambda: spread(-1, 3, "m"),
        "i_k": lambda: regroup("k", k, ks, stage.at[0]),
        "i_q": lambda: regroup("q", q, qs.at[0], stage.at[1]),
        "i_g": lambda: regroup("g", g, gs.at[0], stage.at[2]),
        "fk": lambda: regroup_relay("k", ks, stage.at[0]),
        "fq": lambda: regroup_relay("q", qs.at[0], stage.at[1]),
        "fg": lambda: regroup_relay("g", gs.at[0], stage.at[2]),
        "pos": positions, "LN": norm_glu, "conv": conv, "enc": encode, "encx": encode_x, "er": encode_relay, "adapt": adapt, "place": place,
        "hq": lambda: halo("q"), "hg": lambda: halo("g"),
        "sc0": score_own, "sc1": score_next, "prob": prob, "vgr": vg_relay, "vgf": vg_last,
        "rm": lambda: relay(-1), "delta": delta, "key": key,
    }
    for s in range(4):
        steps[f"a_s{s}"] = lambda s=s: a_step(s)
        steps[f"b_s{s}"] = lambda s=s: b_step(s)
        steps[f"d_s{s}"] = lambda s=s: d_step(s)
        steps[f"p{s}"] = lambda s=s: spread(s, 1, "p")
        steps[f"m{s}"] = lambda s=s: spread(s, 3, "m")
        steps[f"r{s}"] = lambda s=s: relay(s)
    for i in range(NC):
        steps[f"t{i}"] = lambda i=i: terms(i)
        steps[f"rs{i}"] = lambda i=i: chip_sum(i)
        steps[f"ad{i}"] = lambda i=i: added_sum(i)
        steps[f"dh{i}"] = lambda i=i: hidden_grad(i)
    for name in ORDER:
        steps[name]()

    def audio_sent(d, carry):
        audio_copy(d).wait_send()
        return carry

    lax.fori_loop(1, NT, audio_sent, 0)
    for n in range(7):
        pltpu.make_async_remote_copy(
            src_ref=rsend.at[0], dst_ref=rrecv.at[0, my_rows], send_sem=rss.at[n],
            recv_sem=rsr.at[n], device_id=mate, device_id_type=MESH,
        ).wait_send()
    for name in groups:
        need(name)
    for copy in sends:
        copy.wait_send()


def body(
    frames, value_weight, gate_weight, conv_taps, out_weight, adapter, audio_pos, text_rows,
    value_proj, queries, keys, grad_out, window_low,
):
    vm = pl.BlockSpec(memory_space=pltpu.VMEM)
    hbm = pl.BlockSpec(memory_space=pl.ANY)
    vmem = pltpu.VMEM
    dma = pltpu.SemaphoreType.DMA
    return pl.pallas_call(
        kernel,
        out_shape=(
            jax.ShapeDtypeStruct((TOK, HC), BF16),
            jax.ShapeDtypeStruct((TOK, COLS), BF16),
        ),
        in_specs=[hbm] * 6 + [vm] * 2 + [hbm] * 5,
        out_specs=(vm, vm),
        scratch_shapes=[
            vmem((NT, COLS, DH), BF16),
            vmem((DE, QUART), BF16),
            vmem((2, TOK, HC), BF16),
            vmem((2, TOK, HC), BF16),
            vmem((TOK, HC), BF16),
            vmem((8, TOK), jnp.int32),
            vmem((8, TOK), jnp.int32),
            vmem((AUD, DE), BF16),
            vmem((DE, DH), BF16),
            vmem((DE, DH), BF16),
            vmem(conv_taps.shape, F32),
            vmem((DH, DE), BF16),
            vmem((TOK, COLS), BF16),
            vmem((8, NX * AUD), jnp.int32),
            vmem((8, NT * SLOT), jnp.int32),
            vmem((AUD + 32, DE), BF16),
            vmem((AUD + 32, DH), F32),
            vmem((AUD, DE), BF16),
            vmem((NC, 16, DE), BF16),
            vmem((NX, AUD, DE), BF16),
            vmem((NX * AUD, QUART), BF16),
            vmem((NT * NX * SLOT, QUART), BF16),
            vmem((NX, NT * SLOT, QUART), BF16),
            vmem((TOK, COLS), BF16),
            vmem((2, HH, TOK, TOK), F32),
            vmem((2, HH, TOK, TOK), F32),
        ]
        + [vmem((HH, 8, TOK), F32)] * 8
        + [
            vmem((NC, TOK, HC), BF16),
            vmem((NC, HALF, HC), BF16),
            vmem((NC, HALF, HC), BF16),
            vmem((NC, HALF, HC), BF16),
            vmem((NC, HALF, HC), BF16),
            vmem((2, HALF, HC), BF16),
            vmem((3, TOK, HC), BF16),
            vmem((TOK, HC), BF16),
            vmem((COLS // 256, TOK, 256), F32),
            vmem((3, 2, 64, HC), BF16),
            dma((N_SEMS,)),
            dma((N_SEMS,)),
            dma((16,)),
            dma((NT,)),
            dma((NT,)),
            dma((NC,)),
            dma((NC,)),
        ],
        compiler_params=pltpu.CompilerParams(
            collective_id=0, has_side_effects=True, vmem_limit_bytes=60 * 1024 * 1024
        ),
        cost_estimate=pl.CostEstimate(flops=13_000_000_000, bytes_accessed=8_000_000, transcendentals=4_000_000),
    )(
        frames, value_weight, gate_weight, conv_taps, out_weight, text_rows,
        window_low.reshape(1, TOK), audio_pos.reshape(NT, AUD),
        adapter, value_proj, queries, keys, grad_out,
    )


def solution(mesh):
    return jax.shard_map(
        body,
        mesh=mesh,
        in_specs=(
            P("tm", None),
            P(None, "ctx"),
            P(None, "ctx"),
            P(None, "ctx"),
            P("ctx", None),
            P("tm", "ctx"),
            P(),
            P("tm", "ctx"),
            P("ctx", "tm"),
            P(("tm", "ctx"), None),
            P(("tm", "ctx"), None),
            P(("tm", "ctx"), None),
            P("tm"),
        ),
        out_specs=(P("tm", "ctx"), P("tm", "ctx")),
        check_vma=False,
    )
```

```python
import math

import jax
import jax.numpy as jnp
from jax import lax
from jax.experimental import pallas as pl
from jax.experimental.pallas import tpu as pltpu
from jax.sharding import PartitionSpec as P

DH = 128
NORM_EPS = 1e-05
MASK_FILL = -1e30
MESH = pl.DeviceIdType.MESH
F32 = jnp.float32
BF16 = jnp.bfloat16

NT = 32
NC = 8
NX = 4
NZ = 8
TOK = 512
AUD = 128
DE = 1024
COLS = 1024
HC = 512
HH = HC // DH
HALF = TOK // 2
SLOT = 8
TILES = ((0, 0, 0, 256), (0, 256, 0, 512), (1, 0, 0, 512), (1, 256, 256, 256))
N_SEMS = 160
QUART = COLS // NX
ROWS_A = 512
ROWS_B = COLS - ROWS_A
OFFSETS = (0, -1, 1, -2, 2, -3, 3, 4)
ORDER = (
    "issue", "i_q", "i_ax", "b_s0", "i_bm", "mm", "LN", "d_s0", "conv", "b_s1", "m0", "p0",
    "d_s1", "i_k", "a0_s0", "rm", "enc", "hq", "b_s2", "p1", "r0", "a1_s0", "pos", "i_g",
    "encx", "b_s3", "d_s2", "sc0", "a0_s1", "sc1", "er", "d_s3", "p2", "a1_s1", "a0_s2", "hg",
    "adapt", "r1", "m1", "prob", "m3", "r2", "a1_s2", "place", "t0", "m2", "t1", "t2", "rs0",
    "r3", "a0_s3", "p3", "rs1", "vgr", "rs2", "t3", "t4", "t6", "t5", "ad0", "a1_s3", "rs3",
    "ad1", "ad2", "rs4", "vgf", "rs5", "ad3", "t7", "rs6", "ad4", "dh0", "ad5", "rs7", "dh1",
    "dh4", "ad6", "dh2", "ad7", "dh6", "dh5", "dh7", "delta", "dh3", "key",
)


def dot(a, b):
    return jnp.dot(a, b, preferred_element_type=F32)


def dot_t(a, b):
    return lax.dot_general(a, b, (((1,), (1,)), ((), ())), preferred_element_type=F32)


def iota(shape, dim):
    return lax.broadcasted_iota(jnp.int32, shape, dim)


def kernel(
    frames, vw, gw, taps, ow, text, low, aud, adapter, vp, q, k, g,
    dk_out, dh_out,
    W, AD, qs, gs, ks, low_s, lown, frames_s, vw_s, gw_s, taps_s, ow_s, text_s,
    slot_s, land_s, ext, glu_s, mixs, mixr, enc, adp, pick, inc, hid,
    e_ref, gv_ref, st_own, st_nxt, st_fp, st_fn, dl_own, dl_nxt, dl_fp, dl_fn,
    VG, psend, pown, precv, rsend, radd, rrecv, vbuf, acc,
    ssem, rsem, lsem, aus, aur, rss, rsr,
):
    t = lax.axis_index("tm")
    c = lax.axis_index("ctx")
    x = lax.rem(t, NX)
    z = lax.div(t, NX)
    core = lax.rem(c, 2)
    yy = lax.div(c, 2)
    up = (lax.rem(z + 1, NZ) * NX + x, c)
    dn = (lax.rem(z + NZ - 1, NZ) * NX + x, c)
    nxt = (lax.rem(t + 1, NT), c)
    prv = (lax.rem(t + NT - 1, NT), c)
    mate = (t, c + 1 - 2 * core)

    def ctx_peer(d):
        return (t, lax.rem(c + d, NC))

    def x_peer(d):
        return (z * NX + lax.rem(x + d, NX), c)

    def zat(d):
        return lax.rem(z + d + NZ, NZ)

    def al(v, m):
        return pl.multiple_of(v, m)

    sends = []
    groups = {}
    waited = set()

    def send(name, src, dst, dev):
        i = len(sends)
        copy = pltpu.make_async_remote_copy(
            src_ref=src, dst_ref=dst, send_sem=ssem.at[i], recv_sem=rsem.at[i],
            device_id=dev, device_id_type=MESH,
        )
        copy.start()
        sends.append(copy)
        groups.setdefault(name, []).append(copy)

    def need(*names):
        for name in names:
            if name not in waited:
                waited.add(name)
                for copy in groups[name]:
                    if name in here:
                        copy.wait()
                    else:
                        copy.wait_recv()

    here = set()

    def local(name, src, dst):
        copy = pltpu.make_async_copy(src, dst, lsem.at[len(here)])
        copy.start()
        here.add(name)
        groups[name] = [copy]

    own_rows = pl.ds(al(c * 64, 64), 64)
    own_cols = pl.ds(al(c * HC, HC), HC)
    ad_rows = pl.ds(al(t * 32, 32), 32)
    rows_a = pl.ds(0, ROWS_A)
    rows_b = pl.ds(ROWS_A, ROWS_B)

    def issue():
        bar = pltpu.get_barrier_semaphore()

        def greet(d, carry):
            pl.semaphore_signal(bar, inc=1, device_id=(lax.rem(t + d, NT), c), device_id_type=MESH)
            return carry

        lax.fori_loop(1, NT, greet, 0)
        for d in range(1, NC):
            pl.semaphore_signal(bar, inc=1, device_id=ctx_peer(d), device_id_type=MESH)
        local("frames", frames, frames_s)
        local("vw", vw, vw_s)
        local("gw", gw, gw_s)
        local("vp", vp, W.at[t])
        local("ad", adapter.at[:, pl.ds(al(x * QUART, QUART), QUART)], AD.at[ad_rows])
        local("taps", taps, taps_s)
        local("ow", ow, ow_s)
        local("k0", k.at[:, own_cols], ks.at[own_rows])
        local("q0", q.at[:, own_cols], qs.at[0, own_rows])
        local("g0", g.at[:, own_cols], gs.at[0, own_rows])
        local("text", text, text_s)
        low_s[...] = jnp.broadcast_to(low[...], low_s.shape)
        pl.semaphore_wait(bar, NT - 1 + NC - 1)
        send("fh", frames.at[pl.ds(AUD - 16, 16)], ext.at[pl.ds(0, 16)], nxt)
        send("fh", frames.at[pl.ds(0, 16)], ext.at[pl.ds(AUD + 16, 16)], prv)
        for d in (1, 3, 2):
            quarter = pl.ds(al(lax.rem(x + d, NX) * QUART, QUART), QUART)
            send("adx", adapter.at[:, quarter], AD.at[ad_rows], x_peer(d))
        send("low", low_s, lown, prv)

    def b_ref(zz, xx=x):
        return W.at[zz * NX + xx, rows_b]

    def b_part(zz, p):
        return W.at[zz * NX + x, pl.ds(ROWS_A + ROWS_B // 2 * p, ROWS_B // 2)]

    def a_ref(zz, pair):
        return W.at[pl.ds(zz * NX + 2 * pair, 2), rows_a]

    def a_part(zz, pair, p):
        return W.at[zz * NX + 2 * pair + p, rows_a]

    def d_ref(zz):
        return AD.at[pl.ds(al(zz * 128, 128), 128)]

    def d_part(zz, p):
        return AD.at[pl.ds(al(zz * 128 + 64 * p, 64), 64)]

    def ring(name, s, ref_of, part_of):
        if s < NZ // 2 - 1:
            u, v = ref_of(zat(-s)), ref_of(zat(s))
        else:
            u, v = part_of(zat(-s), 0), part_of(zat(s), 1)
        send(f"{name}{s}", u, u, up)
        send(f"{name}{s}", v, v, dn)

    def a_step(pair, s):
        need(*([f"a{pair}_{s - 1}"] if s else ["ax", "vp"]))
        ring(f"a{pair}_", s, lambda zz: a_ref(zz, pair), lambda zz, p: a_part(zz, pair, p))

    def b_step(s):
        need(*([f"b{s - 1}"] if s else ["vp"]))
        ring("b", s, b_ref, b_part)

    def d_step(s):
        need(*([f"d{s - 1}"] if s else ["adx", "ad"]))
        ring("d", s, d_ref, d_part)

    def reached(s):
        return (0,) if s < 0 else ((-1 - s, 1 + s) if s < 3 else (4,))

    def spread(s, d, kind):
        need(f"b{s}" if s >= 0 else "vp")
        for o in reached(s):
            send(f"{kind}{s}", b_ref(zat(o)), b_ref(zat(o)), x_peer(d))

    def relay(s):
        turn = 3 if s in (-1, 3) else 1
        need(f"p{s}" if turn == 1 else f"m{s}")
        origin = lax.rem(x + NX - turn, NX)
        for o in reached(s):
            send(f"r{s}", b_ref(zat(o), origin), b_ref(zat(o), origin), x_peer(turn))

    def issue_ax():
        for d in (1, 3, 2):
            send("ax", vp.at[rows_a], W.at[t, rows_a], x_peer(d))

    def regroup(name, src, dst):
        for d in (4, 1, 7, 2, 6, 3, 5):
            peer = lax.rem(c + d, NC)
            send(name, src.at[:, pl.ds(al(peer * HC, HC), HC)], dst.at[own_rows], (t, peer))

    def positions():
        order = (iota((AUD, AUD), 0) < iota((AUD, AUD), 1)).astype(F32).astype(BF16)
        for b in range(NX):
            target = aud[pl.ds(z * NX + b, 1), :] // TOK
            hit = (iota((NT, AUD), 0) == target).astype(F32)
            rank = jnp.sum(dot(hit.astype(BF16), order) * hit, axis=0, keepdims=True)
            slot = target * (NX * SLOT) + b * SLOT + rank.astype(jnp.int32)
            slot_s[:, pl.ds(b * AUD, AUD)] = jnp.broadcast_to(slot, (8, AUD))
        table = aud[...]
        landing = table // TOK == t
        landing_rank = dot(landing.astype(F32).astype(BF16), order)
        spot = jnp.where(landing, table - t * TOK + 1, 0)
        n = NT * SLOT
        grow = (iota((n, NT), 0) // SLOT == iota((n, NT), 1)).astype(F32).astype(BF16)
        spot_hi = dot(grow, (spot // 16).astype(F32).astype(BF16))
        spot_lo = dot(grow, (spot % 16).astype(F32).astype(BF16))
        ranks = dot(grow, jnp.where(landing, landing_rank, 64.0).astype(BF16))
        spots = spot_hi * 16.0 + spot_lo
        r = (iota((n, AUD), 0) % SLOT).astype(F32)
        col = jnp.sum(jnp.where(ranks == r, spots, 0.0), axis=1, keepdims=True) - 1.0
        eye = iota((n, n), 0) == iota((n, n), 1)
        line = jnp.sum(jnp.where(eye, col, 0.0), axis=0, keepdims=True)
        land_s[...] = jnp.broadcast_to(line, (8, n)).astype(jnp.int32)

    def norm_glu():
        need("frames", "vw", "gw")
        ext[pl.ds(16, AUD), :] = frames_s[...]
        need("fh")
        rows = ext[...].astype(F32)
        centre = jnp.mean(rows, axis=1, keepdims=True)
        off = rows - centre
        spread_ = jnp.mean(off * off, axis=1, keepdims=True)
        normed = (off * lax.rsqrt(spread_ + NORM_EPS)).astype(BF16)
        value_part = dot(normed, vw_s[...])
        gate_part = dot(normed, gw_s[...])
        glu = (value_part * jax.nn.sigmoid(gate_part)).astype(BF16).astype(F32)
        row = iota(glu.shape, 0)
        first = jnp.where(t == 0, 16, 0)
        last = jnp.where(t == NT - 1, AUD + 16, AUD + 32)
        glu_s[...] = jnp.where((row >= first) & (row < last), glu, 0.0)

    def conv():
        need("taps", "ow")
        smooth = jnp.zeros((AUD, DH), F32)
        for j in range(taps_s.shape[0]):
            smooth = smooth + taps_s[pl.ds(j, 1), :] * glu_s[pl.ds(1 + j, AUD), :]
        action = (smooth * jax.nn.sigmoid(smooth)).astype(BF16)
        mixs[...] = dot(action, ow_s[...]).astype(BF16)
        for d in (4, 2, 6, 3, 5, 1, 7):
            rows_d = pl.ds(al(lax.rem(c + d, NC) * 16, 16), 16)
            send("mix", mixs.at[rows_d], mixr.at[d], ctx_peer(d))

    def encode():
        need("mix")
        mine = pl.ds(al(c * 16, 16), 16)
        total = frames_s[mine, :].astype(F32) + mixs[mine, :].astype(F32)
        for d in range(1, NC):
            total = total + mixr[d].astype(F32)
        enc[x, mine, :] = total.astype(BF16)
        for d in (4, 2, 6, 3, 5, 1, 7):
            send("enc", enc.at[x, mine], enc.at[x, mine], ctx_peer(d))

    def encode_x():
        need("enc")
        for d in (1, 3):
            send("ex", enc.at[x], enc.at[x], x_peer(d))

    def encode_relay():
        need("ex")
        for d, at in ((1, 0), (3, AUD // 2)):
            part = enc.at[lax.rem(x + NX - d, NX), pl.ds(at, AUD // 2)]
            send("ex2", part, part, x_peer(d))

    def halo(name):
        part = qs if name == "q" else gs
        need(name, name + "0")
        send("h" + name, part.at[0], part.at[1], prv)

    scale = 1.0 / math.sqrt(DH)
    base = t * TOK
    row8 = iota((8, HALF), 0)

    def head_cols(h):
        return pl.ds(al(h * DH, DH), DH)

    def score_tiles(block, lows, limit, stats):
        def one_head(h, carry):
            hs = head_cols(h)
            for b, i0, j0, jn in TILES:
                if b != block:
                    continue
                qi = pl.ds(i0, HALF)
                s = dot_t(ks[pl.ds(j0, jn), hs], qs[b, qi, hs]) * scale
                jj = iota((jn, HALF), 0) + j0
                ok = jj >= lows[pl.ds(0, 1), qi] - base
                if block == 0:
                    ok = ok & (jj <= iota((jn, HALF), 1) + i0)
                else:
                    ok = ok & (jj < limit)
                s = jnp.where(ok, s, MASK_FILL)
                m = jnp.max(s, axis=0, keepdims=True)
                e = jnp.where(ok, jnp.exp(s - m), 0.0)
                n = jnp.sum(e, axis=0, keepdims=True)
                e_ref[b, h, pl.ds(j0, jn), qi] = e
                stats[h, :, qi] = jnp.where(row8 == 0, m, n)
            return carry

        lax.fori_loop(0, HH, one_head, 0)

    def score_own():
        need("k", "k0", "q", "q0")
        score_tiles(0, low_s, TOK, st_own)
        send("sta", st_own, st_fn, prv)

    def score_next():
        need("k", "k0", "hq", "low")
        score_tiles(1, lown, jnp.where(t == NT - 1, 0, TOK), st_nxt)
        send("stb", st_nxt, st_fp, nxt)

    group_rows = NX * SLOT
    my_slot = pl.ds(al(z * group_rows, group_rows), group_rows)

    def slot_rows(tm):
        return pl.ds(al(tm * group_rows, group_rows), group_rows)

    def audio_copy(d):
        peer = lax.rem(t + d, NT)
        return pltpu.make_async_remote_copy(
            src_ref=pick.at[slot_rows(peer)], dst_ref=inc.at[x, my_slot],
            send_sem=aus.at[d], recv_sem=aur.at[d], device_id=(peer, c), device_id_type=MESH,
        )

    def adapt():
        need("d3", "ex", "ex2")
        adp[...] = dot(enc[...].reshape(NX * AUD, DE), AD[...]).astype(BF16)
        for n in range(4):
            slot_row = iota((256, NX * AUD), 0) + 256 * n
            picker = (slot_row == slot_s[pl.ds(0, 1), :]).astype(F32).astype(BF16)
            pick[pl.ds(256 * n, 256), :] = dot(picker, adp[...]).astype(BF16)

        def audio_start(d, carry):
            audio_copy(d).start()
            return carry

        lax.fori_loop(1, NT, audio_start, 0)
        inc[x, my_slot, :] = pick[slot_rows(t), :]

    def factor(mine_st, other_st, h):
        m1, s1 = mine_st[h, pl.ds(0, 1), :], mine_st[h, pl.ds(1, 1), :]
        m2, s2 = other_st[h, pl.ds(0, 1), :], other_st[h, pl.ds(1, 1), :]
        m = jnp.maximum(m1, m2)
        a1 = jnp.exp(m1 - m)
        return a1 / (s1 * a1 + s2 * jnp.exp(m2 - m))

    def gather_terms(tiles, other, h):
        hs = head_cols(h)
        first, second = pl.ds(0, 256), pl.ds(256, 256)
        top = dot(tiles[0], other[0, first, hs]) + dot(tiles[1][:256], other[0, second, hs])
        top = top + dot(tiles[2][:256], other[1, first, hs])
        bottom = dot(tiles[1][256:], other[0, second, hs])
        bottom = bottom + dot(tiles[2][256:], other[1, first, hs])
        bottom = bottom + dot(tiles[3], other[1, second, hs])
        return top, bottom

    def prob():
        need("sta", "stb", "g", "g0", "hg")

        def prob_head(h, carry):
            f = (factor(st_own, st_fp, h), factor(st_nxt, st_fn, h))
            tiles = []
            for b, i0, j0, jn in TILES:
                p = e_ref[b, h, pl.ds(j0, jn), pl.ds(i0, HALF)] * f[b][:, i0 : i0 + HALF]
                e_ref[b, h, pl.ds(j0, jn), pl.ds(i0, HALF)] = p
                tiles.append(p.astype(BF16))
            top, bottom = gather_terms(tiles, gs, h)
            hs = head_cols(h)
            VG[c, pl.ds(0, 256), hs] = top.astype(BF16)
            VG[c, pl.ds(256, 256), hs] = bottom.astype(BF16)
            return carry

        lax.fori_loop(0, HH, prob_head, 0)
        send("vg1", VG.at[c], VG.at[c], ctx_peer(2))
        send("vg3", VG.at[c], VG.at[c], ctx_peer(6))
        send("vgc", VG.at[c], VG.at[c], mate)

    below, above, across = [lax.rem(c + d, NC) for d in (6, 2, 4)]

    def vg_relay():
        need("vg1", "vg3")
        one, two = VG.at[below, pl.ds(0, 256)], VG.at[above, pl.ds(256, 256)]
        send("vg2", one, one, ctx_peer(2))
        send("vg2", two, two, ctx_peer(6))
        send("vgc", VG.at[below], VG.at[below], mate)
        send("vgc", VG.at[above], VG.at[above], mate)

    def vg_last():
        need("vg2")
        send("vgc", VG.at[across], VG.at[across], mate)

    def place():
        need("text")

        def audio_arrived(d, carry):
            audio_copy(d).wait_recv()
            return carry

        lax.fori_loop(1, NT, audio_arrived, 0)
        hits = (iota((TOK, NT * SLOT), 0) == land_s[pl.ds(0, 1), :]).astype(F32)
        there = jnp.sum(hits, axis=1, keepdims=True) > 0.5
        hits = hits.astype(BF16)
        for n in range(NX):
            cols = pl.ds(QUART * n, QUART)
            rows_in = dot(hits, inc[n])
            hid[:, cols] = jnp.where(there, rows_in, text_s[:, cols].astype(F32)).astype(BF16)

    mate_rows = pl.ds(al((1 - core) * HALF, HALF), HALF)
    my_rows = pl.ds(al(core * HALF, HALF), HALF)

    def weights_ready(i):
        s = (i - 1) // 2
        need(f"m{s}", f"p{s}", f"r{s}")
        need(*([f"a0_{s}", f"a1_{s}", f"b{s}"] if i else ["ax", "vp"]))

    def terms(i):
        weights_ready(i)
        cp = zat(OFFSETS[i])
        w = jnp.concatenate([W[cp * HH + j] for j in range(HH)], axis=1)
        psend[i] = dot(hid[mate_rows, :], w).astype(BF16)
        send(f"pair{i}", psend.at[i], precv.at[i], mate)
        w = jnp.concatenate([W[cp * HH + j] for j in range(HH)], axis=1)
        pown[i] = dot(hid[my_rows, :], w).astype(BF16)

    def owner_copy(side, kd, i):
        owner = lax.rem(yy + 1 + 2 * side, NC // 2) * 2 + kd
        return pltpu.make_async_remote_copy(
            src_ref=rsend.at[i], dst_ref=rrecv.at[1 + side, my_rows],
            send_sem=rss.at[2 * side + kd], recv_sem=rsr.at[2 * side + core],
            device_id=(t, owner), device_id_type=MESH,
        )

    def add_copy(kd, i):
        return pltpu.make_async_remote_copy(
            src_ref=rsend.at[i], dst_ref=radd.at[kd],
            send_sem=rss.at[4 + kd], recv_sem=rsr.at[4 + kd],
            device_id=(t, lax.rem(c + 2 + 4 * core, NC)), device_id_type=MESH,
        )

    def mate_copy(i):
        return pltpu.make_async_remote_copy(
            src_ref=rsend.at[i], dst_ref=rrecv.at[0, my_rows],
            send_sem=rss.at[6], recv_sem=rsr.at[6], device_id=mate, device_id_type=MESH,
        )

    def owner_of(i):
        cp = zat(OFFSETS[i])
        return lax.rem(lax.div(cp, 2) - yy + NC // 2, NC // 2), lax.rem(cp, 2)

    def chip_sum(i):
        e, kd = owner_of(i)
        need(f"pair{i}")
        total = pown[i].astype(F32) + precv[i].astype(F32)
        rsend[i] = total.astype(BF16)

        @pl.when(e == 2)
        def _():
            add_copy(kd, i).start()

        @pl.when(e == 3 - 2 * core)
        def _():
            owner_copy(lax.div(e, 2), kd, i).start()

        @pl.when((e == 0) & (kd != core))
        def _():
            mate_copy(i).start()

        @pl.when((e == 0) & (kd == core))
        def _():
            rrecv[0, my_rows, :] = rsend[i]

    def added_sum(i):
        e, kd = owner_of(i)

        @pl.when(e == 1 + 2 * core)
        def _():
            add_copy(kd, i).wait_recv()
            total = rsend[i].astype(F32) + radd[kd].astype(F32)
            rsend[i] = total.astype(BF16)
            owner_copy(lax.div(e, 2), kd, i).start()

    added = []

    def hidden_grad(i):
        weights_ready(i)
        need("vgc")
        cp = zat(OFFSETS[i])
        added.append(i)
        first, last = len(added) == 1, len(added) == NC

        def part(n, carry):
            rows_n = pl.ds(al(n * 256, 256), 256)
            w = jnp.concatenate([W[cp * HH + j, rows_n, :] for j in range(HH)], axis=1)
            term = dot_t(VG[cp], w)
            if not first:
                term = term + acc[n]
            if last:
                dh_out[:, rows_n] = term.astype(BF16)
            else:
                acc[n] = term
            return carry

        lax.fori_loop(0, COLS // 256, part, 0)

    def delta():
        for n in (0, 1, 2, 3, 6):
            pltpu.make_async_remote_copy(
                src_ref=rsend.at[0], dst_ref=rrecv.at[0, my_rows], send_sem=rss.at[n],
                recv_sem=rsr.at[n], device_id=mate, device_id_type=MESH,
            ).wait_recv()
        total = rrecv[0].astype(F32) + rrecv[1].astype(F32) + rrecv[2].astype(F32)
        vbuf[...] = total.astype(BF16)

        def delta_head(h, carry):
            hs = head_cols(h)
            for b, i0, j0, jn in TILES:
                qi = pl.ds(i0, HALF)
                gv = dot_t(vbuf[pl.ds(j0, jn), hs], gs[b, qi, hs])
                gv_ref[b, h, pl.ds(j0, jn), qi] = gv
                w = e_ref[b, h, pl.ds(j0, jn), qi].astype(BF16).astype(F32)
                part = jnp.sum(w * gv, axis=0, keepdims=True)
                table = dl_own if b == 0 else dl_nxt
                table[h, :, qi] = jnp.where(row8 == 0, part, 0.0)
            return carry

        lax.fori_loop(0, HH, delta_head, 0)
        send("dl", dl_own, dl_fn, prv)
        send("dl", dl_nxt, dl_fp, nxt)

    def key():
        need("dl")

        def key_head(h, carry):
            deltas = (
                dl_own[h, pl.ds(0, 1), :] + dl_fp[h, pl.ds(0, 1), :],
                dl_nxt[h, pl.ds(0, 1), :] + dl_fn[h, pl.ds(0, 1), :],
            )
            tiles = []
            for b, i0, j0, jn in TILES:
                qi = pl.ds(i0, HALF)
                p = e_ref[b, h, pl.ds(j0, jn), qi]
                gv = gv_ref[b, h, pl.ds(j0, jn), qi]
                tiles.append((p * (gv - deltas[b][:, i0 : i0 + HALF])).astype(BF16))
            top, bottom = gather_terms(tiles, qs, h)
            hs = head_cols(h)
            dk_out[pl.ds(0, 256), hs] = (top * scale).astype(BF16)
            dk_out[pl.ds(256, 256), hs] = (bottom * scale).astype(BF16)
            return carry

        lax.fori_loop(0, HH, key_head, 0)

    steps = {
        "issue": issue, "i_ax": issue_ax,
        "i_bm": lambda: spread(-1, 1, "p"), "mm": lambda: spread(-1, 3, "m"),
        "i_k": lambda: regroup("k", k, ks),
        "i_q": lambda: regroup("q", q, qs.at[0]),
        "i_g": lambda: regroup("g", g, gs.at[0]),
        "pos": positions, "LN": norm_glu, "conv": conv, "enc": encode, "encx": encode_x, "er": encode_relay, "adapt": adapt, "place": place,
        "hq": lambda: halo("q"), "hg": lambda: halo("g"),
        "sc0": score_own, "sc1": score_next, "prob": prob, "vgr": vg_relay, "vgf": vg_last,
        "rm": lambda: relay(-1), "delta": delta, "key": key,
    }
    for s in range(4):
        steps[f"a0_s{s}"] = lambda s=s: a_step(0, s)
        steps[f"a1_s{s}"] = lambda s=s: a_step(1, s)
        steps[f"b_s{s}"] = lambda s=s: b_step(s)
        steps[f"d_s{s}"] = lambda s=s: d_step(s)
        steps[f"p{s}"] = lambda s=s: spread(s, 1, "p")
        steps[f"m{s}"] = lambda s=s: spread(s, 3, "m")
        steps[f"r{s}"] = lambda s=s: relay(s)
    for i in range(NC):
        steps[f"t{i}"] = lambda i=i: terms(i)
        steps[f"rs{i}"] = lambda i=i: chip_sum(i)
        steps[f"ad{i}"] = lambda i=i: added_sum(i)
        steps[f"dh{i}"] = lambda i=i: hidden_grad(i)
    for name in ORDER:
        steps[name]()

    def audio_sent(d, carry):
        audio_copy(d).wait_send()
        return carry

    lax.fori_loop(1, NT, audio_sent, 0)
    for n in range(7):
        pltpu.make_async_remote_copy(
            src_ref=rsend.at[0], dst_ref=rrecv.at[0, my_rows], send_sem=rss.at[n],
            recv_sem=rsr.at[n], device_id=mate, device_id_type=MESH,
        ).wait_send()
    for name in groups:
        need(name)
    for copy in sends:
        copy.wait_send()


def body(
    frames, value_weight, gate_weight, conv_taps, out_weight, adapter, audio_pos, text_rows,
    value_proj, queries, keys, grad_out, window_low,
):
    vm = pl.BlockSpec(memory_space=pltpu.VMEM)
    hbm = pl.BlockSpec(memory_space=pl.ANY)
    vmem = pltpu.VMEM
    dma = pltpu.SemaphoreType.DMA
    return pl.pallas_call(
        kernel,
        out_shape=(
            jax.ShapeDtypeStruct((TOK, HC), BF16),
            jax.ShapeDtypeStruct((TOK, COLS), BF16),
        ),
        in_specs=[hbm] * 6 + [vm] * 2 + [hbm] * 5,
        out_specs=(vm, vm),
        scratch_shapes=[
            vmem((NT, COLS, DH), BF16),
            vmem((DE, QUART), BF16),
            vmem((2, TOK, HC), BF16),
            vmem((2, TOK, HC), BF16),
            vmem((TOK, HC), BF16),
            vmem((8, TOK), jnp.int32),
            vmem((8, TOK), jnp.int32),
            vmem((AUD, DE), BF16),
            vmem((DE, DH), BF16),
            vmem((DE, DH), BF16),
            vmem(conv_taps.shape, F32),
            vmem((DH, DE), BF16),
            vmem((TOK, COLS), BF16),
            vmem((8, NX * AUD), jnp.int32),
            vmem((8, NT * SLOT), jnp.int32),
            vmem((AUD + 32, DE), BF16),
            vmem((AUD + 32, DH), F32),
            vmem((AUD, DE), BF16),
            vmem((NC, 16, DE), BF16),
            vmem((NX, AUD, DE), BF16),
            vmem((NX * AUD, QUART), BF16),
            vmem((NT * NX * SLOT, QUART), BF16),
            vmem((NX, NT * SLOT, QUART), BF16),
            vmem((TOK, COLS), BF16),
            vmem((2, HH, TOK, TOK), F32),
            vmem((2, HH, TOK, TOK), F32),
        ]
        + [vmem((HH, 8, TOK), F32)] * 8
        + [
            vmem((NC, TOK, HC), BF16),
            vmem((NC, HALF, HC), BF16),
            vmem((NC, HALF, HC), BF16),
            vmem((NC, HALF, HC), BF16),
            vmem((NC, HALF, HC), BF16),
            vmem((2, HALF, HC), BF16),
            vmem((3, TOK, HC), BF16),
            vmem((TOK, HC), BF16),
            vmem((COLS // 256, TOK, 256), F32),
            dma((N_SEMS,)),
            dma((N_SEMS,)),
            dma((16,)),
            dma((NT,)),
            dma((NT,)),
            dma((NC,)),
            dma((NC,)),
        ],
        compiler_params=pltpu.CompilerParams(
            collective_id=0, has_side_effects=True, vmem_limit_bytes=60 * 1024 * 1024
        ),
        cost_estimate=pl.CostEstimate(flops=13_000_000_000, bytes_accessed=8_000_000, transcendentals=4_000_000),
    )(
        frames, value_weight, gate_weight, conv_taps, out_weight, text_rows,
        window_low.reshape(1, TOK), audio_pos.reshape(NT, AUD),
        adapter, value_proj, queries, keys, grad_out,
    )


def solution(mesh):
    return jax.shard_map(
        body,
        mesh=mesh,
        in_specs=(
            P("tm", None),
            P(None, "ctx"),
            P(None, "ctx"),
            P(None, "ctx"),
            P("ctx", None),
            P("tm", "ctx"),
            P(),
            P("tm", "ctx"),
            P("ctx", "tm"),
            P(("tm", "ctx"), None),
            P(("tm", "ctx"), None),
            P(("tm", "ctx"), None),
            P("tm"),
        ),
        out_specs=(P("tm", "ctx"), P("tm", "ctx")),
        check_vma=False,
    )
```

```python
import math

import jax
import jax.numpy as jnp
from jax import lax
from jax.experimental import pallas as pl
from jax.experimental.pallas import tpu as pltpu
from jax.sharding import PartitionSpec as P

DH = 128
NORM_EPS = 1e-05
MASK_FILL = -1e30
MESH = pl.DeviceIdType.MESH
F32 = jnp.float32
BF16 = jnp.bfloat16

NT = 32
NC = 8
NX = 4
NZ = 8
TOK = 512
AUD = 128
DE = 1024
COLS = 1024
HC = 512
HH = HC // DH
HALF = TOK // 2
SLOT = 8
TILES = ((0, 0, 0, 256), (0, 256, 0, 512), (1, 0, 0, 512), (1, 256, 256, 256))
N_SEMS = 160
QUART = COLS // NX
ROWS_A = 512
ROWS_B = COLS - ROWS_A
OFFSETS = (0, -1, 1, -2, 2, -3, 3, 4)
ORDER = (
    "issue", "i_q", "b_s0", "i_ax", "LN", "mm", "d_s0", "b_s1", "i_bm", "conv", "m0", "p0",
    "d_s1", "i_k", "b_s2", "hq", "a0_s0", "d_s2", "enc", "r0", "pos", "a1_s0", "i_g", "encx",
    "a0_s1", "b_s3", "sc0", "a1_s1", "d_s3", "er", "hg", "p3", "a0_s2", "p1", "sc1", "adapt",
    "p2", "prob", "m1", "rm", "m3", "a1_s2", "r1", "place", "r2", "m2", "t0", "vgr", "r3", "t1",
    "a0_s3", "a1_s3", "rs0", "t2", "t4", "rs2", "rs1", "t3", "t6", "ad0", "t7", "rs4", "rs3",
    "t5", "ad1", "ad4", "vgf", "rs5", "dh0", "dh1", "dh4", "rs6", "rs7", "dh2", "dh3", "dh5",
    "ad3", "ad2", "ad5", "dh6", "ad6", "ad7", "delta", "dh7", "key",
)


def dot(a, b):
    return jnp.dot(a, b, preferred_element_type=F32)


def dot_t(a, b):
    return lax.dot_general(a, b, (((1,), (1,)), ((), ())), preferred_element_type=F32)


def iota(shape, dim):
    return lax.broadcasted_iota(jnp.int32, shape, dim)


def kernel(
    frames, vw, gw, taps, ow, text, low, aud, adapter, vp, q, k, g,
    dk_out, dh_out,
    W, AD, qs, gs, ks, low_s, lown, frames_s, vw_s, gw_s, taps_s, ow_s, text_s,
    slot_s, land_s, ext, glu_s, mixs, mixr, enc, adp, pick, inc, hid,
    e_ref, gv_ref, st_own, st_nxt, st_fp, st_fn, dl_own, dl_nxt, dl_fp, dl_fn,
    VG, psend, pown, precv, rsend, radd, rrecv, vbuf, acc,
    ssem, rsem, lsem, aus, aur, rss, rsr,
):
    t = lax.axis_index("tm")
    c = lax.axis_index("ctx")
    x = lax.rem(t, NX)
    z = lax.div(t, NX)
    core = lax.rem(c, 2)
    yy = lax.div(c, 2)
    up = (lax.rem(z + 1, NZ) * NX + x, c)
    dn = (lax.rem(z + NZ - 1, NZ) * NX + x, c)
    nxt = (lax.rem(t + 1, NT), c)
    prv = (lax.rem(t + NT - 1, NT), c)
    mate = (t, c + 1 - 2 * core)

    def ctx_peer(d):
        return (t, lax.rem(c + d, NC))

    def x_peer(d):
        return (z * NX + lax.rem(x + d, NX), c)

    def zat(d):
        return lax.rem(z + d + NZ, NZ)

    def al(v, m):
        return pl.multiple_of(v, m)

    sends = []
    groups = {}
    waited = set()

    def send(name, src, dst, dev):
        i = len(sends)
        copy = pltpu.make_async_remote_copy(
            src_ref=src, dst_ref=dst, send_sem=ssem.at[i], recv_sem=rsem.at[i],
            device_id=dev, device_id_type=MESH,
        )
        copy.start()
        sends.append(copy)
        groups.setdefault(name, []).append(copy)

    def need(*names):
        for name in names:
            if name not in waited:
                waited.add(name)
                for copy in groups[name]:
                    if name in here:
                        copy.wait()
                    else:
                        copy.wait_recv()

    here = set()

    def local(name, src, dst):
        copy = pltpu.make_async_copy(src, dst, lsem.at[len(here)])
        copy.start()
        here.add(name)
        groups[name] = [copy]

    own_rows = pl.ds(al(c * 64, 64), 64)
    own_cols = pl.ds(al(c * HC, HC), HC)
    ad_rows = pl.ds(al(t * 32, 32), 32)
    rows_a = pl.ds(0, ROWS_A)
    rows_b = pl.ds(ROWS_A, ROWS_B)

    def issue():
        bar = pltpu.get_barrier_semaphore()

        def greet(d, carry):
            pl.semaphore_signal(bar, inc=1, device_id=(lax.rem(t + d, NT), c), device_id_type=MESH)
            return carry

        lax.fori_loop(1, NT, greet, 0)
        for d in range(1, NC):
            pl.semaphore_signal(bar, inc=1, device_id=ctx_peer(d), device_id_type=MESH)
        local("frames", frames, frames_s)
        local("vw", vw, vw_s)
        local("gw", gw, gw_s)
        local("vp", vp, W.at[t])
        local("ad", adapter.at[:, pl.ds(al(x * QUART, QUART), QUART)], AD.at[ad_rows])
        local("taps", taps, taps_s)
        local("ow", ow, ow_s)
        local("k0", k.at[:, own_cols], ks.at[own_rows])
        local("q0", q.at[:, own_cols], qs.at[0, own_rows])
        local("g0", g.at[:, own_cols], gs.at[0, own_rows])
        local("text", text, text_s)
        low_s[...] = jnp.broadcast_to(low[...], low_s.shape)
        pl.semaphore_wait(bar, NT - 1 + NC - 1)
        send("fh", frames.at[pl.ds(AUD - 16, 16)], ext.at[pl.ds(0, 16)], nxt)
        send("fh", frames.at[pl.ds(0, 16)], ext.at[pl.ds(AUD + 16, 16)], prv)
        for d in (1, 3, 2):
            quarter = pl.ds(al(lax.rem(x + d, NX) * QUART, QUART), QUART)
            send("adx", adapter.at[:, quarter], AD.at[ad_rows], x_peer(d))
        send("low", low_s, lown, prv)

    def b_ref(zz, xx=x):
        return W.at[zz * NX + xx, rows_b]

    def b_part(zz, p):
        return W.at[zz * NX + x, pl.ds(ROWS_A + ROWS_B // 2 * p, ROWS_B // 2)]

    def a_ref(zz, pair):
        return W.at[pl.ds(zz * NX + 2 * pair, 2), rows_a]

    def a_part(zz, pair, p):
        return W.at[zz * NX + 2 * pair + p, rows_a]

    def d_ref(zz):
        return AD.at[pl.ds(al(zz * 128, 128), 128)]

    def d_part(zz, p):
        return AD.at[pl.ds(al(zz * 128 + 64 * p, 64), 64)]

    def ring(name, s, ref_of, part_of):
        if s < NZ // 2 - 1:
            u, v = ref_of(zat(-s)), ref_of(zat(s))
        else:
            u, v = part_of(zat(-s), 0), part_of(zat(s), 1)
        send(f"{name}{s}", u, u, up)
        send(f"{name}{s}", v, v, dn)

    def a_step(pair, s):
        need(*([f"a{pair}_{s - 1}"] if s else ["ax", "vp"]))
        ring(f"a{pair}_", s, lambda zz: a_ref(zz, pair), lambda zz, p: a_part(zz, pair, p))

    def b_step(s):
        need(*([f"b{s - 1}"] if s else ["vp"]))
        ring("b", s, b_ref, b_part)

    def d_step(s):
        need(*([f"d{s - 1}"] if s else ["adx", "ad"]))
        ring("d", s, d_ref, d_part)

    def reached(s):
        return (0,) if s < 0 else ((-1 - s, 1 + s) if s < 3 else (4,))

    def spread(s, d, kind):
        need(f"b{s}" if s >= 0 else "vp")
        for o in reached(s):
            send(f"{kind}{s}", b_ref(zat(o)), b_ref(zat(o)), x_peer(d))

    def relay(s):
        turn = 3 if s in (-1, 3) else 1
        need(f"p{s}" if turn == 1 else f"m{s}")
        origin = lax.rem(x + NX - turn, NX)
        for o in reached(s):
            send(f"r{s}", b_ref(zat(o), origin), b_ref(zat(o), origin), x_peer(turn))

    def issue_ax():
        for d in (1, 3, 2):
            send("ax", vp.at[rows_a], W.at[t, rows_a], x_peer(d))

    def regroup(name, src, dst):
        for d in (4, 1, 7, 2, 6, 3, 5):
            peer = lax.rem(c + d, NC)
            send(name, src.at[:, pl.ds(al(peer * HC, HC), HC)], dst.at[own_rows], (t, peer))

    def positions():
        order = (iota((AUD, AUD), 0) < iota((AUD, AUD), 1)).astype(F32).astype(BF16)
        for b in range(NX):
            target = aud[pl.ds(z * NX + b, 1), :] // TOK
            hit = (iota((NT, AUD), 0) == target).astype(F32)
            rank = jnp.sum(dot(hit.astype(BF16), order) * hit, axis=0, keepdims=True)
            slot = target * (NX * SLOT) + b * SLOT + rank.astype(jnp.int32)
            slot_s[:, pl.ds(b * AUD, AUD)] = jnp.broadcast_to(slot, (8, AUD))
        table = aud[...]
        landing = table // TOK == t
        landing_rank = dot(landing.astype(F32).astype(BF16), order)
        spot = jnp.where(landing, table - t * TOK + 1, 0)
        n = NT * SLOT
        grow = (iota((n, NT), 0) // SLOT == iota((n, NT), 1)).astype(F32).astype(BF16)
        spot_hi = dot(grow, (spot // 16).astype(F32).astype(BF16))
        spot_lo = dot(grow, (spot % 16).astype(F32).astype(BF16))
        ranks = dot(grow, jnp.where(landing, landing_rank, 64.0).astype(BF16))
        spots = spot_hi * 16.0 + spot_lo
        r = (iota((n, AUD), 0) % SLOT).astype(F32)
        col = jnp.sum(jnp.where(ranks == r, spots, 0.0), axis=1, keepdims=True) - 1.0
        eye = iota((n, n), 0) == iota((n, n), 1)
        line = jnp.sum(jnp.where(eye, col, 0.0), axis=0, keepdims=True)
        land_s[...] = jnp.broadcast_to(line, (8, n)).astype(jnp.int32)

    def norm_glu():
        need("frames", "vw", "gw")
        ext[pl.ds(16, AUD), :] = frames_s[...]
        need("fh")
        rows = ext[...].astype(F32)
        centre = jnp.mean(rows, axis=1, keepdims=True)
        off = rows - centre
        spread_ = jnp.mean(off * off, axis=1, keepdims=True)
        normed = (off * lax.rsqrt(spread_ + NORM_EPS)).astype(BF16)
        value_part = dot(normed, vw_s[...])
        gate_part = dot(normed, gw_s[...])
        glu = (value_part * jax.nn.sigmoid(gate_part)).astype(BF16).astype(F32)
        row = iota(glu.shape, 0)
        first = jnp.where(t == 0, 16, 0)
        last = jnp.where(t == NT - 1, AUD + 16, AUD + 32)
        glu_s[...] = jnp.where((row >= first) & (row < last), glu, 0.0)

    def conv():
        need("taps", "ow")
        smooth = jnp.zeros((AUD, DH), F32)
        for j in range(taps_s.shape[0]):
            smooth = smooth + taps_s[pl.ds(j, 1), :] * glu_s[pl.ds(1 + j, AUD), :]
        action = (smooth * jax.nn.sigmoid(smooth)).astype(BF16)
        mixs[...] = dot(action, ow_s[...]).astype(BF16)
        for d in (4, 2, 6, 3, 5, 1, 7):
            rows_d = pl.ds(al(lax.rem(c + d, NC) * 16, 16), 16)
            send("mix", mixs.at[rows_d], mixr.at[d], ctx_peer(d))

    def encode():
        need("mix")
        mine = pl.ds(al(c * 16, 16), 16)
        total = frames_s[mine, :].astype(F32) + mixs[mine, :].astype(F32)
        for d in range(1, NC):
            total = total + mixr[d].astype(F32)
        enc[x, mine, :] = total.astype(BF16)
        for d in (4, 2, 6, 3, 5, 1, 7):
            send("enc", enc.at[x, mine], enc.at[x, mine], ctx_peer(d))

    def encode_x():
        need("enc")
        for d in (1, 3):
            send("ex", enc.at[x], enc.at[x], x_peer(d))

    def encode_relay():
        need("ex")
        for d, at in ((1, 0), (3, AUD // 2)):
            part = enc.at[lax.rem(x + NX - d, NX), pl.ds(at, AUD // 2)]
            send("ex2", part, part, x_peer(d))

    def halo(name):
        part = qs if name == "q" else gs
        need(name, name + "0")
        send("h" + name, part.at[0], part.at[1], prv)

    scale = 1.0 / math.sqrt(DH)
    base = t * TOK
    row8 = iota((8, HALF), 0)

    def head_cols(h):
        return pl.ds(al(h * DH, DH), DH)

    def score_tiles(block, lows, limit, stats):
        def one_head(h, carry):
            hs = head_cols(h)
            for b, i0, j0, jn in TILES:
                if b != block:
                    continue
                qi = pl.ds(i0, HALF)
                s = dot_t(ks[pl.ds(j0, jn), hs], qs[b, qi, hs]) * scale
                jj = iota((jn, HALF), 0) + j0
                ok = jj >= lows[pl.ds(0, 1), qi] - base
                if block == 0:
                    ok = ok & (jj <= iota((jn, HALF), 1) + i0)
                else:
                    ok = ok & (jj < limit)
                s = jnp.where(ok, s, MASK_FILL)
                m = jnp.max(s, axis=0, keepdims=True)
                e = jnp.where(ok, jnp.exp(s - m), 0.0)
                n = jnp.sum(e, axis=0, keepdims=True)
                e_ref[b, h, pl.ds(j0, jn), qi] = e
                stats[h, :, qi] = jnp.where(row8 == 0, m, n)
            return carry

        lax.fori_loop(0, HH, one_head, 0)

    def score_own():
        need("k", "k0", "q", "q0")
        score_tiles(0, low_s, TOK, st_own)
        send("sta", st_own, st_fn, prv)

    def score_next():
        need("k", "k0", "hq", "low")
        score_tiles(1, lown, jnp.where(t == NT - 1, 0, TOK), st_nxt)
        send("stb", st_nxt, st_fp, nxt)

    group_rows = NX * SLOT
    my_slot = pl.ds(al(z * group_rows, group_rows), group_rows)

    def slot_rows(tm):
        return pl.ds(al(tm * group_rows, group_rows), group_rows)

    def audio_copy(d):
        peer = lax.rem(t + d, NT)
        return pltpu.make_async_remote_copy(
            src_ref=pick.at[slot_rows(peer)], dst_ref=inc.at[x, my_slot],
            send_sem=aus.at[d], recv_sem=aur.at[d], device_id=(peer, c), device_id_type=MESH,
        )

    def adapt():
        need("d3", "ex", "ex2")
        adp[...] = dot(enc[...].reshape(NX * AUD, DE), AD[...]).astype(BF16)
        for n in range(4):
            slot_row = iota((256, NX * AUD), 0) + 256 * n
            picker = (slot_row == slot_s[pl.ds(0, 1), :]).astype(F32).astype(BF16)
            pick[pl.ds(256 * n, 256), :] = dot(picker, adp[...]).astype(BF16)

        def audio_start(d, carry):
            audio_copy(d).start()
            return carry

        lax.fori_loop(1, NT, audio_start, 0)
        inc[x, my_slot, :] = pick[slot_rows(t), :]

    def factor(mine_st, other_st, h):
        m1, s1 = mine_st[h, pl.ds(0, 1), :], mine_st[h, pl.ds(1, 1), :]
        m2, s2 = other_st[h, pl.ds(0, 1), :], other_st[h, pl.ds(1, 1), :]
        m = jnp.maximum(m1, m2)
        a1 = jnp.exp(m1 - m)
        return a1 / (s1 * a1 + s2 * jnp.exp(m2 - m))

    def gather_terms(tiles, other, h):
        hs = head_cols(h)
        first, second = pl.ds(0, 256), pl.ds(256, 256)
        top = dot(tiles[0], other[0, first, hs]) + dot(tiles[1][:256], other[0, second, hs])
        top = top + dot(tiles[2][:256], other[1, first, hs])
        bottom = dot(tiles[1][256:], other[0, second, hs])
        bottom = bottom + dot(tiles[2][256:], other[1, first, hs])
        bottom = bottom + dot(tiles[3], other[1, second, hs])
        return top, bottom

    def prob():
        need("sta", "stb", "g", "g0", "hg")

        def prob_head(h, carry):
            f = (factor(st_own, st_fp, h), factor(st_nxt, st_fn, h))
            tiles = []
            for b, i0, j0, jn in TILES:
                p = e_ref[b, h, pl.ds(j0, jn), pl.ds(i0, HALF)] * f[b][:, i0 : i0 + HALF]
                e_ref[b, h, pl.ds(j0, jn), pl.ds(i0, HALF)] = p
                tiles.append(p.astype(BF16))
            top, bottom = gather_terms(tiles, gs, h)
            hs = head_cols(h)
            VG[c, pl.ds(0, 256), hs] = top.astype(BF16)
            VG[c, pl.ds(256, 256), hs] = bottom.astype(BF16)
            return carry

        lax.fori_loop(0, HH, prob_head, 0)
        send("vg1", VG.at[c], VG.at[c], ctx_peer(2))
        send("vg3", VG.at[c], VG.at[c], ctx_peer(6))
        send("vgc", VG.at[c], VG.at[c], mate)

    below, above, across = [lax.rem(c + d, NC) for d in (6, 2, 4)]

    def vg_relay():
        need("vg1", "vg3")
        one, two = VG.at[below, pl.ds(0, 256)], VG.at[above, pl.ds(256, 256)]
        send("vg2", one, one, ctx_peer(2))
        send("vg2", two, two, ctx_peer(6))
        send("vgc", VG.at[below], VG.at[below], mate)
        send("vgc", VG.at[above], VG.at[above], mate)

    def vg_last():
        need("vg2")
        send("vgc", VG.at[across], VG.at[across], mate)

    def place():
        need("text")

        def audio_arrived(d, carry):
            audio_copy(d).wait_recv()
            return carry

        lax.fori_loop(1, NT, audio_arrived, 0)
        hits = (iota((TOK, NT * SLOT), 0) == land_s[pl.ds(0, 1), :]).astype(F32)
        there = jnp.sum(hits, axis=1, keepdims=True) > 0.5
        hits = hits.astype(BF16)
        for n in range(NX):
            cols = pl.ds(QUART * n, QUART)
            rows_in = dot(hits, inc[n])
            hid[:, cols] = jnp.where(there, rows_in, text_s[:, cols].astype(F32)).astype(BF16)

    mate_rows = pl.ds(al((1 - core) * HALF, HALF), HALF)
    my_rows = pl.ds(al(core * HALF, HALF), HALF)

    def weights_ready(i):
        s = (i - 1) // 2
        need(f"m{s}", f"p{s}", f"r{s}")
        need(*([f"a0_{s}", f"a1_{s}", f"b{s}"] if i else ["ax", "vp"]))

    def terms(i):
        weights_ready(i)
        cp = zat(OFFSETS[i])
        w = jnp.concatenate([W[cp * HH + j] for j in range(HH)], axis=1)
        psend[i] = dot(hid[mate_rows, :], w).astype(BF16)
        send(f"pair{i}", psend.at[i], precv.at[i], mate)
        w = jnp.concatenate([W[cp * HH + j] for j in range(HH)], axis=1)
        pown[i] = dot(hid[my_rows, :], w).astype(BF16)

    def owner_copy(side, kd, i):
        owner = lax.rem(yy + 1 + 2 * side, NC // 2) * 2 + kd
        return pltpu.make_async_remote_copy(
            src_ref=rsend.at[i], dst_ref=rrecv.at[1 + side, my_rows],
            send_sem=rss.at[2 * side + kd], recv_sem=rsr.at[2 * side + core],
            device_id=(t, owner), device_id_type=MESH,
        )

    def add_copy(kd, i):
        return pltpu.make_async_remote_copy(
            src_ref=rsend.at[i], dst_ref=radd.at[kd],
            send_sem=rss.at[4 + kd], recv_sem=rsr.at[4 + kd],
            device_id=(t, lax.rem(c + 2 + 4 * core, NC)), device_id_type=MESH,
        )

    def mate_copy(i):
        return pltpu.make_async_remote_copy(
            src_ref=rsend.at[i], dst_ref=rrecv.at[0, my_rows],
            send_sem=rss.at[6], recv_sem=rsr.at[6], device_id=mate, device_id_type=MESH,
        )

    def owner_of(i):
        cp = zat(OFFSETS[i])
        return lax.rem(lax.div(cp, 2) - yy + NC // 2, NC // 2), lax.rem(cp, 2)

    def chip_sum(i):
        e, kd = owner_of(i)
        need(f"pair{i}")
        total = pown[i].astype(F32) + precv[i].astype(F32)
        rsend[i] = total.astype(BF16)

        @pl.when(e == 2)
        def _():
            add_copy(kd, i).start()

        @pl.when(e == 3 - 2 * core)
        def _():
            owner_copy(lax.div(e, 2), kd, i).start()

        @pl.when((e == 0) & (kd != core))
        def _():
            mate_copy(i).start()

        @pl.when((e == 0) & (kd == core))
        def _():
            rrecv[0, my_rows, :] = rsend[i]

    def added_sum(i):
        e, kd = owner_of(i)

        @pl.when(e == 1 + 2 * core)
        def _():
            add_copy(kd, i).wait_recv()
            total = rsend[i].astype(F32) + radd[kd].astype(F32)
            rsend[i] = total.astype(BF16)
            owner_copy(lax.div(e, 2), kd, i).start()

    added = []

    def hidden_grad(i):
        weights_ready(i)
        need("vgc")
        cp = zat(OFFSETS[i])
        added.append(i)
        first, last = len(added) == 1, len(added) == NC

        def part(n, carry):
            rows_n = pl.ds(al(n * 256, 256), 256)
            w = jnp.concatenate([W[cp * HH + j, rows_n, :] for j in range(HH)], axis=1)
            term = dot_t(VG[cp], w)
            if not first:
                term = term + acc[n]
            if last:
                dh_out[:, rows_n] = term.astype(BF16)
            else:
                acc[n] = term
            return carry

        lax.fori_loop(0, COLS // 256, part, 0)

    def delta():
        for n in (0, 1, 2, 3, 6):
            pltpu.make_async_remote_copy(
                src_ref=rsend.at[0], dst_ref=rrecv.at[0, my_rows], send_sem=rss.at[n],
                recv_sem=rsr.at[n], device_id=mate, device_id_type=MESH,
            ).wait_recv()
        total = rrecv[0].astype(F32) + rrecv[1].astype(F32) + rrecv[2].astype(F32)
        vbuf[...] = total.astype(BF16)

        def delta_head(h, carry):
            hs = head_cols(h)
            for b, i0, j0, jn in TILES:
                qi = pl.ds(i0, HALF)
                gv = dot_t(vbuf[pl.ds(j0, jn), hs], gs[b, qi, hs])
                gv_ref[b, h, pl.ds(j0, jn), qi] = gv
                w = e_ref[b, h, pl.ds(j0, jn), qi].astype(BF16).astype(F32)
                part = jnp.sum(w * gv, axis=0, keepdims=True)
                table = dl_own if b == 0 else dl_nxt
                table[h, :, qi] = jnp.where(row8 == 0, part, 0.0)
            return carry

        lax.fori_loop(0, HH, delta_head, 0)
        send("dl", dl_own, dl_fn, prv)
        send("dl", dl_nxt, dl_fp, nxt)

    def key():
        need("dl")

        def key_head(h, carry):
            deltas = (
                dl_own[h, pl.ds(0, 1), :] + dl_fp[h, pl.ds(0, 1), :],
                dl_nxt[h, pl.ds(0, 1), :] + dl_fn[h, pl.ds(0, 1), :],
            )
            tiles = []
            for b, i0, j0, jn in TILES:
                qi = pl.ds(i0, HALF)
                p = e_ref[b, h, pl.ds(j0, jn), qi]
                gv = gv_ref[b, h, pl.ds(j0, jn), qi]
                tiles.append((p * (gv - deltas[b][:, i0 : i0 + HALF])).astype(BF16))
            top, bottom = gather_terms(tiles, qs, h)
            hs = head_cols(h)
            dk_out[pl.ds(0, 256), hs] = (top * scale).astype(BF16)
            dk_out[pl.ds(256, 256), hs] = (bottom * scale).astype(BF16)
            return carry

        lax.fori_loop(0, HH, key_head, 0)

    steps = {
        "issue": issue, "i_ax": issue_ax,
        "i_bm": lambda: spread(-1, 1, "p"), "mm": lambda: spread(-1, 3, "m"),
        "i_k": lambda: regroup("k", k, ks),
        "i_q": lambda: regroup("q", q, qs.at[0]),
        "i_g": lambda: regroup("g", g, gs.at[0]),
        "pos": positions, "LN": norm_glu, "conv": conv, "enc": encode, "encx": encode_x, "er": encode_relay, "adapt": adapt, "place": place,
        "hq": lambda: halo("q"), "hg": lambda: halo("g"),
        "sc0": score_own, "sc1": score_next, "prob": prob, "vgr": vg_relay, "vgf": vg_last,
        "rm": lambda: relay(-1), "delta": delta, "key": key,
    }
    for s in range(4):
        steps[f"a0_s{s}"] = lambda s=s: a_step(0, s)
        steps[f"a1_s{s}"] = lambda s=s: a_step(1, s)
        steps[f"b_s{s}"] = lambda s=s: b_step(s)
        steps[f"d_s{s}"] = lambda s=s: d_step(s)
        steps[f"p{s}"] = lambda s=s: spread(s, 1, "p")
        steps[f"m{s}"] = lambda s=s: spread(s, 3, "m")
        steps[f"r{s}"] = lambda s=s: relay(s)
    for i in range(NC):
        steps[f"t{i}"] = lambda i=i: terms(i)
        steps[f"rs{i}"] = lambda i=i: chip_sum(i)
        steps[f"ad{i}"] = lambda i=i: added_sum(i)
        steps[f"dh{i}"] = lambda i=i: hidden_grad(i)
    for name in ORDER:
        steps[name]()

    def audio_sent(d, carry):
        audio_copy(d).wait_send()
        return carry

    lax.fori_loop(1, NT, audio_sent, 0)
    for n in range(7):
        pltpu.make_async_remote_copy(
            src_ref=rsend.at[0], dst_ref=rrecv.at[0, my_rows], send_sem=rss.at[n],
            recv_sem=rsr.at[n], device_id=mate, device_id_type=MESH,
        ).wait_send()
    for name in groups:
        need(name)
    for copy in sends:
        copy.wait_send()


def body(
    frames, value_weight, gate_weight, conv_taps, out_weight, adapter, audio_pos, text_rows,
    value_proj, queries, keys, grad_out, window_low,
):
    vm = pl.BlockSpec(memory_space=pltpu.VMEM)
    hbm = pl.BlockSpec(memory_space=pl.ANY)
    vmem = pltpu.VMEM
    dma = pltpu.SemaphoreType.DMA
    return pl.pallas_call(
        kernel,
        out_shape=(
            jax.ShapeDtypeStruct((TOK, HC), BF16),
            jax.ShapeDtypeStruct((TOK, COLS), BF16),
        ),
        in_specs=[hbm] * 6 + [vm] * 2 + [hbm] * 5,
        out_specs=(vm, vm),
        scratch_shapes=[
            vmem((NT, COLS, DH), BF16),
            vmem((DE, QUART), BF16),
            vmem((2, TOK, HC), BF16),
            vmem((2, TOK, HC), BF16),
            vmem((TOK, HC), BF16),
            vmem((8, TOK), jnp.int32),
            vmem((8, TOK), jnp.int32),
            vmem((AUD, DE), BF16),
            vmem((DE, DH), BF16),
            vmem((DE, DH), BF16),
            vmem(conv_taps.shape, F32),
            vmem((DH, DE), BF16),
            vmem((TOK, COLS), BF16),
            vmem((8, NX * AUD), jnp.int32),
            vmem((8, NT * SLOT), jnp.int32),
            vmem((AUD + 32, DE), BF16),
            vmem((AUD + 32, DH), F32),
            vmem((AUD, DE), BF16),
            vmem((NC, 16, DE), BF16),
            vmem((NX, AUD, DE), BF16),
            vmem((NX * AUD, QUART), BF16),
            vmem((NT * NX * SLOT, QUART), BF16),
            vmem((NX, NT * SLOT, QUART), BF16),
            vmem((TOK, COLS), BF16),
            vmem((2, HH, TOK, TOK), F32),
            vmem((2, HH, TOK, TOK), F32),
        ]
        + [vmem((HH, 8, TOK), F32)] * 8
        + [
            vmem((NC, TOK, HC), BF16),
            vmem((NC, HALF, HC), BF16),
            vmem((NC, HALF, HC), BF16),
            vmem((NC, HALF, HC), BF16),
            vmem((NC, HALF, HC), BF16),
            vmem((2, HALF, HC), BF16),
            vmem((3, TOK, HC), BF16),
            vmem((TOK, HC), BF16),
            vmem((COLS // 256, TOK, 256), F32),
            dma((N_SEMS,)),
            dma((N_SEMS,)),
            dma((16,)),
            dma((NT,)),
            dma((NT,)),
            dma((NC,)),
            dma((NC,)),
        ],
        compiler_params=pltpu.CompilerParams(
            collective_id=0, has_side_effects=True, vmem_limit_bytes=60 * 1024 * 1024
        ),
        cost_estimate=pl.CostEstimate(flops=13_000_000_000, bytes_accessed=8_000_000, transcendentals=4_000_000),
    )(
        frames, value_weight, gate_weight, conv_taps, out_weight, text_rows,
        window_low.reshape(1, TOK), audio_pos.reshape(NT, AUD),
        adapter, value_proj, queries, keys, grad_out,
    )


def solution(mesh):
    return jax.shard_map(
        body,
        mesh=mesh,
        in_specs=(
            P("tm", None),
            P(None, "ctx"),
            P(None, "ctx"),
            P(None, "ctx"),
            P("ctx", None),
            P("tm", "ctx"),
            P(),
            P("tm", "ctx"),
            P("ctx", "tm"),
            P(("tm", "ctx"), None),
            P(("tm", "ctx"), None),
            P(("tm", "ctx"), None),
            P("tm"),
        ),
        out_specs=(P("tm", "ctx"), P("tm", "ctx")),
        check_vma=False,
    )
```

```python
import math

import jax
import jax.numpy as jnp
from jax import lax
from jax.experimental import pallas as pl
from jax.experimental.pallas import tpu as pltpu
from jax.sharding import PartitionSpec as P

DH = 128
NORM_EPS = 1e-05
MASK_FILL = -1e30
MESH = pl.DeviceIdType.MESH
F32 = jnp.float32
BF16 = jnp.bfloat16

NT = 32
NC = 8
NX = 4
NZ = 8
TOK = 512
AUD = 128
DE = 1024
COLS = 1024
HC = 512
HH = HC // DH
HALF = TOK // 2
SLOT = 8
TILES = ((0, 0, 0, 256), (0, 256, 0, 512), (1, 0, 0, 512), (1, 256, 256, 256))
N_SEMS = 160
ROWS_A = 384
ROWS_B = COLS - ROWS_A
OFFSETS = (0, -1, 1, -2, 2, -3, 3, 4)
ORDER = (
    "issue", "b_s0", "i_k", "i_bm", "mm", "d_s0", "m0", "p0", "LN", "i_q", "conv", "b_s1",
    "d_s1", "i_ax", "p1", "r0", "pos", "hq", "b_s2", "i_g", "d_s2", "sc0", "a1_s0", "hg", "rm",
    "p2", "d_s3", "enc", "b_s3", "a0_s0", "sc1", "a1_s1", "adapt", "m1", "r1", "prob", "vgr",
    "a0_s1", "p3", "m3", "m2", "r2", "place", "t0", "t1", "t2", "rs0", "a1_s2", "t3", "a0_s2",
    "rs1", "vgf", "rs2", "t4", "ad1", "r3", "rs3", "dh3", "rs4", "dh1", "ad0", "dh2", "a1_s3",
    "ad3", "ad2", "t5", "a0_s3", "t6", "ad4", "rs5", "rs6", "t7", "ad5", "ad6", "rs7", "dh4",
    "dh0", "dh5", "ad7", "delta", "dh7", "dh6", "key",
)


def dot(a, b):
    return jnp.dot(a, b, preferred_element_type=F32)


def dot_t(a, b):
    return lax.dot_general(a, b, (((1,), (1,)), ((), ())), preferred_element_type=F32)


def iota(shape, dim):
    return lax.broadcasted_iota(jnp.int32, shape, dim)


def kernel(
    frames, vw, gw, taps, ow, text, low, aud, adapter, vp, q, k, g,
    dk_out, dh_out,
    W, AD, qs, gs, ks, low_s, lown, frames_s, vw_s, gw_s, taps_s, ow_s, text_s,
    slot_s, land_s, ext, glu_s, mixs, mixr, enc, adp, pick, inc, hid,
    e_ref, gv_ref, st_own, st_nxt, st_fp, st_fn, dl_own, dl_nxt, dl_fp, dl_fn,
    VG, psend, pown, precv, rsend, radd, rrecv, vbuf, acc,
    ssem, rsem, lsem, aus, aur, rss, rsr,
):
    t = lax.axis_index("tm")
    c = lax.axis_index("ctx")
    x = lax.rem(t, NX)
    z = lax.div(t, NX)
    core = lax.rem(c, 2)
    yy = lax.div(c, 2)
    up = (lax.rem(z + 1, NZ) * NX + x, c)
    dn = (lax.rem(z + NZ - 1, NZ) * NX + x, c)
    nxt = (lax.rem(t + 1, NT), c)
    prv = (lax.rem(t + NT - 1, NT), c)
    mate = (t, c + 1 - 2 * core)

    def ctx_peer(d):
        return (t, lax.rem(c + d, NC))

    def x_peer(d):
        return (z * NX + lax.rem(x + d, NX), c)

    def zat(d):
        return lax.rem(z + d + NZ, NZ)

    def al(v, m):
        return pl.multiple_of(v, m)

    sends = []
    groups = {}
    waited = set()

    def send(name, src, dst, dev):
        i = len(sends)
        copy = pltpu.make_async_remote_copy(
            src_ref=src, dst_ref=dst, send_sem=ssem.at[i], recv_sem=rsem.at[i],
            device_id=dev, device_id_type=MESH,
        )
        copy.start()
        sends.append(copy)
        groups.setdefault(name, []).append(copy)

    def need(*names):
        for name in names:
            if name not in waited:
                waited.add(name)
                for copy in groups[name]:
                    if name in here:
                        copy.wait()
                    else:
                        copy.wait_recv()

    here = set()

    def local(name, src, dst):
        copy = pltpu.make_async_copy(src, dst, lsem.at[len(here)])
        copy.start()
        here.add(name)
        groups[name] = [copy]

    own_rows = pl.ds(al(c * 64, 64), 64)
    own_cols = pl.ds(al(c * HC, HC), HC)
    ad_rows = pl.ds(al(t * 32, 32), 32)
    rows_a = pl.ds(0, ROWS_A)
    rows_b = pl.ds(ROWS_A, ROWS_B)

    def issue():
        bar = pltpu.get_barrier_semaphore()

        def greet(d, carry):
            pl.semaphore_signal(bar, inc=1, device_id=(lax.rem(t + d, NT), c), device_id_type=MESH)
            return carry

        lax.fori_loop(1, NT, greet, 0)
        for d in range(1, NC):
            pl.semaphore_signal(bar, inc=1, device_id=ctx_peer(d), device_id_type=MESH)
        local("frames", frames, frames_s)
        local("vw", vw, vw_s)
        local("gw", gw, gw_s)
        local("vp", vp, W.at[t])
        local("ad", adapter, AD.at[ad_rows])
        local("taps", taps, taps_s)
        local("ow", ow, ow_s)
        local("k0", k.at[:, own_cols], ks.at[own_rows])
        local("q0", q.at[:, own_cols], qs.at[0, own_rows])
        local("g0", g.at[:, own_cols], gs.at[0, own_rows])
        local("text", text, text_s)
        low_s[...] = jnp.broadcast_to(low[...], low_s.shape)
        pl.semaphore_wait(bar, NT - 1 + NC - 1)
        send("fh", frames.at[pl.ds(AUD - 16, 16)], ext.at[pl.ds(0, 16)], nxt)
        send("fh", frames.at[pl.ds(0, 16)], ext.at[pl.ds(AUD + 16, 16)], prv)
        for d in (1, 3, 2):
            send("adx", adapter, AD.at[ad_rows], x_peer(d))
        send("low", low_s, lown, prv)

    def b_ref(zz, xx=x):
        return W.at[zz * NX + xx, rows_b]

    def b_part(zz, p):
        return W.at[zz * NX + x, pl.ds(ROWS_A + ROWS_B // 2 * p, ROWS_B // 2)]

    def a_ref(zz, pair):
        return W.at[pl.ds(zz * NX + 2 * pair, 2), rows_a]

    def a_part(zz, pair, p):
        return W.at[zz * NX + 2 * pair + p, rows_a]

    def d_ref(zz):
        return AD.at[pl.ds(al(zz * 128, 128), 128)]

    def d_part(zz, p):
        return AD.at[pl.ds(al(zz * 128 + 64 * p, 64), 64)]

    def ring(name, s, ref_of, part_of):
        if s < NZ // 2 - 1:
            u, v = ref_of(zat(-s)), ref_of(zat(s))
        else:
            u, v = part_of(zat(-s), 0), part_of(zat(s), 1)
        send(f"{name}{s}", u, u, up)
        send(f"{name}{s}", v, v, dn)

    def a_step(pair, s):
        need(*([f"a{pair}_{s - 1}"] if s else ["ax", "vp"]))
        ring(f"a{pair}_", s, lambda zz: a_ref(zz, pair), lambda zz, p: a_part(zz, pair, p))

    def b_step(s):
        need(*([f"b{s - 1}"] if s else ["vp"]))
        ring("b", s, b_ref, b_part)

    def d_step(s):
        need(*([f"d{s - 1}"] if s else ["adx", "ad"]))
        ring("d", s, d_ref, d_part)

    def reached(s):
        return (0,) if s < 0 else ((-1 - s, 1 + s) if s < 3 else (4,))

    def spread(s, d, kind):
        need(f"b{s}" if s >= 0 else "vp")
        for o in reached(s):
            send(f"{kind}{s}", b_ref(zat(o)), b_ref(zat(o)), x_peer(d))

    def relay(s):
        turn = 3 if s in (-1, 3) else 1
        need(f"p{s}" if turn == 1 else f"m{s}")
        origin = lax.rem(x + NX - turn, NX)
        for o in reached(s):
            send(f"r{s}", b_ref(zat(o), origin), b_ref(zat(o), origin), x_peer(turn))

    def issue_ax():
        for d in (1, 3, 2):
            send("ax", vp.at[rows_a], W.at[t, rows_a], x_peer(d))

    def regroup(name, src, dst):
        for d in (4, 1, 7, 2, 6, 3, 5):
            peer = lax.rem(c + d, NC)
            send(name, src.at[:, pl.ds(al(peer * HC, HC), HC)], dst.at[own_rows], (t, peer))

    def positions():
        order = (iota((AUD, AUD), 0) < iota((AUD, AUD), 1)).astype(F32).astype(BF16)
        own = aud[pl.ds(t, 1), :]
        target = own // TOK
        hit = (iota((NT, AUD), 0) == target).astype(F32)
        rank = jnp.sum(dot(hit.astype(BF16), order) * hit, axis=0, keepdims=True)
        slot = target * SLOT + rank.astype(jnp.int32)
        slot_s[...] = jnp.broadcast_to(slot, slot_s.shape)
        table = aud[...]
        landing = table // TOK == t
        landing_rank = dot(landing.astype(F32).astype(BF16), order)
        spot = jnp.where(landing, table - t * TOK + 1, 0)
        n = NT * 16
        grow = (iota((n, NT), 0) // 16 == iota((n, NT), 1)).astype(F32).astype(BF16)
        spot_hi = dot(grow, (spot // 16).astype(F32).astype(BF16))
        spot_lo = dot(grow, (spot % 16).astype(F32).astype(BF16))
        ranks = dot(grow, jnp.where(landing, landing_rank, 64.0).astype(BF16))
        place = spot_hi * 16.0 + spot_lo
        r = (iota((n, AUD), 0) % 16).astype(F32)
        eye = iota((n, n), 0) == iota((n, n), 1)
        for half in range(2):
            col = jnp.sum(jnp.where(ranks == r - 8.0 * half, place, 0.0), axis=1, keepdims=True) - 1.0
            line = jnp.sum(jnp.where(eye, col, 0.0), axis=0, keepdims=True)
            land_s[half] = jnp.broadcast_to(line, (8, n)).astype(jnp.int32)

    def norm_glu():
        need("frames", "vw", "gw")
        ext[pl.ds(16, AUD), :] = frames_s[...]
        need("fh")
        rows = ext[...].astype(F32)
        centre = jnp.mean(rows, axis=1, keepdims=True)
        off = rows - centre
        spread_ = jnp.mean(off * off, axis=1, keepdims=True)
        normed = (off * lax.rsqrt(spread_ + NORM_EPS)).astype(BF16)
        value_part = dot(normed, vw_s[...])
        gate_part = dot(normed, gw_s[...])
        glu = (value_part * jax.nn.sigmoid(gate_part)).astype(BF16).astype(F32)
        row = iota(glu.shape, 0)
        first = jnp.where(t == 0, 16, 0)
        last = jnp.where(t == NT - 1, AUD + 16, AUD + 32)
        glu_s[...] = jnp.where((row >= first) & (row < last), glu, 0.0)

    def conv():
        need("taps", "ow")
        smooth = jnp.zeros((AUD, DH), F32)
        for j in range(taps_s.shape[0]):
            smooth = smooth + taps_s[pl.ds(j, 1), :] * glu_s[pl.ds(1 + j, AUD), :]
        action = (smooth * jax.nn.sigmoid(smooth)).astype(BF16)
        mixs[...] = dot(action, ow_s[...]).astype(BF16)
        for d in (4, 2, 6, 3, 5, 1, 7):
            rows_d = pl.ds(al(lax.rem(c + d, NC) * 16, 16), 16)
            send("mix", mixs.at[rows_d], mixr.at[d], ctx_peer(d))

    def encode():
        need("mix")
        mine = pl.ds(al(c * 16, 16), 16)
        total = frames_s[mine, :].astype(F32) + mixs[mine, :].astype(F32)
        for d in range(1, NC):
            total = total + mixr[d].astype(F32)
        enc[mine, :] = total.astype(BF16)
        for d in (4, 2, 6, 3, 5, 1, 7):
            send("enc", enc.at[mine], enc.at[mine], ctx_peer(d))

    def halo(name):
        part = qs if name == "q" else gs
        need(name, name + "0")
        send("h" + name, part.at[0], part.at[1], prv)

    scale = 1.0 / math.sqrt(DH)
    base = t * TOK
    row8 = iota((8, HALF), 0)

    def head_cols(h):
        return pl.ds(al(h * DH, DH), DH)

    def score_tiles(block, lows, limit, stats):
        def one_head(h, carry):
            hs = head_cols(h)
            for b, i0, j0, jn in TILES:
                if b != block:
                    continue
                qi = pl.ds(i0, HALF)
                s = dot_t(ks[pl.ds(j0, jn), hs], qs[b, qi, hs]) * scale
                jj = iota((jn, HALF), 0) + j0
                ok = jj >= lows[pl.ds(0, 1), qi] - base
                if block == 0:
                    ok = ok & (jj <= iota((jn, HALF), 1) + i0)
                else:
                    ok = ok & (jj < limit)
                s = jnp.where(ok, s, MASK_FILL)
                m = jnp.max(s, axis=0, keepdims=True)
                e = jnp.where(ok, jnp.exp(s - m), 0.0)
                n = jnp.sum(e, axis=0, keepdims=True)
                e_ref[b, h, pl.ds(j0, jn), qi] = e
                stats[h, :, qi] = jnp.where(row8 == 0, m, n)
            return carry

        lax.fori_loop(0, HH, one_head, 0)

    def score_own():
        need("k", "k0", "q", "q0")
        score_tiles(0, low_s, TOK, st_own)
        send("sta", st_own, st_fn, prv)

    def score_next():
        need("k", "k0", "hq", "low")
        score_tiles(1, lown, jnp.where(t == NT - 1, 0, TOK), st_nxt)
        send("stb", st_nxt, st_fp, nxt)

    my_slot = pl.ds(al(t * 16, 16), 16)

    def audio_copy(d):
        peer = lax.rem(t + d, NT)
        return pltpu.make_async_remote_copy(
            src_ref=pick.at[pl.ds(al(peer * 16, 16), 16)], dst_ref=inc.at[my_slot],
            send_sem=aus.at[d], recv_sem=aur.at[d], device_id=(peer, c), device_id_type=MESH,
        )

    def adapt():
        need("d3", "enc")
        for n in range(4):
            cols = pl.ds(256 * n, 256)
            adp[:, cols] = dot(enc[...], AD[:, cols]).astype(BF16)
        slot_row = iota((NT * 16, AUD), 0)
        picker = ((slot_row // 16) * SLOT + slot_row % SLOT == slot_s[pl.ds(0, 1), :]).astype(F32)
        picker = picker.astype(BF16)
        low_half = dot(picker, adp[:, pl.ds(0, 512)])
        high_half = dot(picker, adp[:, pl.ds(512, 512)])
        upper = iota((NT * 16, 512), 0) % 16 < SLOT
        pick[...] = jnp.where(upper, low_half, high_half).astype(BF16)

        def audio_start(d, carry):
            audio_copy(d).start()
            return carry

        lax.fori_loop(1, NT, audio_start, 0)
        inc[my_slot, :] = pick[my_slot, :]

    def factor(mine_st, other_st, h):
        m1, s1 = mine_st[h, pl.ds(0, 1), :], mine_st[h, pl.ds(1, 1), :]
        m2, s2 = other_st[h, pl.ds(0, 1), :], other_st[h, pl.ds(1, 1), :]
        m = jnp.maximum(m1, m2)
        a1 = jnp.exp(m1 - m)
        return a1 / (s1 * a1 + s2 * jnp.exp(m2 - m))

    def gather_terms(tiles, other, h):
        hs = head_cols(h)
        first, second = pl.ds(0, 256), pl.ds(256, 256)
        top = dot(tiles[0], other[0, first, hs]) + dot(tiles[1][:256], other[0, second, hs])
        top = top + dot(tiles[2][:256], other[1, first, hs])
        bottom = dot(tiles[1][256:], other[0, second, hs])
        bottom = bottom + dot(tiles[2][256:], other[1, first, hs])
        bottom = bottom + dot(tiles[3], other[1, second, hs])
        return top, bottom

    def prob():
        need("sta", "stb", "g", "g0", "hg")

        def prob_head(h, carry):
            f = (factor(st_own, st_fp, h), factor(st_nxt, st_fn, h))
            tiles = []
            for b, i0, j0, jn in TILES:
                p = e_ref[b, h, pl.ds(j0, jn), pl.ds(i0, HALF)] * f[b][:, i0 : i0 + HALF]
                e_ref[b, h, pl.ds(j0, jn), pl.ds(i0, HALF)] = p
                tiles.append(p.astype(BF16))
            top, bottom = gather_terms(tiles, gs, h)
            hs = head_cols(h)
            VG[c, pl.ds(0, 256), hs] = top.astype(BF16)
            VG[c, pl.ds(256, 256), hs] = bottom.astype(BF16)
            return carry

        lax.fori_loop(0, HH, prob_head, 0)
        send("vg1", VG.at[c], VG.at[c], ctx_peer(2))
        send("vg3", VG.at[c], VG.at[c], ctx_peer(6))
        send("vgc", VG.at[c], VG.at[c], mate)

    below, above, across = [lax.rem(c + d, NC) for d in (6, 2, 4)]

    def vg_relay():
        need("vg1", "vg3")
        one, two = VG.at[below, pl.ds(0, 256)], VG.at[above, pl.ds(256, 256)]
        send("vg2", one, one, ctx_peer(2))
        send("vg2", two, two, ctx_peer(6))
        send("vgc", VG.at[below], VG.at[below], mate)
        send("vgc", VG.at[above], VG.at[above], mate)

    def vg_last():
        need("vg2")
        send("vgc", VG.at[across], VG.at[across], mate)

    def place():
        need("text")

        def audio_arrived(d, carry):
            audio_copy(d).wait_recv()
            return carry

        lax.fori_loop(1, NT, audio_arrived, 0)
        for half in range(2):
            cols = pl.ds(512 * half, 512)
            hits = (iota((TOK, NT * 16), 0) == land_s[half, pl.ds(0, 1), :]).astype(F32)
            there = jnp.sum(hits, axis=1, keepdims=True) > 0.5
            rows_in = dot(hits.astype(BF16), inc[...])
            hid[:, cols] = jnp.where(there, rows_in, text_s[:, cols].astype(F32)).astype(BF16)

    mate_rows = pl.ds(al((1 - core) * HALF, HALF), HALF)
    my_rows = pl.ds(al(core * HALF, HALF), HALF)

    def weights_ready(i):
        s = (i - 1) // 2
        need(f"m{s}", f"p{s}", f"r{s}")
        need(*([f"a0_{s}", f"a1_{s}", f"b{s}"] if i else ["ax", "vp"]))

    def terms(i):
        weights_ready(i)
        cp = zat(OFFSETS[i])
        w = jnp.concatenate([W[cp * HH + j] for j in range(HH)], axis=1)
        psend[i] = dot(hid[mate_rows, :], w).astype(BF16)
        send(f"pair{i}", psend.at[i], precv.at[i], mate)
        w = jnp.concatenate([W[cp * HH + j] for j in range(HH)], axis=1)
        pown[i] = dot(hid[my_rows, :], w).astype(BF16)

    def owner_copy(side, kd, i):
        owner = lax.rem(yy + 1 + 2 * side, NC // 2) * 2 + kd
        return pltpu.make_async_remote_copy(
            src_ref=rsend.at[i], dst_ref=rrecv.at[1 + side, my_rows],
            send_sem=rss.at[2 * side + kd], recv_sem=rsr.at[2 * side + core],
            device_id=(t, owner), device_id_type=MESH,
        )

    def add_copy(kd, i):
        return pltpu.make_async_remote_copy(
            src_ref=rsend.at[i], dst_ref=radd.at[kd],
            send_sem=rss.at[4 + kd], recv_sem=rsr.at[4 + kd],
            device_id=(t, lax.rem(c + 2 + 4 * core, NC)), device_id_type=MESH,
        )

    def mate_copy(i):
        return pltpu.make_async_remote_copy(
            src_ref=rsend.at[i], dst_ref=rrecv.at[0, my_rows],
            send_sem=rss.at[6], recv_sem=rsr.at[6], device_id=mate, device_id_type=MESH,
        )

    def owner_of(i):
        cp = zat(OFFSETS[i])
        return lax.rem(lax.div(cp, 2) - yy + NC // 2, NC // 2), lax.rem(cp, 2)

    def chip_sum(i):
        e, kd = owner_of(i)
        need(f"pair{i}")
        total = pown[i].astype(F32) + precv[i].astype(F32)
        rsend[i] = total.astype(BF16)

        @pl.when(e == 2)
        def _():
            add_copy(kd, i).start()

        @pl.when(e == 3 - 2 * core)
        def _():
            owner_copy(lax.div(e, 2), kd, i).start()

        @pl.when((e == 0) & (kd != core))
        def _():
            mate_copy(i).start()

        @pl.when((e == 0) & (kd == core))
        def _():
            rrecv[0, my_rows, :] = rsend[i]

    def added_sum(i):
        e, kd = owner_of(i)

        @pl.when(e == 1 + 2 * core)
        def _():
            add_copy(kd, i).wait_recv()
            total = rsend[i].astype(F32) + radd[kd].astype(F32)
            rsend[i] = total.astype(BF16)
            owner_copy(lax.div(e, 2), kd, i).start()

    added = []

    def hidden_grad(i):
        weights_ready(i)
        need("vgc")
        cp = zat(OFFSETS[i])
        added.append(i)
        first, last = len(added) == 1, len(added) == NC

        def part(n, carry):
            rows_n = pl.ds(al(n * 256, 256), 256)
            w = jnp.concatenate([W[cp * HH + j, rows_n, :] for j in range(HH)], axis=1)
            term = dot_t(VG[cp], w)
            if not first:
                term = term + acc[n]
            if last:
                dh_out[:, rows_n] = term.astype(BF16)
            else:
                acc[n] = term
            return carry

        lax.fori_loop(0, COLS // 256, part, 0)

    def delta():
        for n in (0, 1, 2, 3, 6):
            pltpu.make_async_remote_copy(
                src_ref=rsend.at[0], dst_ref=rrecv.at[0, my_rows], send_sem=rss.at[n],
                recv_sem=rsr.at[n], device_id=mate, device_id_type=MESH,
            ).wait_recv()
        total = rrecv[0].astype(F32) + rrecv[1].astype(F32) + rrecv[2].astype(F32)
        vbuf[...] = total.astype(BF16)

        def delta_head(h, carry):
            hs = head_cols(h)
            for b, i0, j0, jn in TILES:
                qi = pl.ds(i0, HALF)
                gv = dot_t(vbuf[pl.ds(j0, jn), hs], gs[b, qi, hs])
                gv_ref[b, h, pl.ds(j0, jn), qi] = gv
                w = e_ref[b, h, pl.ds(j0, jn), qi].astype(BF16).astype(F32)
                part = jnp.sum(w * gv, axis=0, keepdims=True)
                table = dl_own if b == 0 else dl_nxt
                table[h, :, qi] = jnp.where(row8 == 0, part, 0.0)
            return carry

        lax.fori_loop(0, HH, delta_head, 0)
        send("dl", dl_own, dl_fn, prv)
        send("dl", dl_nxt, dl_fp, nxt)

    def key():
        need("dl")

        def key_head(h, carry):
            deltas = (
                dl_own[h, pl.ds(0, 1), :] + dl_fp[h, pl.ds(0, 1), :],
                dl_nxt[h, pl.ds(0, 1), :] + dl_fn[h, pl.ds(0, 1), :],
            )
            tiles = []
            for b, i0, j0, jn in TILES:
                qi = pl.ds(i0, HALF)
                p = e_ref[b, h, pl.ds(j0, jn), qi]
                gv = gv_ref[b, h, pl.ds(j0, jn), qi]
                tiles.append((p * (gv - deltas[b][:, i0 : i0 + HALF])).astype(BF16))
            top, bottom = gather_terms(tiles, qs, h)
            hs = head_cols(h)
            dk_out[pl.ds(0, 256), hs] = (top * scale).astype(BF16)
            dk_out[pl.ds(256, 256), hs] = (bottom * scale).astype(BF16)
            return carry

        lax.fori_loop(0, HH, key_head, 0)

    steps = {
        "issue": issue, "i_ax": issue_ax,
        "i_bm": lambda: spread(-1, 1, "p"), "mm": lambda: spread(-1, 3, "m"),
        "i_k": lambda: regroup("k", k, ks),
        "i_q": lambda: regroup("q", q, qs.at[0]),
        "i_g": lambda: regroup("g", g, gs.at[0]),
        "pos": positions, "LN": norm_glu, "conv": conv, "enc": encode, "adapt": adapt, "place": place,
        "hq": lambda: halo("q"), "hg": lambda: halo("g"),
        "sc0": score_own, "sc1": score_next, "prob": prob, "vgr": vg_relay, "vgf": vg_last,
        "rm": lambda: relay(-1), "delta": delta, "key": key,
    }
    for s in range(4):
        steps[f"a0_s{s}"] = lambda s=s: a_step(0, s)
        steps[f"a1_s{s}"] = lambda s=s: a_step(1, s)
        steps[f"b_s{s}"] = lambda s=s: b_step(s)
        steps[f"d_s{s}"] = lambda s=s: d_step(s)
        steps[f"p{s}"] = lambda s=s: spread(s, 1, "p")
        steps[f"m{s}"] = lambda s=s: spread(s, 3, "m")
        steps[f"r{s}"] = lambda s=s: relay(s)
    for i in range(NC):
        steps[f"t{i}"] = lambda i=i: terms(i)
        steps[f"rs{i}"] = lambda i=i: chip_sum(i)
        steps[f"ad{i}"] = lambda i=i: added_sum(i)
        steps[f"dh{i}"] = lambda i=i: hidden_grad(i)
    for name in ORDER:
        steps[name]()

    def audio_sent(d, carry):
        audio_copy(d).wait_send()
        return carry

    lax.fori_loop(1, NT, audio_sent, 0)
    for n in range(7):
        pltpu.make_async_remote_copy(
            src_ref=rsend.at[0], dst_ref=rrecv.at[0, my_rows], send_sem=rss.at[n],
            recv_sem=rsr.at[n], device_id=mate, device_id_type=MESH,
        ).wait_send()
    for name in groups:
        need(name)
    for copy in sends:
        copy.wait_send()


def body(
    frames, value_weight, gate_weight, conv_taps, out_weight, adapter, audio_pos, text_rows,
    value_proj, queries, keys, grad_out, window_low,
):
    vm = pl.BlockSpec(memory_space=pltpu.VMEM)
    hbm = pl.BlockSpec(memory_space=pl.ANY)
    vmem = pltpu.VMEM
    dma = pltpu.SemaphoreType.DMA
    return pl.pallas_call(
        kernel,
        out_shape=(
            jax.ShapeDtypeStruct((TOK, HC), BF16),
            jax.ShapeDtypeStruct((TOK, COLS), BF16),
        ),
        in_specs=[hbm] * 6 + [vm] * 2 + [hbm] * 5,
        out_specs=(vm, vm),
        scratch_shapes=[
            vmem((NT, COLS, DH), BF16),
            vmem((DE, COLS), BF16),
            vmem((2, TOK, HC), BF16),
            vmem((2, TOK, HC), BF16),
            vmem((TOK, HC), BF16),
            vmem((8, TOK), jnp.int32),
            vmem((8, TOK), jnp.int32),
            vmem((AUD, DE), BF16),
            vmem((DE, DH), BF16),
            vmem((DE, DH), BF16),
            vmem(conv_taps.shape, F32),
            vmem((DH, DE), BF16),
            vmem((TOK, COLS), BF16),
            vmem((8, AUD), jnp.int32),
            vmem((2, 8, NT * 16), jnp.int32),
            vmem((AUD + 32, DE), BF16),
            vmem((AUD + 32, DH), F32),
            vmem((AUD, DE), BF16),
            vmem((NC, 16, DE), BF16),
            vmem((AUD, DE), BF16),
            vmem((AUD, COLS), BF16),
            vmem((NT * 16, 512), BF16),
            vmem((NT * 16, 512), BF16),
            vmem((TOK, COLS), BF16),
            vmem((2, HH, TOK, TOK), F32),
            vmem((2, HH, TOK, TOK), F32),
        ]
        + [vmem((HH, 8, TOK), F32)] * 8
        + [
            vmem((NC, TOK, HC), BF16),
            vmem((NC, HALF, HC), BF16),
            vmem((NC, HALF, HC), BF16),
            vmem((NC, HALF, HC), BF16),
            vmem((NC, HALF, HC), BF16),
            vmem((2, HALF, HC), BF16),
            vmem((3, TOK, HC), BF16),
            vmem((TOK, HC), BF16),
            vmem((COLS // 256, TOK, 256), F32),
            dma((N_SEMS,)),
            dma((N_SEMS,)),
            dma((16,)),
            dma((NT,)),
            dma((NT,)),
            dma((NC,)),
            dma((NC,)),
        ],
        compiler_params=pltpu.CompilerParams(
            collective_id=0, has_side_effects=True, vmem_limit_bytes=60 * 1024 * 1024
        ),
        cost_estimate=pl.CostEstimate(flops=13_000_000_000, bytes_accessed=8_000_000, transcendentals=4_000_000),
    )(
        frames, value_weight, gate_weight, conv_taps, out_weight, text_rows,
        window_low.reshape(1, TOK), audio_pos.reshape(NT, AUD),
        adapter, value_proj, queries, keys, grad_out,
    )


def solution(mesh):
    return jax.shard_map(
        body,
        mesh=mesh,
        in_specs=(
            P("tm", None),
            P(None, "ctx"),
            P(None, "ctx"),
            P(None, "ctx"),
            P("ctx", None),
            P("tm", "ctx"),
            P(),
            P("tm", "ctx"),
            P("ctx", "tm"),
            P(("tm", "ctx"), None),
            P(("tm", "ctx"), None),
            P(("tm", "ctx"), None),
            P("tm"),
        ),
        out_specs=(P("tm", "ctx"), P("tm", "ctx")),
        check_vma=False,
    )
```

```python
import math

import jax
import jax.numpy as jnp
from jax import lax
from jax.experimental import pallas as pl
from jax.experimental.pallas import tpu as pltpu
from jax.sharding import PartitionSpec as P

DH = 128
NORM_EPS = 1e-05
MASK_FILL = -1e30
MESH = pl.DeviceIdType.MESH
F32 = jnp.float32
BF16 = jnp.bfloat16

NT = 32
NC = 8
NX = 4
NZ = 8
TOK = 512
AUD = 128
DE = 1024
COLS = 1024
HC = 512
HH = HC // DH
HALF = TOK // 2
SLOT = 8
TILES = ((0, 0, 0, 256), (0, 256, 0, 512), (1, 0, 0, 512), (1, 256, 256, 256))
N_SEMS = 176
QUART = COLS // NX
ROWS_A = 512
ROWS_B = COLS - ROWS_A
OFFSETS = (0, -1, 1, -2, 2, -3, 3, 4)
ORDER = (
    "issue", "i_q", "i_ax", "hq", "b_s0", "d_s0", "hg", "b_s1", "p0", "LN", "conv", "a0_s0",
    "d_s1", "pos", "r0", "enc", "d_s2", "a1_s0", "d_s3", "i_bm", "i_k", "encx", "a0_s1", "i_g",
    "b_s2", "er", "a0_s2", "p1", "sc0", "a1_s1", "sc1", "m2", "adapt", "mm", "m0", "p2", "prob",
    "rm", "m1", "b_s3", "r1", "vgr", "a1_s2", "place", "t0", "m3", "t1", "r2", "t2", "rs0",
    "t3", "rs1", "t4", "vgf", "r3", "rs2", "a1_s3", "p3", "rs3", "rs4", "a0_s3", "ad0", "t5",
    "t6", "ad3", "dh0", "ad1", "ad4", "dh1", "ad2", "rs5", "dh3", "rs6", "t7", "dh4", "dh6",
    "ad5", "ad6", "rs7", "dh5", "ad7", "dh2", "dh7", "delta", "key",
)


def dot(a, b):
    return jnp.dot(a, b, preferred_element_type=F32)


def dot_t(a, b):
    return lax.dot_general(a, b, (((1,), (1,)), ((), ())), preferred_element_type=F32)


def iota(shape, dim):
    return lax.broadcasted_iota(jnp.int32, shape, dim)


def kernel(
    frames, vw, gw, taps, ow, text, low, aud, adapter, vp, q, k, g,
    dk_out, dh_out,
    W, AD, qs, gs, ks, low_s, lown, frames_s, vw_s, gw_s, taps_s, ow_s, text_s,
    slot_s, land_s, ext, glu_s, mixs, mixr, enc, adp, pick, inc, hid,
    e_ref, gv_ref, st_own, st_nxt, st_fp, st_fn, dl_own, dl_nxt, dl_fp, dl_fn,
    VG, psend, pown, precv, rsend, radd, rrecv, vbuf, acc,
    ssem, rsem, lsem, aus, aur, rss, rsr,
):
    t = lax.axis_index("tm")
    c = lax.axis_index("ctx")
    x = lax.rem(t, NX)
    z = lax.div(t, NX)
    core = lax.rem(c, 2)
    yy = lax.div(c, 2)
    up = (lax.rem(z + 1, NZ) * NX + x, c)
    dn = (lax.rem(z + NZ - 1, NZ) * NX + x, c)
    nxt = (lax.rem(t + 1, NT), c)
    prv = (lax.rem(t + NT - 1, NT), c)
    mate = (t, c + 1 - 2 * core)

    def ctx_peer(d):
        return (t, lax.rem(c + d, NC))

    def x_peer(d):
        return (z * NX + lax.rem(x + d, NX), c)

    def zat(d):
        return lax.rem(z + d + NZ, NZ)

    def al(v, m):
        return pl.multiple_of(v, m)

    sends = []
    groups = {}
    waited = set()

    def send(name, src, dst, dev):
        i = len(sends)
        copy = pltpu.make_async_remote_copy(
            src_ref=src, dst_ref=dst, send_sem=ssem.at[i], recv_sem=rsem.at[i],
            device_id=dev, device_id_type=MESH,
        )
        copy.start()
        sends.append(copy)
        groups.setdefault(name, []).append(copy)

    def need(*names):
        for name in names:
            if name not in waited:
                waited.add(name)
                for copy in groups[name]:
                    if name in here:
                        copy.wait()
                    else:
                        copy.wait_recv()

    here = set()

    def local(name, src, dst):
        copy = pltpu.make_async_copy(src, dst, lsem.at[len(here)])
        copy.start()
        here.add(name)
        groups[name] = [copy]

    own_rows = pl.ds(al(c * 64, 64), 64)
    own_cols = pl.ds(al(c * HC, HC), HC)
    ad_rows = pl.ds(al(t * 32, 32), 32)
    rows_a = pl.ds(0, ROWS_A)
    rows_b = pl.ds(ROWS_A, ROWS_B)

    def issue():
        bar = pltpu.get_barrier_semaphore()

        def greet(d, carry):
            pl.semaphore_signal(bar, inc=1, device_id=(lax.rem(t + d, NT), c), device_id_type=MESH)
            return carry

        lax.fori_loop(1, NT, greet, 0)
        for d in range(1, NC):
            pl.semaphore_signal(bar, inc=1, device_id=ctx_peer(d), device_id_type=MESH)
            for beside in (lax.rem(t + 1, NT), lax.rem(t + NT - 1, NT)):
                peer = (beside, lax.rem(c + d, NC))
                pl.semaphore_signal(bar, inc=1, device_id=peer, device_id_type=MESH)
        local("frames", frames, frames_s)
        local("vw", vw, vw_s)
        local("gw", gw, gw_s)
        local("vp", vp, W.at[t])
        local("ad", adapter.at[:, pl.ds(al(x * QUART, QUART), QUART)], AD.at[ad_rows])
        local("taps", taps, taps_s)
        local("ow", ow, ow_s)
        local("k0", k.at[:, own_cols], ks.at[own_rows])
        local("q0", q.at[:, own_cols], qs.at[0, own_rows])
        local("g0", g.at[:, own_cols], gs.at[0, own_rows])
        local("text", text, text_s)
        low_s[...] = jnp.broadcast_to(low[...], low_s.shape)
        pl.semaphore_wait(bar, NT - 1 + 3 * (NC - 1))
        send("fh", frames.at[pl.ds(AUD - 16, 16)], ext.at[pl.ds(0, 16)], nxt)
        send("fh", frames.at[pl.ds(0, 16)], ext.at[pl.ds(AUD + 16, 16)], prv)
        for d in (1, 3, 2):
            quarter = pl.ds(al(lax.rem(x + d, NX) * QUART, QUART), QUART)
            send("adx", adapter.at[:, quarter], AD.at[ad_rows], x_peer(d))
        send("low", low_s, lown, prv)

    def b_ref(zz, xx=x):
        return W.at[zz * NX + xx, rows_b]

    def b_part(zz, p):
        return W.at[zz * NX + x, pl.ds(ROWS_A + ROWS_B // 2 * p, ROWS_B // 2)]

    def a_ref(zz, pair):
        return W.at[pl.ds(zz * NX + 2 * pair, 2), rows_a]

    def a_part(zz, pair, p):
        return W.at[zz * NX + 2 * pair + p, rows_a]

    def d_ref(zz):
        return AD.at[pl.ds(al(zz * 128, 128), 128)]

    def d_part(zz, p):
        return AD.at[pl.ds(al(zz * 128 + 64 * p, 64), 64)]

    def ring(name, s, ref_of, part_of):
        if s < NZ // 2 - 1:
            u, v = ref_of(zat(-s)), ref_of(zat(s))
        else:
            u, v = part_of(zat(-s), 0), part_of(zat(s), 1)
        send(f"{name}{s}", u, u, up)
        send(f"{name}{s}", v, v, dn)

    def a_step(pair, s):
        need(*([f"a{pair}_{s - 1}"] if s else ["ax", "vp"]))
        ring(f"a{pair}_", s, lambda zz: a_ref(zz, pair), lambda zz, p: a_part(zz, pair, p))

    def b_step(s):
        need(*([f"b{s - 1}"] if s else ["vp"]))
        ring("b", s, b_ref, b_part)

    def d_step(s):
        need(*([f"d{s - 1}"] if s else ["adx", "ad"]))
        ring("d", s, d_ref, d_part)

    def reached(s):
        return (0,) if s < 0 else ((-1 - s, 1 + s) if s < 3 else (4,))

    def spread(s, d, kind):
        need(f"b{s}" if s >= 0 else "vp")
        for o in reached(s):
            send(f"{kind}{s}", b_ref(zat(o)), b_ref(zat(o)), x_peer(d))

    def relay(s):
        turn = 3 if s in (-1, 3) else 1
        need(f"p{s}" if turn == 1 else f"m{s}")
        origin = lax.rem(x + NX - turn, NX)
        for o in reached(s):
            send(f"r{s}", b_ref(zat(o), origin), b_ref(zat(o), origin), x_peer(turn))

    def issue_ax():
        for d in (1, 3, 2):
            send("ax", vp.at[rows_a], W.at[t, rows_a], x_peer(d))

    def regroup(name, src, dst):
        for d in (4, 1, 7, 2, 6, 3, 5):
            peer = lax.rem(c + d, NC)
            send(name, src.at[:, pl.ds(al(peer * HC, HC), HC)], dst.at[own_rows], (t, peer))

    def positions():
        order = (iota((AUD, AUD), 0) < iota((AUD, AUD), 1)).astype(F32).astype(BF16)
        for b in range(NX):
            target = aud[pl.ds(z * NX + b, 1), :] // TOK
            hit = (iota((NT, AUD), 0) == target).astype(F32)
            rank = jnp.sum(dot(hit.astype(BF16), order) * hit, axis=0, keepdims=True)
            slot = target * (NX * SLOT) + b * SLOT + rank.astype(jnp.int32)
            slot_s[:, pl.ds(b * AUD, AUD)] = jnp.broadcast_to(slot, (8, AUD))
        table = aud[...]
        landing = table // TOK == t
        landing_rank = dot(landing.astype(F32).astype(BF16), order)
        spot = jnp.where(landing, table - t * TOK + 1, 0)
        n = NT * SLOT
        grow = (iota((n, NT), 0) // SLOT == iota((n, NT), 1)).astype(F32).astype(BF16)
        spot_hi = dot(grow, (spot // 16).astype(F32).astype(BF16))
        spot_lo = dot(grow, (spot % 16).astype(F32).astype(BF16))
        ranks = dot(grow, jnp.where(landing, landing_rank, 64.0).astype(BF16))
        spots = spot_hi * 16.0 + spot_lo
        r = (iota((n, AUD), 0) % SLOT).astype(F32)
        col = jnp.sum(jnp.where(ranks == r, spots, 0.0), axis=1, keepdims=True) - 1.0
        eye = iota((n, n), 0) == iota((n, n), 1)
        line = jnp.sum(jnp.where(eye, col, 0.0), axis=0, keepdims=True)
        land_s[...] = jnp.broadcast_to(line, (8, n)).astype(jnp.int32)

    def norm_glu():
        need("frames", "vw", "gw")
        ext[pl.ds(16, AUD), :] = frames_s[...]
        need("fh")
        rows = ext[...].astype(F32)
        centre = jnp.mean(rows, axis=1, keepdims=True)
        off = rows - centre
        spread_ = jnp.mean(off * off, axis=1, keepdims=True)
        normed = (off * lax.rsqrt(spread_ + NORM_EPS)).astype(BF16)
        value_part = dot(normed, vw_s[...])
        gate_part = dot(normed, gw_s[...])
        glu = (value_part * jax.nn.sigmoid(gate_part)).astype(BF16).astype(F32)
        row = iota(glu.shape, 0)
        first = jnp.where(t == 0, 16, 0)
        last = jnp.where(t == NT - 1, AUD + 16, AUD + 32)
        glu_s[...] = jnp.where((row >= first) & (row < last), glu, 0.0)

    def conv():
        need("taps", "ow")
        smooth = jnp.zeros((AUD, DH), F32)
        for j in range(taps_s.shape[0]):
            smooth = smooth + taps_s[pl.ds(j, 1), :] * glu_s[pl.ds(1 + j, AUD), :]
        action = (smooth * jax.nn.sigmoid(smooth)).astype(BF16)
        mixs[...] = dot(action, ow_s[...]).astype(BF16)
        for d in (4, 2, 6, 3, 5, 1, 7):
            rows_d = pl.ds(al(lax.rem(c + d, NC) * 16, 16), 16)
            send("mix", mixs.at[rows_d], mixr.at[d], ctx_peer(d))

    def encode():
        need("mix")
        mine = pl.ds(al(c * 16, 16), 16)
        total = frames_s[mine, :].astype(F32) + mixs[mine, :].astype(F32)
        for d in range(1, NC):
            total = total + mixr[d].astype(F32)
        enc[x, mine, :] = total.astype(BF16)
        for d in (4, 2, 6, 3, 5, 1, 7):
            send("enc", enc.at[x, mine], enc.at[x, mine], ctx_peer(d))

    def encode_x():
        need("enc")
        for d in (1, 3):
            send("ex", enc.at[x], enc.at[x], x_peer(d))

    def encode_relay():
        need("ex")
        for d, at in ((1, 0), (3, AUD // 2)):
            part = enc.at[lax.rem(x + NX - d, NX), pl.ds(at, AUD // 2)]
            send("ex2", part, part, x_peer(d))

    def halo(name, src, dst):
        before = lax.rem(t + NT - 1, NT)
        for d in (4, 1, 7, 2, 6, 3, 5, 0):
            peer = lax.rem(c + d, NC)
            send("h" + name, src.at[:, pl.ds(al(peer * HC, HC), HC)], dst.at[own_rows], (before, peer))

    scale = 1.0 / math.sqrt(DH)
    base = t * TOK
    row8 = iota((8, HALF), 0)

    def head_cols(h):
        return pl.ds(al(h * DH, DH), DH)

    def score_tiles(block, lows, limit, stats):
        def one_head(h, carry):
            hs = head_cols(h)
            for b, i0, j0, jn in TILES:
                if b != block:
                    continue
                qi = pl.ds(i0, HALF)
                s = dot_t(ks[pl.ds(j0, jn), hs], qs[b, qi, hs]) * scale
                jj = iota((jn, HALF), 0) + j0
                ok = jj >= lows[pl.ds(0, 1), qi] - base
                if block == 0:
                    ok = ok & (jj <= iota((jn, HALF), 1) + i0)
                else:
                    ok = ok & (jj < limit)
                s = jnp.where(ok, s, MASK_FILL)
                m = jnp.max(s, axis=0, keepdims=True)
                e = jnp.where(ok, jnp.exp(s - m), 0.0)
                n = jnp.sum(e, axis=0, keepdims=True)
                e_ref[b, h, pl.ds(j0, jn), qi] = e
                stats[h, :, qi] = jnp.where(row8 == 0, m, n)
            return carry

        lax.fori_loop(0, HH, one_head, 0)

    def score_own():
        need("k", "k0", "q", "q0")
        score_tiles(0, low_s, TOK, st_own)
        send("sta", st_own, st_fn, prv)

    def score_next():
        need("k", "k0", "hq", "low")
        score_tiles(1, lown, jnp.where(t == NT - 1, 0, TOK), st_nxt)
        send("stb", st_nxt, st_fp, nxt)

    group_rows = NX * SLOT
    my_slot = pl.ds(al(z * group_rows, group_rows), group_rows)

    def slot_rows(tm):
        return pl.ds(al(tm * group_rows, group_rows), group_rows)

    def audio_copy(d):
        peer = lax.rem(t + d, NT)
        return pltpu.make_async_remote_copy(
            src_ref=pick.at[slot_rows(peer)], dst_ref=inc.at[x, my_slot],
            send_sem=aus.at[d], recv_sem=aur.at[d], device_id=(peer, c), device_id_type=MESH,
        )

    def adapt():
        need("d3", "ex", "ex2")
        adp[...] = dot(enc[...].reshape(NX * AUD, DE), AD[...]).astype(BF16)
        for n in range(4):
            slot_row = iota((256, NX * AUD), 0) + 256 * n
            picker = (slot_row == slot_s[pl.ds(0, 1), :]).astype(F32).astype(BF16)
            pick[pl.ds(256 * n, 256), :] = dot(picker, adp[...]).astype(BF16)

        def audio_start(d, carry):
            audio_copy(d).start()
            return carry

        lax.fori_loop(1, NT, audio_start, 0)
        inc[x, my_slot, :] = pick[slot_rows(t), :]

    def factor(mine_st, other_st, h):
        m1, s1 = mine_st[h, pl.ds(0, 1), :], mine_st[h, pl.ds(1, 1), :]
        m2, s2 = other_st[h, pl.ds(0, 1), :], other_st[h, pl.ds(1, 1), :]
        m = jnp.maximum(m1, m2)
        a1 = jnp.exp(m1 - m)
        return a1 / (s1 * a1 + s2 * jnp.exp(m2 - m))

    def gather_terms(tiles, other, h):
        hs = head_cols(h)
        first, second = pl.ds(0, 256), pl.ds(256, 256)
        top = dot(tiles[0], other[0, first, hs]) + dot(tiles[1][:256], other[0, second, hs])
        top = top + dot(tiles[2][:256], other[1, first, hs])
        bottom = dot(tiles[1][256:], other[0, second, hs])
        bottom = bottom + dot(tiles[2][256:], other[1, first, hs])
        bottom = bottom + dot(tiles[3], other[1, second, hs])
        return top, bottom

    def prob():
        need("sta", "stb", "g", "g0", "hg")

        def prob_head(h, carry):
            f = (factor(st_own, st_fp, h), factor(st_nxt, st_fn, h))
            tiles = []
            for b, i0, j0, jn in TILES:
                p = e_ref[b, h, pl.ds(j0, jn), pl.ds(i0, HALF)] * f[b][:, i0 : i0 + HALF]
                e_ref[b, h, pl.ds(j0, jn), pl.ds(i0, HALF)] = p
                tiles.append(p.astype(BF16))
            top, bottom = gather_terms(tiles, gs, h)
            hs = head_cols(h)
            VG[c, pl.ds(0, 256), hs] = top.astype(BF16)
            VG[c, pl.ds(256, 256), hs] = bottom.astype(BF16)
            return carry

        lax.fori_loop(0, HH, prob_head, 0)
        send("vg1", VG.at[c], VG.at[c], ctx_peer(2))
        send("vg3", VG.at[c], VG.at[c], ctx_peer(6))
        send("vgc", VG.at[c], VG.at[c], mate)

    below, above, across = [lax.rem(c + d, NC) for d in (6, 2, 4)]

    def vg_relay():
        need("vg1", "vg3")
        one, two = VG.at[below, pl.ds(0, 256)], VG.at[above, pl.ds(256, 256)]
        send("vg2", one, one, ctx_peer(2))
        send("vg2", two, two, ctx_peer(6))
        send("vgc", VG.at[below], VG.at[below], mate)
        send("vgc", VG.at[above], VG.at[above], mate)

    def vg_last():
        need("vg2")
        send("vgc", VG.at[across], VG.at[across], mate)

    def place():
        need("text")

        def audio_arrived(d, carry):
            audio_copy(d).wait_recv()
            return carry

        lax.fori_loop(1, NT, audio_arrived, 0)
        hits = (iota((TOK, NT * SLOT), 0) == land_s[pl.ds(0, 1), :]).astype(F32)
        there = jnp.sum(hits, axis=1, keepdims=True) > 0.5
        hits = hits.astype(BF16)
        for n in range(NX):
            cols = pl.ds(QUART * n, QUART)
            rows_in = dot(hits, inc[n])
            hid[:, cols] = jnp.where(there, rows_in, text_s[:, cols].astype(F32)).astype(BF16)

    mate_rows = pl.ds(al((1 - core) * HALF, HALF), HALF)
    my_rows = pl.ds(al(core * HALF, HALF), HALF)

    def weights_ready(i):
        s = (i - 1) // 2
        need(f"m{s}", f"p{s}", f"r{s}")
        need(*([f"a0_{s}", f"a1_{s}", f"b{s}"] if i else ["ax", "vp"]))

    def terms(i):
        weights_ready(i)
        cp = zat(OFFSETS[i])
        w = jnp.concatenate([W[cp * HH + j] for j in range(HH)], axis=1)
        psend[i] = dot(hid[mate_rows, :], w).astype(BF16)
        send(f"pair{i}", psend.at[i], precv.at[i], mate)
        w = jnp.concatenate([W[cp * HH + j] for j in range(HH)], axis=1)
        pown[i] = dot(hid[my_rows, :], w).astype(BF16)

    def owner_copy(side, kd, i):
        owner = lax.rem(yy + 1 + 2 * side, NC // 2) * 2 + kd
        return pltpu.make_async_remote_copy(
            src_ref=rsend.at[i], dst_ref=rrecv.at[1 + side, my_rows],
            send_sem=rss.at[2 * side + kd], recv_sem=rsr.at[2 * side + core],
            device_id=(t, owner), device_id_type=MESH,
        )

    def add_copy(kd, i):
        return pltpu.make_async_remote_copy(
            src_ref=rsend.at[i], dst_ref=radd.at[kd],
            send_sem=rss.at[4 + kd], recv_sem=rsr.at[4 + kd],
            device_id=(t, lax.rem(c + 2 + 4 * core, NC)), device_id_type=MESH,
        )

    def mate_copy(i):
        return pltpu.make_async_remote_copy(
            src_ref=rsend.at[i], dst_ref=rrecv.at[0, my_rows],
            send_sem=rss.at[6], recv_sem=rsr.at[6], device_id=mate, device_id_type=MESH,
        )

    def owner_of(i):
        cp = zat(OFFSETS[i])
        return lax.rem(lax.div(cp, 2) - yy + NC // 2, NC // 2), lax.rem(cp, 2)

    def chip_sum(i):
        e, kd = owner_of(i)
        need(f"pair{i}")
        total = pown[i].astype(F32) + precv[i].astype(F32)
        rsend[i] = total.astype(BF16)

        @pl.when(e == 2)
        def _():
            add_copy(kd, i).start()

        @pl.when(e == 3 - 2 * core)
        def _():
            owner_copy(lax.div(e, 2), kd, i).start()

        @pl.when((e == 0) & (kd != core))
        def _():
            mate_copy(i).start()

        @pl.when((e == 0) & (kd == core))
        def _():
            rrecv[0, my_rows, :] = rsend[i]

    def added_sum(i):
        e, kd = owner_of(i)

        @pl.when(e == 1 + 2 * core)
        def _():
            add_copy(kd, i).wait_recv()
            total = rsend[i].astype(F32) + radd[kd].astype(F32)
            rsend[i] = total.astype(BF16)
            owner_copy(lax.div(e, 2), kd, i).start()

    added = []

    def hidden_grad(i):
        weights_ready(i)
        need("vgc")
        cp = zat(OFFSETS[i])
        added.append(i)
        first, last = len(added) == 1, len(added) == NC

        def part(n, carry):
            rows_n = pl.ds(al(n * 256, 256), 256)
            w = jnp.concatenate([W[cp * HH + j, rows_n, :] for j in range(HH)], axis=1)
            term = dot_t(VG[cp], w)
            if not first:
                term = term + acc[n]
            if last:
                dh_out[:, rows_n] = term.astype(BF16)
            else:
                acc[n] = term
            return carry

        lax.fori_loop(0, COLS // 256, part, 0)

    def delta():
        for n in (0, 1, 2, 3, 6):
            pltpu.make_async_remote_copy(
                src_ref=rsend.at[0], dst_ref=rrecv.at[0, my_rows], send_sem=rss.at[n],
                recv_sem=rsr.at[n], device_id=mate, device_id_type=MESH,
            ).wait_recv()
        total = rrecv[0].astype(F32) + rrecv[1].astype(F32) + rrecv[2].astype(F32)
        vbuf[...] = total.astype(BF16)

        def delta_head(h, carry):
            hs = head_cols(h)
            for b, i0, j0, jn in TILES:
                qi = pl.ds(i0, HALF)
                gv = dot_t(vbuf[pl.ds(j0, jn), hs], gs[b, qi, hs])
                gv_ref[b, h, pl.ds(j0, jn), qi] = gv
                w = e_ref[b, h, pl.ds(j0, jn), qi].astype(BF16).astype(F32)
                part = jnp.sum(w * gv, axis=0, keepdims=True)
                table = dl_own if b == 0 else dl_nxt
                table[h, :, qi] = jnp.where(row8 == 0, part, 0.0)
            return carry

        lax.fori_loop(0, HH, delta_head, 0)
        send("dl", dl_own, dl_fn, prv)
        send("dl", dl_nxt, dl_fp, nxt)

    def key():
        need("dl")

        def key_head(h, carry):
            deltas = (
                dl_own[h, pl.ds(0, 1), :] + dl_fp[h, pl.ds(0, 1), :],
                dl_nxt[h, pl.ds(0, 1), :] + dl_fn[h, pl.ds(0, 1), :],
            )
            tiles = []
            for b, i0, j0, jn in TILES:
                qi = pl.ds(i0, HALF)
                p = e_ref[b, h, pl.ds(j0, jn), qi]
                gv = gv_ref[b, h, pl.ds(j0, jn), qi]
                tiles.append((p * (gv - deltas[b][:, i0 : i0 + HALF])).astype(BF16))
            top, bottom = gather_terms(tiles, qs, h)
            hs = head_cols(h)
            dk_out[pl.ds(0, 256), hs] = (top * scale).astype(BF16)
            dk_out[pl.ds(256, 256), hs] = (bottom * scale).astype(BF16)
            return carry

        lax.fori_loop(0, HH, key_head, 0)

    steps = {
        "issue": issue, "i_ax": issue_ax,
        "i_bm": lambda: spread(-1, 1, "p"), "mm": lambda: spread(-1, 3, "m"),
        "i_k": lambda: regroup("k", k, ks),
        "i_q": lambda: regroup("q", q, qs.at[0]),
        "i_g": lambda: regroup("g", g, gs.at[0]),
        "pos": positions, "LN": norm_glu, "conv": conv, "enc": encode, "encx": encode_x, "er": encode_relay, "adapt": adapt, "place": place,
        "hq": lambda: halo("q", q, qs.at[1]), "hg": lambda: halo("g", g, gs.at[1]),
        "sc0": score_own, "sc1": score_next, "prob": prob, "vgr": vg_relay, "vgf": vg_last,
        "rm": lambda: relay(-1), "delta": delta, "key": key,
    }
    for s in range(4):
        steps[f"a0_s{s}"] = lambda s=s: a_step(0, s)
        steps[f"a1_s{s}"] = lambda s=s: a_step(1, s)
        steps[f"b_s{s}"] = lambda s=s: b_step(s)
        steps[f"d_s{s}"] = lambda s=s: d_step(s)
        steps[f"p{s}"] = lambda s=s: spread(s, 1, "p")
        steps[f"m{s}"] = lambda s=s: spread(s, 3, "m")
        steps[f"r{s}"] = lambda s=s: relay(s)
    for i in range(NC):
        steps[f"t{i}"] = lambda i=i: terms(i)
        steps[f"rs{i}"] = lambda i=i: chip_sum(i)
        steps[f"ad{i}"] = lambda i=i: added_sum(i)
        steps[f"dh{i}"] = lambda i=i: hidden_grad(i)
    for name in ORDER:
        steps[name]()

    def audio_sent(d, carry):
        audio_copy(d).wait_send()
        return carry

    lax.fori_loop(1, NT, audio_sent, 0)
    for n in range(7):
        pltpu.make_async_remote_copy(
            src_ref=rsend.at[0], dst_ref=rrecv.at[0, my_rows], send_sem=rss.at[n],
            recv_sem=rsr.at[n], device_id=mate, device_id_type=MESH,
        ).wait_send()
    for name in groups:
        need(name)
    for copy in sends:
        copy.wait_send()


def body(
    frames, value_weight, gate_weight, conv_taps, out_weight, adapter, audio_pos, text_rows,
    value_proj, queries, keys, grad_out, window_low,
):
    vm = pl.BlockSpec(memory_space=pltpu.VMEM)
    hbm = pl.BlockSpec(memory_space=pl.ANY)
    vmem = pltpu.VMEM
    dma = pltpu.SemaphoreType.DMA
    return pl.pallas_call(
        kernel,
        out_shape=(
            jax.ShapeDtypeStruct((TOK, HC), BF16),
            jax.ShapeDtypeStruct((TOK, COLS), BF16),
        ),
        in_specs=[hbm] * 6 + [vm] * 2 + [hbm] * 5,
        out_specs=(vm, vm),
        scratch_shapes=[
            vmem((NT, COLS, DH), BF16),
            vmem((DE, QUART), BF16),
            vmem((2, TOK, HC), BF16),
            vmem((2, TOK, HC), BF16),
            vmem((TOK, HC), BF16),
            vmem((8, TOK), jnp.int32),
            vmem((8, TOK), jnp.int32),
            vmem((AUD, DE), BF16),
            vmem((DE, DH), BF16),
            vmem((DE, DH), BF16),
            vmem(conv_taps.shape, F32),
            vmem((DH, DE), BF16),
            vmem((TOK, COLS), BF16),
            vmem((8, NX * AUD), jnp.int32),
            vmem((8, NT * SLOT), jnp.int32),
            vmem((AUD + 32, DE), BF16),
            vmem((AUD + 32, DH), F32),
            vmem((AUD, DE), BF16),
            vmem((NC, 16, DE), BF16),
            vmem((NX, AUD, DE), BF16),
            vmem((NX * AUD, QUART), BF16),
            vmem((NT * NX * SLOT, QUART), BF16),
            vmem((NX, NT * SLOT, QUART), BF16),
            vmem((TOK, COLS), BF16),
            vmem((2, HH, TOK, TOK), F32),
            vmem((2, HH, TOK, TOK), F32),
        ]
        + [vmem((HH, 8, TOK), F32)] * 8
        + [
            vmem((NC, TOK, HC), BF16),
            vmem((NC, HALF, HC), BF16),
            vmem((NC, HALF, HC), BF16),
            vmem((NC, HALF, HC), BF16),
            vmem((NC, HALF, HC), BF16),
            vmem((2, HALF, HC), BF16),
            vmem((3, TOK, HC), BF16),
            vmem((TOK, HC), BF16),
            vmem((COLS // 256, TOK, 256), F32),
            dma((N_SEMS,)),
            dma((N_SEMS,)),
            dma((16,)),
            dma((NT,)),
            dma((NT,)),
            dma((NC,)),
            dma((NC,)),
        ],
        compiler_params=pltpu.CompilerParams(
            collective_id=0, has_side_effects=True, vmem_limit_bytes=60 * 1024 * 1024
        ),
        cost_estimate=pl.CostEstimate(flops=13_000_000_000, bytes_accessed=8_000_000, transcendentals=4_000_000),
    )(
        frames, value_weight, gate_weight, conv_taps, out_weight, text_rows,
        window_low.reshape(1, TOK), audio_pos.reshape(NT, AUD),
        adapter, value_proj, queries, keys, grad_out,
    )


def solution(mesh):
    return jax.shard_map(
        body,
        mesh=mesh,
        in_specs=(
            P("tm", None),
            P(None, "ctx"),
            P(None, "ctx"),
            P(None, "ctx"),
            P("ctx", None),
            P("tm", "ctx"),
            P(),
            P("tm", "ctx"),
            P("ctx", "tm"),
            P(("tm", "ctx"), None),
            P(("tm", "ctx"), None),
            P(("tm", "ctx"), None),
            P("tm"),
        ),
        out_specs=(P("tm", "ctx"), P("tm", "ctx")),
        check_vma=False,
    )
```

```python
import math

import jax
import jax.numpy as jnp
from jax import lax
from jax.experimental import pallas as pl
from jax.experimental.pallas import tpu as pltpu
from jax.sharding import PartitionSpec as P

DH = 128
NORM_EPS = 1e-05
MASK_FILL = -1e30
MESH = pl.DeviceIdType.MESH
F32 = jnp.float32
BF16 = jnp.bfloat16

NT = 32
NC = 8
NX = 4
NZ = 8
TOK = 512
AUD = 128
DE = 1024
COLS = 1024
HC = 512
HH = HC // DH
HALF = TOK // 2
SLOT = 8
TILES = ((0, 0, 0, 256), (0, 256, 0, 512), (1, 0, 0, 512), (1, 256, 256, 256))
N_SEMS = 160
QUART = COLS // NX
ROWS_A = 512
ROWS_B = COLS - ROWS_A
OFFSETS = (0, -1, 1, -2, 2, -3, 3, 4)
ORDER = (
    "issue", "i_q", "b_s0", "i_ax", "LN", "mm", "d_s0", "b_s1", "i_bm", "conv", "m0", "p0",
    "d_s1", "i_k", "b_s2", "hq", "a0_s0", "d_s2", "enc", "r0", "pos", "a1_s0", "i_g", "encx",
    "a0_s1", "b_s3", "sc0", "a1_s1", "d_s3", "er", "hg", "p3", "a0_s2", "p1", "sc1", "adapt",
    "p2", "prob", "m1", "rm", "m3", "a1_s2", "r1", "place", "r2", "m2", "t0", "vgr", "r3", "t1",
    "a0_s3", "a1_s3", "rs0", "t2", "t4", "rs2", "rs1", "t3", "t6", "ad0", "t7", "rs4", "rs3",
    "t5", "ad1", "ad4", "vgf", "rs5", "dh0", "dh1", "dh4", "rs6", "rs7", "dh2", "dh3", "dh5",
    "ad3", "ad2", "ad5", "dh6", "ad6", "ad7", "delta", "dh7", "key",
)


def dot(a, b):
    return jnp.dot(a, b, preferred_element_type=F32)


def dot_t(a, b):
    return lax.dot_general(a, b, (((1,), (1,)), ((), ())), preferred_element_type=F32)


def iota(shape, dim):
    return lax.broadcasted_iota(jnp.int32, shape, dim)


def kernel(
    frames, vw, gw, taps, ow, text, low, aud, adapter, vp, q, k, g,
    dk_out, dh_out,
    W, AD, qs, gs, ks, low_s, lown, frames_s, vw_s, gw_s, taps_s, ow_s, text_s,
    slot_s, land_s, ext, glu_s, mixs, mixr, enc, adp, pick, inc, hid,
    e_ref, gv_ref, st_own, st_nxt, st_fp, st_fn, dl_own, dl_nxt, dl_fp, dl_fn,
    VG, pfull, precv, rsend, radd, rrecv, vbuf, acc,
    ssem, rsem, lsem, aus, aur, rss, rsr,
):
    t = lax.axis_index("tm")
    c = lax.axis_index("ctx")
    x = lax.rem(t, NX)
    z = lax.div(t, NX)
    core = lax.rem(c, 2)
    yy = lax.div(c, 2)
    up = (lax.rem(z + 1, NZ) * NX + x, c)
    dn = (lax.rem(z + NZ - 1, NZ) * NX + x, c)
    nxt = (lax.rem(t + 1, NT), c)
    prv = (lax.rem(t + NT - 1, NT), c)
    mate = (t, c + 1 - 2 * core)

    def ctx_peer(d):
        return (t, lax.rem(c + d, NC))

    def x_peer(d):
        return (z * NX + lax.rem(x + d, NX), c)

    def zat(d):
        return lax.rem(z + d + NZ, NZ)

    def al(v, m):
        return pl.multiple_of(v, m)

    sends = []
    groups = {}
    waited = set()

    def send(name, src, dst, dev):
        i = len(sends)
        copy = pltpu.make_async_remote_copy(
            src_ref=src, dst_ref=dst, send_sem=ssem.at[i], recv_sem=rsem.at[i],
            device_id=dev, device_id_type=MESH,
        )
        copy.start()
        sends.append(copy)
        groups.setdefault(name, []).append(copy)

    def need(*names):
        for name in names:
            if name not in waited:
                waited.add(name)
                for copy in groups[name]:
                    if name in here:
                        copy.wait()
                    else:
                        copy.wait_recv()

    here = set()

    def local(name, src, dst):
        copy = pltpu.make_async_copy(src, dst, lsem.at[len(here)])
        copy.start()
        here.add(name)
        groups[name] = [copy]

    own_rows = pl.ds(al(c * 64, 64), 64)
    own_cols = pl.ds(al(c * HC, HC), HC)
    ad_rows = pl.ds(al(t * 32, 32), 32)
    rows_a = pl.ds(0, ROWS_A)
    rows_b = pl.ds(ROWS_A, ROWS_B)

    def issue():
        bar = pltpu.get_barrier_semaphore()

        def greet(d, carry):
            pl.semaphore_signal(bar, inc=1, device_id=(lax.rem(t + d, NT), c), device_id_type=MESH)
            return carry

        lax.fori_loop(1, NT, greet, 0)
        for d in range(1, NC):
            pl.semaphore_signal(bar, inc=1, device_id=ctx_peer(d), device_id_type=MESH)
        local("frames", frames, frames_s)
        local("vw", vw, vw_s)
        local("gw", gw, gw_s)
        local("vp", vp, W.at[t])
        local("ad", adapter.at[:, pl.ds(al(x * QUART, QUART), QUART)], AD.at[ad_rows])
        local("taps", taps, taps_s)
        local("ow", ow, ow_s)
        local("k0", k.at[:, own_cols], ks.at[own_rows])
        local("q0", q.at[:, own_cols], qs.at[0, own_rows])
        local("g0", g.at[:, own_cols], gs.at[0, own_rows])
        local("text", text, text_s)
        low_s[...] = jnp.broadcast_to(low[...], low_s.shape)
        pl.semaphore_wait(bar, NT - 1 + NC - 1)
        send("fh", frames.at[pl.ds(AUD - 16, 16)], ext.at[pl.ds(0, 16)], nxt)
        send("fh", frames.at[pl.ds(0, 16)], ext.at[pl.ds(AUD + 16, 16)], prv)
        for d in (1, 3, 2):
            quarter = pl.ds(al(lax.rem(x + d, NX) * QUART, QUART), QUART)
            send("adx", adapter.at[:, quarter], AD.at[ad_rows], x_peer(d))
        send("low", low_s, lown, prv)

    def b_ref(zz, xx=x):
        return W.at[zz * NX + xx, rows_b]

    def b_part(zz, p):
        return W.at[zz * NX + x, pl.ds(ROWS_A + ROWS_B // 2 * p, ROWS_B // 2)]

    def a_ref(zz, pair):
        return W.at[pl.ds(zz * NX + 2 * pair, 2), rows_a]

    def a_part(zz, pair, p):
        return W.at[zz * NX + 2 * pair + p, rows_a]

    def d_ref(zz):
        return AD.at[pl.ds(al(zz * 128, 128), 128)]

    def d_part(zz, p):
        return AD.at[pl.ds(al(zz * 128 + 64 * p, 64), 64)]

    def ring(name, s, ref_of, part_of):
        if s < NZ // 2 - 1:
            u, v = ref_of(zat(-s)), ref_of(zat(s))
        else:
            u, v = part_of(zat(-s), 0), part_of(zat(s), 1)
        send(f"{name}{s}", u, u, up)
        send(f"{name}{s}", v, v, dn)

    def a_step(pair, s):
        need(*([f"a{pair}_{s - 1}"] if s else ["ax", "vp"]))
        ring(f"a{pair}_", s, lambda zz: a_ref(zz, pair), lambda zz, p: a_part(zz, pair, p))

    def b_step(s):
        need(*([f"b{s - 1}"] if s else ["vp"]))
        ring("b", s, b_ref, b_part)

    def d_step(s):
        need(*([f"d{s - 1}"] if s else ["adx", "ad"]))
        ring("d", s, d_ref, d_part)

    def reached(s):
        return (0,) if s < 0 else ((-1 - s, 1 + s) if s < 3 else (4,))

    def spread(s, d, kind):
        need(f"b{s}" if s >= 0 else "vp")
        for o in reached(s):
            send(f"{kind}{s}", b_ref(zat(o)), b_ref(zat(o)), x_peer(d))

    def relay(s):
        turn = 3 if s in (-1, 3) else 1
        need(f"p{s}" if turn == 1 else f"m{s}")
        origin = lax.rem(x + NX - turn, NX)
        for o in reached(s):
            send(f"r{s}", b_ref(zat(o), origin), b_ref(zat(o), origin), x_peer(turn))

    def issue_ax():
        for d in (1, 3, 2):
            send("ax", vp.at[rows_a], W.at[t, rows_a], x_peer(d))

    def regroup(name, src, dst):
        for d in (4, 1, 7, 2, 6, 3, 5):
            peer = lax.rem(c + d, NC)
            send(name, src.at[:, pl.ds(al(peer * HC, HC), HC)], dst.at[own_rows], (t, peer))

    def positions():
        order = (iota((AUD, AUD), 0) < iota((AUD, AUD), 1)).astype(F32).astype(BF16)
        for b in range(NX):
            target = aud[pl.ds(z * NX + b, 1), :] // TOK
            hit = (iota((NT, AUD), 0) == target).astype(F32)
            rank = jnp.sum(dot(hit.astype(BF16), order) * hit, axis=0, keepdims=True)
            slot = target * (NX * SLOT) + b * SLOT + rank.astype(jnp.int32)
            slot_s[:, pl.ds(b * AUD, AUD)] = jnp.broadcast_to(slot, (8, AUD))
        table = aud[...]
        landing = table // TOK == t
        landing_rank = dot(landing.astype(F32).astype(BF16), order)
        spot = jnp.where(landing, table - t * TOK + 1, 0)
        n = NT * SLOT
        grow = (iota((n, NT), 0) // SLOT == iota((n, NT), 1)).astype(F32).astype(BF16)
        spot_hi = dot(grow, (spot // 16).astype(F32).astype(BF16))
        spot_lo = dot(grow, (spot % 16).astype(F32).astype(BF16))
        ranks = dot(grow, jnp.where(landing, landing_rank, 64.0).astype(BF16))
        spots = spot_hi * 16.0 + spot_lo
        r = (iota((n, AUD), 0) % SLOT).astype(F32)
        col = jnp.sum(jnp.where(ranks == r, spots, 0.0), axis=1, keepdims=True) - 1.0
        eye = iota((n, n), 0) == iota((n, n), 1)
        line = jnp.sum(jnp.where(eye, col, 0.0), axis=0, keepdims=True)
        land_s[...] = jnp.broadcast_to(line, (8, n)).astype(jnp.int32)

    def norm_glu():
        need("frames", "vw", "gw")
        ext[pl.ds(16, AUD), :] = frames_s[...]
        need("fh")
        rows = ext[...].astype(F32)
        centre = jnp.mean(rows, axis=1, keepdims=True)
        off = rows - centre
        spread_ = jnp.mean(off * off, axis=1, keepdims=True)
        normed = (off * lax.rsqrt(spread_ + NORM_EPS)).astype(BF16)
        value_part = dot(normed, vw_s[...])
        gate_part = dot(normed, gw_s[...])
        glu = (value_part * jax.nn.sigmoid(gate_part)).astype(BF16).astype(F32)
        row = iota(glu.shape, 0)
        first = jnp.where(t == 0, 16, 0)
        last = jnp.where(t == NT - 1, AUD + 16, AUD + 32)
        glu_s[...] = jnp.where((row >= first) & (row < last), glu, 0.0)

    def conv():
        need("taps", "ow")
        smooth = jnp.zeros((AUD, DH), F32)
        for j in range(taps_s.shape[0]):
            smooth = smooth + taps_s[pl.ds(j, 1), :] * glu_s[pl.ds(1 + j, AUD), :]
        action = (smooth * jax.nn.sigmoid(smooth)).astype(BF16)
        mixs[...] = dot(action, ow_s[...]).astype(BF16)
        for d in (4, 2, 6, 3, 5, 1, 7):
            rows_d = pl.ds(al(lax.rem(c + d, NC) * 16, 16), 16)
            send("mix", mixs.at[rows_d], mixr.at[d], ctx_peer(d))

    def encode():
        need("mix")
        mine = pl.ds(al(c * 16, 16), 16)
        total = frames_s[mine, :].astype(F32) + mixs[mine, :].astype(F32)
        for d in range(1, NC):
            total = total + mixr[d].astype(F32)
        enc[x, mine, :] = total.astype(BF16)
        for d in (4, 2, 6, 3, 5, 1, 7):
            send("enc", enc.at[x, mine], enc.at[x, mine], ctx_peer(d))

    def encode_x():
        need("enc")
        for d in (1, 3):
            send("ex", enc.at[x], enc.at[x], x_peer(d))

    def encode_relay():
        need("ex")
        for d, at in ((1, 0), (3, AUD // 2)):
            part = enc.at[lax.rem(x + NX - d, NX), pl.ds(at, AUD // 2)]
            send("ex2", part, part, x_peer(d))

    def halo(name):
        part = qs if name == "q" else gs
        need(name, name + "0")
        send("h" + name, part.at[0], part.at[1], prv)

    scale = 1.0 / math.sqrt(DH)
    base = t * TOK
    row8 = iota((8, HALF), 0)

    def head_cols(h):
        return pl.ds(al(h * DH, DH), DH)

    def score_tiles(block, lows, floor, stats):
        def one_head(h, carry):
            hs = head_cols(h)
            for b, i0, j0, jn in TILES:
                if b != block:
                    continue
                qi = pl.ds(i0, HALF)
                s = dot_t(ks[pl.ds(j0, jn), hs], qs[b, qi, hs]) * scale
                jj = iota((jn, HALF), 0) + j0
                ok = jj >= jnp.maximum(lows[pl.ds(0, 1), qi] - base, floor)
                if block == 0:
                    ok = ok & (jj <= iota((jn, HALF), 1) + i0)
                s = jnp.where(ok, s, MASK_FILL)
                m = jnp.maximum(jnp.max(s, axis=0, keepdims=True), MASK_FILL / 10)
                e = jnp.exp(s - m)
                n = jnp.sum(e, axis=0, keepdims=True)
                e_ref[b, h, pl.ds(j0, jn), qi] = e
                stats[h, :, qi] = jnp.where(row8 == 0, m, n)
            return carry

        lax.fori_loop(0, HH, one_head, 0)

    def score_own():
        need("k", "k0", "q", "q0")
        score_tiles(0, low_s, 0, st_own)
        send("sta", st_own, st_fn, prv)

    def score_next():
        need("k", "k0", "hq", "low")
        score_tiles(1, lown, jnp.where(t == NT - 1, TOK, 0), st_nxt)
        send("stb", st_nxt, st_fp, nxt)

    group_rows = NX * SLOT
    my_slot = pl.ds(al(z * group_rows, group_rows), group_rows)

    def slot_rows(tm):
        return pl.ds(al(tm * group_rows, group_rows), group_rows)

    def audio_copy(d):
        peer = lax.rem(t + d, NT)
        return pltpu.make_async_remote_copy(
            src_ref=pick.at[slot_rows(peer)], dst_ref=inc.at[x, my_slot],
            send_sem=aus.at[d], recv_sem=aur.at[d], device_id=(peer, c), device_id_type=MESH,
        )

    def adapt():
        need("d3", "ex", "ex2")
        adp[...] = dot(enc[...].reshape(NX * AUD, DE), AD[...]).astype(BF16)
        for n in range(4):
            slot_row = iota((256, NX * AUD), 0) + 256 * n
            picker = (slot_row == slot_s[pl.ds(0, 1), :]).astype(F32).astype(BF16)
            pick[pl.ds(256 * n, 256), :] = dot(picker, adp[...]).astype(BF16)

        def audio_start(d, carry):
            audio_copy(d).start()
            return carry

        lax.fori_loop(1, NT, audio_start, 0)
        inc[x, my_slot, :] = pick[slot_rows(t), :]

    def factor(mine_st, other_st, h):
        m1, s1 = mine_st[h, pl.ds(0, 1), :], mine_st[h, pl.ds(1, 1), :]
        m2, s2 = other_st[h, pl.ds(0, 1), :], other_st[h, pl.ds(1, 1), :]
        m = jnp.maximum(m1, m2)
        a1 = jnp.exp(m1 - m)
        return a1 / (s1 * a1 + s2 * jnp.exp(m2 - m))

    def gather_terms(tiles, other, h):
        hs = head_cols(h)
        first, second = pl.ds(0, 256), pl.ds(256, 256)
        top = dot(tiles[0], other[0, first, hs]) + dot(tiles[1][:256], other[0, second, hs])
        top = top + dot(tiles[2][:256], other[1, first, hs])
        bottom = dot(tiles[1][256:], other[0, second, hs])
        bottom = bottom + dot(tiles[2][256:], other[1, first, hs])
        bottom = bottom + dot(tiles[3], other[1, second, hs])
        return top, bottom

    def prob():
        need("sta", "stb", "g", "g0", "hg")

        def prob_head(h, carry):
            f = (factor(st_own, st_fp, h), factor(st_nxt, st_fn, h))
            tiles = []
            for b, i0, j0, jn in TILES:
                p = e_ref[b, h, pl.ds(j0, jn), pl.ds(i0, HALF)] * f[b][:, i0 : i0 + HALF]
                e_ref[b, h, pl.ds(j0, jn), pl.ds(i0, HALF)] = p
                tiles.append(p.astype(BF16))
            top, bottom = gather_terms(tiles, gs, h)
            hs = head_cols(h)
            VG[c, pl.ds(0, 256), hs] = top.astype(BF16)
            VG[c, pl.ds(256, 256), hs] = bottom.astype(BF16)
            return carry

        lax.fori_loop(0, HH, prob_head, 0)
        send("vg1", VG.at[c], VG.at[c], ctx_peer(2))
        send("vg3", VG.at[c], VG.at[c], ctx_peer(6))
        send("vgc", VG.at[c], VG.at[c], mate)

    below, above, across = [lax.rem(c + d, NC) for d in (6, 2, 4)]

    def vg_relay():
        need("vg1", "vg3")
        one, two = VG.at[below, pl.ds(0, 256)], VG.at[above, pl.ds(256, 256)]
        send("vg2", one, one, ctx_peer(2))
        send("vg2", two, two, ctx_peer(6))
        send("vgc", VG.at[below], VG.at[below], mate)
        send("vgc", VG.at[above], VG.at[above], mate)

    def vg_last():
        need("vg2")
        send("vgc", VG.at[across], VG.at[across], mate)

    def place():
        need("text")

        def audio_arrived(d, carry):
            audio_copy(d).wait_recv()
            return carry

        lax.fori_loop(1, NT, audio_arrived, 0)
        hits = (iota((TOK, NT * SLOT), 0) == land_s[pl.ds(0, 1), :]).astype(F32)
        there = jnp.sum(hits, axis=1, keepdims=True) > 0.5
        hits = hits.astype(BF16)
        for n in range(NX):
            cols = pl.ds(QUART * n, QUART)
            rows_in = dot(hits, inc[n])
            hid[:, cols] = jnp.where(there, rows_in, text_s[:, cols].astype(F32)).astype(BF16)

    mate_rows = pl.ds(al((1 - core) * HALF, HALF), HALF)
    my_rows = pl.ds(al(core * HALF, HALF), HALF)

    def weights_ready(i):
        s = (i - 1) // 2
        need(f"m{s}", f"p{s}", f"r{s}")
        need(*([f"a0_{s}", f"a1_{s}", f"b{s}"] if i else ["ax", "vp"]))

    def terms(i):
        weights_ready(i)
        cp = zat(OFFSETS[i])
        for j in range(0, HH, 2):
            w = jnp.concatenate([W[cp * HH + j], W[cp * HH + j + 1]], axis=1)
            pfull[i, :, pl.ds(j * DH, 2 * DH)] = dot(hid[...], w).astype(BF16)
        send(f"pair{i}", pfull.at[i, mate_rows], precv.at[i], mate)

    def owner_copy(side, kd, i):
        owner = lax.rem(yy + 1 + 2 * side, NC // 2) * 2 + kd
        return pltpu.make_async_remote_copy(
            src_ref=rsend.at[i], dst_ref=rrecv.at[1 + side, my_rows],
            send_sem=rss.at[2 * side + kd], recv_sem=rsr.at[2 * side + core],
            device_id=(t, owner), device_id_type=MESH,
        )

    def add_copy(kd, i):
        return pltpu.make_async_remote_copy(
            src_ref=rsend.at[i], dst_ref=radd.at[kd],
            send_sem=rss.at[4 + kd], recv_sem=rsr.at[4 + kd],
            device_id=(t, lax.rem(c + 2 + 4 * core, NC)), device_id_type=MESH,
        )

    def mate_copy(i):
        return pltpu.make_async_remote_copy(
            src_ref=rsend.at[i], dst_ref=rrecv.at[0, my_rows],
            send_sem=rss.at[6], recv_sem=rsr.at[6], device_id=mate, device_id_type=MESH,
        )

    def owner_of(i):
        cp = zat(OFFSETS[i])
        return lax.rem(lax.div(cp, 2) - yy + NC // 2, NC // 2), lax.rem(cp, 2)

    def chip_sum(i):
        e, kd = owner_of(i)
        need(f"pair{i}")
        total = pfull[i, my_rows, :].astype(F32) + precv[i].astype(F32)
        rsend[i] = total.astype(BF16)

        @pl.when(e == 2)
        def _():
            add_copy(kd, i).start()

        @pl.when(e == 3 - 2 * core)
        def _():
            owner_copy(lax.div(e, 2), kd, i).start()

        @pl.when((e == 0) & (kd != core))
        def _():
            mate_copy(i).start()

        @pl.when((e == 0) & (kd == core))
        def _():
            rrecv[0, my_rows, :] = rsend[i]

    def added_sum(i):
        e, kd = owner_of(i)

        @pl.when(e == 1 + 2 * core)
        def _():
            add_copy(kd, i).wait_recv()
            total = rsend[i].astype(F32) + radd[kd].astype(F32)
            rsend[i] = total.astype(BF16)
            owner_copy(lax.div(e, 2), kd, i).start()

    added = []

    def hidden_grad(i):
        weights_ready(i)
        need("vgc")
        cp = zat(OFFSETS[i])
        added.append(i)
        first, last = len(added) == 1, len(added) == NC

        def part(n, carry):
            rows_n = pl.ds(al(n * 256, 256), 256)
            w = jnp.concatenate([W[cp * HH + j, rows_n, :] for j in range(HH)], axis=1)
            term = dot_t(VG[cp], w)
            if not first:
                term = term + acc[n]
            if last:
                dh_out[:, rows_n] = term.astype(BF16)
            else:
                acc[n] = term
            return carry

        lax.fori_loop(0, COLS // 256, part, 0)

    def delta():
        for n in (0, 1, 2, 3, 6):
            pltpu.make_async_remote_copy(
                src_ref=rsend.at[0], dst_ref=rrecv.at[0, my_rows], send_sem=rss.at[n],
                recv_sem=rsr.at[n], device_id=mate, device_id_type=MESH,
            ).wait_recv()
        total = rrecv[0].astype(F32) + rrecv[1].astype(F32) + rrecv[2].astype(F32)
        vbuf[...] = total.astype(BF16)

        def delta_head(h, carry):
            hs = head_cols(h)
            for b, i0, j0, jn in TILES:
                qi = pl.ds(i0, HALF)
                gv = dot_t(vbuf[pl.ds(j0, jn), hs], gs[b, qi, hs])
                gv_ref[b, h, pl.ds(j0, jn), qi] = gv
                w = e_ref[b, h, pl.ds(j0, jn), qi].astype(BF16).astype(F32)
                part = jnp.sum(w * gv, axis=0, keepdims=True)
                table = dl_own if b == 0 else dl_nxt
                table[h, :, qi] = jnp.where(row8 == 0, part, 0.0)
            return carry

        lax.fori_loop(0, HH, delta_head, 0)
        send("dl", dl_own, dl_fn, prv)
        send("dl", dl_nxt, dl_fp, nxt)

    def key():
        need("dl")

        def key_head(h, carry):
            deltas = (
                dl_own[h, pl.ds(0, 1), :] + dl_fp[h, pl.ds(0, 1), :],
                dl_nxt[h, pl.ds(0, 1), :] + dl_fn[h, pl.ds(0, 1), :],
            )
            tiles = []
            for b, i0, j0, jn in TILES:
                qi = pl.ds(i0, HALF)
                p = e_ref[b, h, pl.ds(j0, jn), qi]
                gv = gv_ref[b, h, pl.ds(j0, jn), qi]
                tiles.append((p * (gv - deltas[b][:, i0 : i0 + HALF])).astype(BF16))
            top, bottom = gather_terms(tiles, qs, h)
            hs = head_cols(h)
            dk_out[pl.ds(0, 256), hs] = (top * scale).astype(BF16)
            dk_out[pl.ds(256, 256), hs] = (bottom * scale).astype(BF16)
            return carry

        lax.fori_loop(0, HH, key_head, 0)

    steps = {
        "issue": issue, "i_ax": issue_ax,
        "i_bm": lambda: spread(-1, 1, "p"), "mm": lambda: spread(-1, 3, "m"),
        "i_k": lambda: regroup("k", k, ks),
        "i_q": lambda: regroup("q", q, qs.at[0]),
        "i_g": lambda: regroup("g", g, gs.at[0]),
        "pos": positions, "LN": norm_glu, "conv": conv, "enc": encode, "encx": encode_x, "er": encode_relay, "adapt": adapt, "place": place,
        "hq": lambda: halo("q"), "hg": lambda: halo("g"),
        "sc0": score_own, "sc1": score_next, "prob": prob, "vgr": vg_relay, "vgf": vg_last,
        "rm": lambda: relay(-1), "delta": delta, "key": key,
    }
    for s in range(4):
        steps[f"a0_s{s}"] = lambda s=s: a_step(0, s)
        steps[f"a1_s{s}"] = lambda s=s: a_step(1, s)
        steps[f"b_s{s}"] = lambda s=s: b_step(s)
        steps[f"d_s{s}"] = lambda s=s: d_step(s)
        steps[f"p{s}"] = lambda s=s: spread(s, 1, "p")
        steps[f"m{s}"] = lambda s=s: spread(s, 3, "m")
        steps[f"r{s}"] = lambda s=s: relay(s)
    for i in range(NC):
        steps[f"t{i}"] = lambda i=i: terms(i)
        steps[f"rs{i}"] = lambda i=i: chip_sum(i)
        steps[f"ad{i}"] = lambda i=i: added_sum(i)
        steps[f"dh{i}"] = lambda i=i: hidden_grad(i)
    for name in ORDER:
        steps[name]()

    def audio_sent(d, carry):
        audio_copy(d).wait_send()
        return carry

    lax.fori_loop(1, NT, audio_sent, 0)
    for n in range(7):
        pltpu.make_async_remote_copy(
            src_ref=rsend.at[0], dst_ref=rrecv.at[0, my_rows], send_sem=rss.at[n],
            recv_sem=rsr.at[n], device_id=mate, device_id_type=MESH,
        ).wait_send()
    for name in groups:
        need(name)
    for copy in sends:
        copy.wait_send()


def body(
    frames, value_weight, gate_weight, conv_taps, out_weight, adapter, audio_pos, text_rows,
    value_proj, queries, keys, grad_out, window_low,
):
    vm = pl.BlockSpec(memory_space=pltpu.VMEM)
    hbm = pl.BlockSpec(memory_space=pl.ANY)
    vmem = pltpu.VMEM
    dma = pltpu.SemaphoreType.DMA
    return pl.pallas_call(
        kernel,
        out_shape=(
            jax.ShapeDtypeStruct((TOK, HC), BF16),
            jax.ShapeDtypeStruct((TOK, COLS), BF16),
        ),
        in_specs=[hbm] * 6 + [vm] * 2 + [hbm] * 5,
        out_specs=(vm, vm),
        scratch_shapes=[
            vmem((NT, COLS, DH), BF16),
            vmem((DE, QUART), BF16),
            vmem((2, TOK, HC), BF16),
            vmem((2, TOK, HC), BF16),
            vmem((TOK, HC), BF16),
            vmem((8, TOK), jnp.int32),
            vmem((8, TOK), jnp.int32),
            vmem((AUD, DE), BF16),
            vmem((DE, DH), BF16),
            vmem((DE, DH), BF16),
            vmem(conv_taps.shape, F32),
            vmem((DH, DE), BF16),
            vmem((TOK, COLS), BF16),
            vmem((8, NX * AUD), jnp.int32),
            vmem((8, NT * SLOT), jnp.int32),
            vmem((AUD + 32, DE), BF16),
            vmem((AUD + 32, DH), F32),
            vmem((AUD, DE), BF16),
            vmem((NC, 16, DE), BF16),
            vmem((NX, AUD, DE), BF16),
            vmem((NX * AUD, QUART), BF16),
            vmem((NT * NX * SLOT, QUART), BF16),
            vmem((NX, NT * SLOT, QUART), BF16),
            vmem((TOK, COLS), BF16),
            vmem((2, HH, TOK, TOK), F32),
            vmem((2, HH, TOK, TOK), F32),
        ]
        + [vmem((HH, 8, TOK), F32)] * 8
        + [
            vmem((NC, TOK, HC), BF16),
            vmem((NC, TOK, HC), BF16),
            vmem((NC, HALF, HC), BF16),
            vmem((NC, HALF, HC), BF16),
            vmem((2, HALF, HC), BF16),
            vmem((3, TOK, HC), BF16),
            vmem((TOK, HC), BF16),
            vmem((COLS // 256, TOK, 256), F32),
            dma((N_SEMS,)),
            dma((N_SEMS,)),
            dma((16,)),
            dma((NT,)),
            dma((NT,)),
            dma((NC,)),
            dma((NC,)),
        ],
        compiler_params=pltpu.CompilerParams(
            collective_id=0, has_side_effects=True, vmem_limit_bytes=60 * 1024 * 1024
        ),
        cost_estimate=pl.CostEstimate(flops=13_000_000_000, bytes_accessed=8_000_000, transcendentals=4_000_000),
    )(
        frames, value_weight, gate_weight, conv_taps, out_weight, text_rows,
        window_low.reshape(1, TOK), audio_pos.reshape(NT, AUD),
        adapter, value_proj, queries, keys, grad_out,
    )


def solution(mesh):
    return jax.shard_map(
        body,
        mesh=mesh,
        in_specs=(
            P("tm", None),
            P(None, "ctx"),
            P(None, "ctx"),
            P(None, "ctx"),
            P("ctx", None),
            P("tm", "ctx"),
            P(),
            P("tm", "ctx"),
            P("ctx", "tm"),
            P(("tm", "ctx"), None),
            P(("tm", "ctx"), None),
            P(("tm", "ctx"), None),
            P("tm"),
        ),
        out_specs=(P("tm", "ctx"), P("tm", "ctx")),
        check_vma=False,
    )
```

```python
import math

import jax
import jax.numpy as jnp
from jax import lax
from jax.experimental import pallas as pl
from jax.experimental.pallas import tpu as pltpu
from jax.sharding import PartitionSpec as P

DH = 128
NORM_EPS = 1e-05
MASK_FILL = -1e30
MESH = pl.DeviceIdType.MESH
F32 = jnp.float32
BF16 = jnp.bfloat16

NT = 32
NC = 8
NX = 4
NZ = 8
TOK = 512
AUD = 128
DE = 1024
COLS = 1024
HC = 512
HH = HC // DH
HALF = TOK // 2
SLOT = 8
TILES = ((0, 0, 0, 256), (0, 256, 0, 512), (1, 0, 0, 512), (1, 256, 256, 256))
N_SEMS = 160
ROWS_A = 384
ROWS_B = COLS - ROWS_A
OFFSETS = (0, -1, 1, -2, 2, -3, 3, 4)
ORDER = (
    "issue", "i_b0", "i_k", "i_q", "mm", "pos", "LN", "d_s0", "i_bm", "p0", "m0", "conv",
    "d_s1", "b_s1", "i_ax", "hq", "rm", "sc0", "i_g", "enc", "b_s2", "p1", "d_s2", "r0", "hg",
    "p2", "d_s3", "b_s3", "a_s0", "sc1", "m3", "adapt", "r1", "m1", "m2", "prob", "a_s1", "r2",
    "vgr", "place", "t0", "t1", "t2", "rs0", "rs1", "a_s2", "t3", "vgf", "p3", "rs2", "t4",
    "rs3", "dh0", "ad0", "rs4", "dh1", "ad1", "r3", "dh2", "ad2", "dh3", "dh4", "a_s3", "ad3",
    "ad4", "t5", "t6", "dh5", "dh6", "rs5", "rs6", "t7", "dh7", "rs7", "ad5", "ad6", "ad7",
    "delta", "key",
)


def dot(a, b):
    return jnp.dot(a, b, preferred_element_type=F32)


def dot_t(a, b):
    return lax.dot_general(a, b, (((1,), (1,)), ((), ())), preferred_element_type=F32)


def iota(shape, dim):
    return lax.broadcasted_iota(jnp.int32, shape, dim)


def kernel(
    frames, vw, gw, taps, ow, text, low, aud, adapter, vp, q, k, g,
    dk_out, dh_out,
    W, AD, qs, gs, ks, low_s, lown, frames_s, vw_s, gw_s, taps_s, ow_s, text_s,
    slot_s, land_s, ext, glu_s, mixs, mixr, enc, adp, pick, inc, hid,
    e_ref, gv_ref, st_own, st_nxt, st_fp, st_fn, dl_own, dl_nxt, dl_fp, dl_fn,
    VG, psend, pown, precv, rsend, radd, rrecv, vbuf, acc,
    ssem, rsem, lsem, aus, aur, rss, rsr,
):
    t = lax.axis_index("tm")
    c = lax.axis_index("ctx")
    x = lax.rem(t, NX)
    z = lax.div(t, NX)
    core = lax.rem(c, 2)
    yy = lax.div(c, 2)
    up = (lax.rem(z + 1, NZ) * NX + x, c)
    dn = (lax.rem(z + NZ - 1, NZ) * NX + x, c)
    nxt = (lax.rem(t + 1, NT), c)
    prv = (lax.rem(t + NT - 1, NT), c)
    mate = (t, c + 1 - 2 * core)

    def ctx_peer(d):
        return (t, lax.rem(c + d, NC))

    def x_peer(d):
        return (z * NX + lax.rem(x + d, NX), c)

    def zat(d):
        return lax.rem(z + d + NZ, NZ)

    def al(v, m):
        return pl.multiple_of(v, m)

    sends = []
    groups = {}
    waited = set()

    def send(name, src, dst, dev):
        i = len(sends)
        copy = pltpu.make_async_remote_copy(
            src_ref=src, dst_ref=dst, send_sem=ssem.at[i], recv_sem=rsem.at[i],
            device_id=dev, device_id_type=MESH,
        )
        copy.start()
        sends.append(copy)
        groups.setdefault(name, []).append(copy)

    def need(*names):
        for name in names:
            if name not in waited:
                waited.add(name)
                for copy in groups[name]:
                    if name in here:
                        copy.wait()
                    else:
                        copy.wait_recv()

    here = set()

    def local(name, src, dst):
        copy = pltpu.make_async_copy(src, dst, lsem.at[len(here)])
        copy.start()
        here.add(name)
        groups[name] = [copy]

    own_rows = pl.ds(al(c * 64, 64), 64)
    own_cols = pl.ds(al(c * HC, HC), HC)
    ad_rows = pl.ds(al(t * 32, 32), 32)
    rows_a = pl.ds(0, ROWS_A)
    rows_b = pl.ds(ROWS_A, ROWS_B)

    def issue():
        bar = pltpu.get_barrier_semaphore()

        def greet(d, carry):
            pl.semaphore_signal(bar, inc=1, device_id=(lax.rem(t + d, NT), c), device_id_type=MESH)
            return carry

        lax.fori_loop(1, NT, greet, 0)
        for d in range(1, NC):
            pl.semaphore_signal(bar, inc=1, device_id=ctx_peer(d), device_id_type=MESH)
        local("frames", frames, frames_s)
        local("vw", vw, vw_s)
        local("gw", gw, gw_s)
        local("vp", vp, W.at[t])
        local("ad", adapter, AD.at[ad_rows])
        local("taps", taps, taps_s)
        local("ow", ow, ow_s)
        local("k0", k.at[:, own_cols], ks.at[own_rows])
        local("q0", q.at[:, own_cols], qs.at[0, own_rows])
        local("g0", g.at[:, own_cols], gs.at[0, own_rows])
        local("text", text, text_s)
        low_s[...] = jnp.broadcast_to(low[...], low_s.shape)
        pl.semaphore_wait(bar, NT - 1 + NC - 1)
        send("fh", frames.at[pl.ds(AUD - 16, 16)], ext.at[pl.ds(0, 16)], nxt)
        send("fh", frames.at[pl.ds(0, 16)], ext.at[pl.ds(AUD + 16, 16)], prv)
        for d in (1, 3, 2):
            send("adx", adapter, AD.at[ad_rows], x_peer(d))
        send("low", low_s, lown, prv)

    def b_ref(zz, xx=x):
        return W.at[zz * NX + xx, rows_b]

    def b_part(zz, p):
        return W.at[zz * NX + x, pl.ds(ROWS_A + ROWS_B // 2 * p, ROWS_B // 2)]

    def a_ref(zz):
        return W.at[pl.ds(zz * NX, NX), rows_a]

    def a_part(zz, p):
        return W.at[pl.ds(zz * NX + 2 * p, 2), rows_a]

    def d_ref(zz):
        return AD.at[pl.ds(al(zz * 128, 128), 128)]

    def d_part(zz, p):
        return AD.at[pl.ds(al(zz * 128 + 64 * p, 64), 64)]

    def ring(name, s, ref_of, part_of):
        if s < NZ // 2 - 1:
            u, v = ref_of(zat(-s)), ref_of(zat(s))
        else:
            u, v = part_of(zat(-s), 0), part_of(zat(s), 1)
        send(f"{name}{s}", u, u, up)
        send(f"{name}{s}", v, v, dn)

    def a_step(s):
        need(*([f"a{s - 1}"] if s else ["ax", "vp"]))
        ring("a", s, a_ref, a_part)

    def b_step(s):
        need(*([f"b{s - 1}"] if s else ["vp"]))
        ring("b", s, b_ref, b_part)

    def d_step(s):
        need(*([f"d{s - 1}"] if s else ["adx", "ad"]))
        ring("d", s, d_ref, d_part)

    def reached(s):
        return (0,) if s < 0 else ((-1 - s, 1 + s) if s < 3 else (4,))

    def spread(s, d, kind):
        need(f"b{s}" if s >= 0 else "vp")
        for o in reached(s):
            send(f"{kind}{s}", b_ref(zat(o)), b_ref(zat(o)), x_peer(d))

    def relay(s):
        need(f"p{s}")
        behind = lax.rem(x + NX - 1, NX)
        for o in reached(s):
            send(f"r{s}", b_ref(zat(o), behind), b_ref(zat(o), behind), x_peer(1))

    def issue_ax():
        for d in (1, 3, 2):
            send("ax", vp.at[rows_a], W.at[t, rows_a], x_peer(d))

    def regroup(name, src, dst):
        for d in (1, 7, 2, 6, 3, 5, 4):
            peer = lax.rem(c + d, NC)
            send(name, src.at[:, pl.ds(al(peer * HC, HC), HC)], dst.at[own_rows], (t, peer))

    def positions():
        order = (iota((AUD, AUD), 0) < iota((AUD, AUD), 1)).astype(F32).astype(BF16)
        own = aud[pl.ds(t, 1), :]
        target = own // TOK
        hit = (iota((NT, AUD), 0) == target).astype(F32)
        rank = jnp.sum(dot(hit.astype(BF16), order) * hit, axis=0, keepdims=True)
        slot = target * SLOT + rank.astype(jnp.int32)
        slot_s[...] = jnp.broadcast_to(slot, slot_s.shape)
        table = aud[...]
        landing = table // TOK == t
        landing_rank = dot(landing.astype(F32).astype(BF16), order)
        spot = jnp.where(landing, table - t * TOK + 1, 0)
        n = NT * 16
        grow = (iota((n, NT), 0) // 16 == iota((n, NT), 1)).astype(F32).astype(BF16)
        spot_hi = dot(grow, (spot // 16).astype(F32).astype(BF16))
        spot_lo = dot(grow, (spot % 16).astype(F32).astype(BF16))
        ranks = dot(grow, jnp.where(landing, landing_rank, 64.0).astype(BF16))
        place = spot_hi * 16.0 + spot_lo
        r = (iota((n, AUD), 0) % 16).astype(F32)
        eye = iota((n, n), 0) == iota((n, n), 1)
        for half in range(2):
            col = jnp.sum(jnp.where(ranks == r - 8.0 * half, place, 0.0), axis=1, keepdims=True) - 1.0
            line = jnp.sum(jnp.where(eye, col, 0.0), axis=0, keepdims=True)
            land_s[half] = jnp.broadcast_to(line, (8, n)).astype(jnp.int32)

    def norm_glu():
        need("frames", "vw", "gw")
        ext[pl.ds(16, AUD), :] = frames_s[...]
        need("fh")
        rows = ext[...].astype(F32)
        centre = jnp.mean(rows, axis=1, keepdims=True)
        off = rows - centre
        spread_ = jnp.mean(off * off, axis=1, keepdims=True)
        normed = (off * lax.rsqrt(spread_ + NORM_EPS)).astype(BF16)
        value_part = dot(normed, vw_s[...])
        gate_part = dot(normed, gw_s[...])
        glu = (value_part * jax.nn.sigmoid(gate_part)).astype(BF16).astype(F32)
        row = iota(glu.shape, 0)
        first = jnp.where(t == 0, 16, 0)
        last = jnp.where(t == NT - 1, AUD + 16, AUD + 32)
        glu_s[...] = jnp.where((row >= first) & (row < last), glu, 0.0)

    def conv():
        need("taps", "ow")
        smooth = jnp.zeros((AUD, DH), F32)
        for j in range(taps_s.shape[0]):
            smooth = smooth + taps_s[pl.ds(j, 1), :] * glu_s[pl.ds(1 + j, AUD), :]
        action = (smooth * jax.nn.sigmoid(smooth)).astype(BF16)
        mixs[...] = dot(action, ow_s[...]).astype(BF16)
        for d in (4, 2, 6, 3, 5, 1, 7):
            rows_d = pl.ds(al(lax.rem(c + d, NC) * 16, 16), 16)
            send("mix", mixs.at[rows_d], mixr.at[d], ctx_peer(d))

    def encode():
        need("mix")
        mine = pl.ds(al(c * 16, 16), 16)
        total = frames_s[mine, :].astype(F32) + mixs[mine, :].astype(F32)
        for d in range(1, NC):
            total = total + mixr[d].astype(F32)
        enc[mine, :] = total.astype(BF16)
        for d in (4, 2, 6, 3, 5, 1, 7):
            send("enc", enc.at[mine], enc.at[mine], ctx_peer(d))

    def halo(name):
        part = qs if name == "q" else gs
        need(name, name + "0")
        send("h" + name, part.at[0], part.at[1], prv)

    scale = 1.0 / math.sqrt(DH)
    base = t * TOK
    row8 = iota((8, HALF), 0)

    def head_cols(h):
        return pl.ds(al(h * DH, DH), DH)

    def score_tiles(block, lows, limit, stats):
        def one_head(h, carry):
            hs = head_cols(h)
            for b, i0, j0, jn in TILES:
                if b != block:
                    continue
                qi = pl.ds(i0, HALF)
                s = dot_t(ks[pl.ds(j0, jn), hs], qs[b, qi, hs]) * scale
                jj = iota((jn, HALF), 0) + j0
                ok = jj >= lows[pl.ds(0, 1), qi] - base
                if block == 0:
                    ok = ok & (jj <= iota((jn, HALF), 1) + i0)
                else:
                    ok = ok & (jj < limit)
                s = jnp.where(ok, s, MASK_FILL)
                m = jnp.max(s, axis=0, keepdims=True)
                e = jnp.where(ok, jnp.exp(s - m), 0.0)
                n = jnp.sum(e, axis=0, keepdims=True)
                e_ref[b, h, pl.ds(j0, jn), qi] = e
                stats[h, :, qi] = jnp.where(row8 == 0, m, n)
            return carry

        lax.fori_loop(0, HH, one_head, 0)

    def score_own():
        need("k", "k0", "q", "q0")
        score_tiles(0, low_s, TOK, st_own)
        send("sta", st_own, st_fn, prv)

    def score_next():
        need("k", "k0", "hq", "low")
        score_tiles(1, lown, jnp.where(t == NT - 1, 0, TOK), st_nxt)
        send("stb", st_nxt, st_fp, nxt)

    my_slot = pl.ds(al(t * 16, 16), 16)

    def audio_copy(d):
        peer = lax.rem(t + d, NT)
        return pltpu.make_async_remote_copy(
            src_ref=pick.at[pl.ds(al(peer * 16, 16), 16)], dst_ref=inc.at[my_slot],
            send_sem=aus.at[d], recv_sem=aur.at[d], device_id=(peer, c), device_id_type=MESH,
        )

    def adapt():
        need("d3", "enc")
        for n in range(4):
            cols = pl.ds(256 * n, 256)
            adp[:, cols] = dot(enc[...], AD[:, cols]).astype(BF16)
        slot_row = iota((NT * 16, AUD), 0)
        picker = ((slot_row // 16) * SLOT + slot_row % SLOT == slot_s[pl.ds(0, 1), :]).astype(F32)
        picker = picker.astype(BF16)
        low_half = dot(picker, adp[:, pl.ds(0, 512)])
        high_half = dot(picker, adp[:, pl.ds(512, 512)])
        upper = iota((NT * 16, 512), 0) % 16 < SLOT
        pick[...] = jnp.where(upper, low_half, high_half).astype(BF16)

        def audio_start(d, carry):
            audio_copy(d).start()
            return carry

        lax.fori_loop(1, NT, audio_start, 0)
        inc[my_slot, :] = pick[my_slot, :]

    def factor(mine_st, other_st, h):
        m1, s1 = mine_st[h, pl.ds(0, 1), :], mine_st[h, pl.ds(1, 1), :]
        m2, s2 = other_st[h, pl.ds(0, 1), :], other_st[h, pl.ds(1, 1), :]
        m = jnp.maximum(m1, m2)
        a1 = jnp.exp(m1 - m)
        return a1 / (s1 * a1 + s2 * jnp.exp(m2 - m))

    def gather_terms(tiles, other, h):
        hs = head_cols(h)
        first, second = pl.ds(0, 256), pl.ds(256, 256)
        top = dot(tiles[0], other[0, first, hs]) + dot(tiles[1][:256], other[0, second, hs])
        top = top + dot(tiles[2][:256], other[1, first, hs])
        bottom = dot(tiles[1][256:], other[0, second, hs])
        bottom = bottom + dot(tiles[2][256:], other[1, first, hs])
        bottom = bottom + dot(tiles[3], other[1, second, hs])
        return top, bottom

    def prob():
        need("sta", "stb", "g", "g0", "hg")

        def prob_head(h, carry):
            f = (factor(st_own, st_fp, h), factor(st_nxt, st_fn, h))
            tiles = []
            for b, i0, j0, jn in TILES:
                p = e_ref[b, h, pl.ds(j0, jn), pl.ds(i0, HALF)] * f[b][:, i0 : i0 + HALF]
                e_ref[b, h, pl.ds(j0, jn), pl.ds(i0, HALF)] = p
                tiles.append(p.astype(BF16))
            top, bottom = gather_terms(tiles, gs, h)
            hs = head_cols(h)
            VG[c, pl.ds(0, 256), hs] = top.astype(BF16)
            VG[c, pl.ds(256, 256), hs] = bottom.astype(BF16)
            return carry

        lax.fori_loop(0, HH, prob_head, 0)
        send("vg1", VG.at[c], VG.at[c], ctx_peer(2))
        send("vg3", VG.at[c], VG.at[c], ctx_peer(6))
        send("vgc", VG.at[c], VG.at[c], mate)

    below, above, across = [lax.rem(c + d, NC) for d in (6, 2, 4)]

    def vg_relay():
        need("vg1", "vg3")
        one, two = VG.at[below, pl.ds(0, 256)], VG.at[above, pl.ds(256, 256)]
        send("vg2", one, one, ctx_peer(2))
        send("vg2", two, two, ctx_peer(6))
        send("vgc", VG.at[below], VG.at[below], mate)
        send("vgc", VG.at[above], VG.at[above], mate)

    def vg_last():
        need("vg2")
        send("vgc", VG.at[across], VG.at[across], mate)

    def place():
        need("text")

        def audio_arrived(d, carry):
            audio_copy(d).wait_recv()
            return carry

        lax.fori_loop(1, NT, audio_arrived, 0)
        for half in range(2):
            cols = pl.ds(512 * half, 512)
            hits = (iota((TOK, NT * 16), 0) == land_s[half, pl.ds(0, 1), :]).astype(F32)
            there = jnp.sum(hits, axis=1, keepdims=True) > 0.5
            rows_in = dot(hits.astype(BF16), inc[...])
            hid[:, cols] = jnp.where(there, rows_in, text_s[:, cols].astype(F32)).astype(BF16)

    mate_rows = pl.ds(al((1 - core) * HALF, HALF), HALF)
    my_rows = pl.ds(al(core * HALF, HALF), HALF)

    def weights_ready(i):
        s = (i - 1) // 2
        need(f"m{s}", f"p{s}", f"r{s}")
        need(*([f"a{s}", f"b{s}"] if i else ["ax", "vp"]))

    def terms(i):
        weights_ready(i)
        cp = zat(OFFSETS[i])
        w = jnp.concatenate([W[cp * HH + j] for j in range(HH)], axis=1)
        psend[i] = dot(hid[mate_rows, :], w).astype(BF16)
        send(f"pair{i}", psend.at[i], precv.at[i], mate)
        w = jnp.concatenate([W[cp * HH + j] for j in range(HH)], axis=1)
        pown[i] = dot(hid[my_rows, :], w).astype(BF16)

    def owner_copy(side, kd, i):
        owner = lax.rem(yy + 1 + 2 * side, NC // 2) * 2 + kd
        return pltpu.make_async_remote_copy(
            src_ref=rsend.at[i], dst_ref=rrecv.at[1 + side, my_rows],
            send_sem=rss.at[2 * side + kd], recv_sem=rsr.at[2 * side + core],
            device_id=(t, owner), device_id_type=MESH,
        )

    def add_copy(kd, i):
        return pltpu.make_async_remote_copy(
            src_ref=rsend.at[i], dst_ref=radd.at[kd],
            send_sem=rss.at[4 + kd], recv_sem=rsr.at[4 + kd],
            device_id=(t, lax.rem(c + 2 + 4 * core, NC)), device_id_type=MESH,
        )

    def mate_copy(i):
        return pltpu.make_async_remote_copy(
            src_ref=rsend.at[i], dst_ref=rrecv.at[0, my_rows],
            send_sem=rss.at[6], recv_sem=rsr.at[6], device_id=mate, device_id_type=MESH,
        )

    def owner_of(i):
        cp = zat(OFFSETS[i])
        return lax.rem(lax.div(cp, 2) - yy + NC // 2, NC // 2), lax.rem(cp, 2)

    def chip_sum(i):
        e, kd = owner_of(i)
        need(f"pair{i}")
        total = pown[i].astype(F32) + precv[i].astype(F32)
        rsend[i] = total.astype(BF16)

        @pl.when(e == 2)
        def _():
            add_copy(kd, i).start()

        @pl.when(e == 3 - 2 * core)
        def _():
            owner_copy(lax.div(e, 2), kd, i).start()

        @pl.when((e == 0) & (kd != core))
        def _():
            mate_copy(i).start()

        @pl.when((e == 0) & (kd == core))
        def _():
            rrecv[0, my_rows, :] = rsend[i]

    def added_sum(i):
        e, kd = owner_of(i)

        @pl.when(e == 1 + 2 * core)
        def _():
            add_copy(kd, i).wait_recv()
            total = rsend[i].astype(F32) + radd[kd].astype(F32)
            rsend[i] = total.astype(BF16)
            owner_copy(lax.div(e, 2), kd, i).start()

    added = []

    def hidden_grad(i):
        weights_ready(i)
        need("vgc")
        cp = zat(OFFSETS[i])
        added.append(i)
        first, last = len(added) == 1, len(added) == NC

        def part(n, carry):
            rows_n = pl.ds(al(n * 256, 256), 256)
            w = jnp.concatenate([W[cp * HH + j, rows_n, :] for j in range(HH)], axis=1)
            term = dot_t(VG[cp], w)
            if not first:
                term = term + acc[n]
            if last:
                dh_out[:, rows_n] = term.astype(BF16)
            else:
                acc[n] = term
            return carry

        lax.fori_loop(0, COLS // 256, part, 0)

    def delta():
        for n in (0, 1, 2, 3, 6):
            pltpu.make_async_remote_copy(
                src_ref=rsend.at[0], dst_ref=rrecv.at[0, my_rows], send_sem=rss.at[n],
                recv_sem=rsr.at[n], device_id=mate, device_id_type=MESH,
            ).wait_recv()
        total = rrecv[0].astype(F32) + rrecv[1].astype(F32) + rrecv[2].astype(F32)
        vbuf[...] = total.astype(BF16)

        def delta_head(h, carry):
            hs = head_cols(h)
            for b, i0, j0, jn in TILES:
                qi = pl.ds(i0, HALF)
                gv = dot_t(vbuf[pl.ds(j0, jn), hs], gs[b, qi, hs])
                gv_ref[b, h, pl.ds(j0, jn), qi] = gv
                w = e_ref[b, h, pl.ds(j0, jn), qi].astype(BF16).astype(F32)
                part = jnp.sum(w * gv, axis=0, keepdims=True)
                table = dl_own if b == 0 else dl_nxt
                table[h, :, qi] = jnp.where(row8 == 0, part, 0.0)
            return carry

        lax.fori_loop(0, HH, delta_head, 0)
        send("dl", dl_own, dl_fn, prv)
        send("dl", dl_nxt, dl_fp, nxt)

    def key():
        need("dl")

        def key_head(h, carry):
            deltas = (
                dl_own[h, pl.ds(0, 1), :] + dl_fp[h, pl.ds(0, 1), :],
                dl_nxt[h, pl.ds(0, 1), :] + dl_fn[h, pl.ds(0, 1), :],
            )
            tiles = []
            for b, i0, j0, jn in TILES:
                qi = pl.ds(i0, HALF)
                p = e_ref[b, h, pl.ds(j0, jn), qi]
                gv = gv_ref[b, h, pl.ds(j0, jn), qi]
                tiles.append((p * (gv - deltas[b][:, i0 : i0 + HALF])).astype(BF16))
            top, bottom = gather_terms(tiles, qs, h)
            hs = head_cols(h)
            dk_out[pl.ds(0, 256), hs] = (top * scale).astype(BF16)
            dk_out[pl.ds(256, 256), hs] = (bottom * scale).astype(BF16)
            return carry

        lax.fori_loop(0, HH, key_head, 0)

    steps = {
        "issue": issue, "i_ax": issue_ax,
        "i_b0": lambda: b_step(0), "i_bm": lambda: spread(-1, 1, "p"), "mm": lambda: spread(-1, 3, "m"),
        "i_k": lambda: regroup("k", k, ks),
        "i_q": lambda: regroup("q", q, qs.at[0]),
        "i_g": lambda: regroup("g", g, gs.at[0]),
        "pos": positions, "LN": norm_glu, "conv": conv, "enc": encode, "adapt": adapt, "place": place,
        "hq": lambda: halo("q"), "hg": lambda: halo("g"),
        "sc0": score_own, "sc1": score_next, "prob": prob, "vgr": vg_relay, "vgf": vg_last,
        "rm": lambda: relay(-1), "delta": delta, "key": key,
    }
    for s in range(4):
        steps[f"a_s{s}"] = lambda s=s: a_step(s)
        steps[f"b_s{s}"] = lambda s=s: b_step(s)
        steps[f"d_s{s}"] = lambda s=s: d_step(s)
        steps[f"p{s}"] = lambda s=s: spread(s, 1, "p")
        steps[f"m{s}"] = lambda s=s: spread(s, 3, "m")
        steps[f"r{s}"] = lambda s=s: relay(s)
    for i in range(NC):
        steps[f"t{i}"] = lambda i=i: terms(i)
        steps[f"rs{i}"] = lambda i=i: chip_sum(i)
        steps[f"ad{i}"] = lambda i=i: added_sum(i)
        steps[f"dh{i}"] = lambda i=i: hidden_grad(i)
    for name in ORDER:
        steps[name]()

    def audio_sent(d, carry):
        audio_copy(d).wait_send()
        return carry

    lax.fori_loop(1, NT, audio_sent, 0)
    for n in range(7):
        pltpu.make_async_remote_copy(
            src_ref=rsend.at[0], dst_ref=rrecv.at[0, my_rows], send_sem=rss.at[n],
            recv_sem=rsr.at[n], device_id=mate, device_id_type=MESH,
        ).wait_send()
    for name in groups:
        need(name)
    for copy in sends:
        copy.wait_send()


def body(
    frames, value_weight, gate_weight, conv_taps, out_weight, adapter, audio_pos, text_rows,
    value_proj, queries, keys, grad_out, window_low,
):
    vm = pl.BlockSpec(memory_space=pltpu.VMEM)
    hbm = pl.BlockSpec(memory_space=pl.ANY)
    vmem = pltpu.VMEM
    dma = pltpu.SemaphoreType.DMA
    return pl.pallas_call(
        kernel,
        out_shape=(
            jax.ShapeDtypeStruct((TOK, HC), BF16),
            jax.ShapeDtypeStruct((TOK, COLS), BF16),
        ),
        in_specs=[hbm] * 6 + [vm] * 2 + [hbm] * 5,
        out_specs=(vm, vm),
        scratch_shapes=[
            vmem((NT, COLS, DH), BF16),
            vmem((DE, COLS), BF16),
            vmem((2, TOK, HC), BF16),
            vmem((2, TOK, HC), BF16),
            vmem((TOK, HC), BF16),
            vmem((8, TOK), jnp.int32),
            vmem((8, TOK), jnp.int32),
            vmem((AUD, DE), BF16),
            vmem((DE, DH), BF16),
            vmem((DE, DH), BF16),
            vmem(conv_taps.shape, F32),
            vmem((DH, DE), BF16),
            vmem((TOK, COLS), BF16),
            vmem((8, AUD), jnp.int32),
            vmem((2, 8, NT * 16), jnp.int32),
            vmem((AUD + 32, DE), BF16),
            vmem((AUD + 32, DH), F32),
            vmem((AUD, DE), BF16),
            vmem((NC, 16, DE), BF16),
            vmem((AUD, DE), BF16),
            vmem((AUD, COLS), BF16),
            vmem((NT * 16, 512), BF16),
            vmem((NT * 16, 512), BF16),
            vmem((TOK, COLS), BF16),
            vmem((2, HH, TOK, TOK), F32),
            vmem((2, HH, TOK, TOK), F32),
        ]
        + [vmem((HH, 8, TOK), F32)] * 8
        + [
            vmem((NC, TOK, HC), BF16),
            vmem((NC, HALF, HC), BF16),
            vmem((NC, HALF, HC), BF16),
            vmem((NC, HALF, HC), BF16),
            vmem((NC, HALF, HC), BF16),
            vmem((2, HALF, HC), BF16),
            vmem((3, TOK, HC), BF16),
            vmem((TOK, HC), BF16),
            vmem((COLS // 256, TOK, 256), F32),
            dma((N_SEMS,)),
            dma((N_SEMS,)),
            dma((16,)),
            dma((NT,)),
            dma((NT,)),
            dma((NC,)),
            dma((NC,)),
        ],
        compiler_params=pltpu.CompilerParams(
            collective_id=0, has_side_effects=True, vmem_limit_bytes=60 * 1024 * 1024
        ),
        cost_estimate=pl.CostEstimate(flops=13_000_000_000, bytes_accessed=8_000_000, transcendentals=4_000_000),
    )(
        frames, value_weight, gate_weight, conv_taps, out_weight, text_rows,
        window_low.reshape(1, TOK), audio_pos.reshape(NT, AUD),
        adapter, value_proj, queries, keys, grad_out,
    )


def solution(mesh):
    return jax.shard_map(
        body,
        mesh=mesh,
        in_specs=(
            P("tm", None),
            P(None, "ctx"),
            P(None, "ctx"),
            P(None, "ctx"),
            P("ctx", None),
            P("tm", "ctx"),
            P(),
            P("tm", "ctx"),
            P("ctx", "tm"),
            P(("tm", "ctx"), None),
            P(("tm", "ctx"), None),
            P(("tm", "ctx"), None),
            P("tm"),
        ),
        out_specs=(P("tm", "ctx"), P("tm", "ctx")),
        check_vma=False,
    )
```
